32 devices in a mesh: dp: 2 (over core), expert: 16 (over z, y, x).
Axes of the slice: x: 2, y: 2, z: 4, core: 2. Of those that a mesh axis runs over, the one named last changes fastest.
Arguments:
- tokens: bfloat16 [4096, 2048], P(('dp', 'expert')), may hold values from -6 to 6
- cotangent: bfloat16 [4096, 2048], P(('dp', 'expert')), may hold values from -3 to 3
- experts: int32 [4096, 4], P(('dp', 'expert')), may hold values from 0 to 15, as said below
- mixing: float32 [4096, 4], P(('dp', 'expert')), may hold values from 0.1 to 0.9
- gate_matrix: bfloat16 [16, 2048, 768], P('expert'), may hold values from -0.125 to 0.125
- up_matrix: bfloat16 [16, 2048, 768], P('expert'), may hold values from -0.125 to 0.125
- down_matrix: bfloat16 [16, 768, 2048], P('expert'), may hold values from -0.21875 to 0.21875
Outputs:
- input_grad: bfloat16 [4096, 2048], P(('dp', 'expert'))
- gate_grad: float32 [16, 2048, 768], P('expert', 'dp')
- up_grad: float32 [16, 2048, 768], P('expert', 'dp')
- down_grad: float32 [16, 768, 2048], P('expert', 'dp')
The draws below stay inside these ranges and needn't reach their ends.
Inputs may be any that keep to these rules, and one draw needn't show every extreme that they name: A token names 4 different experts. Among the 128 tokens of one device, expert e and expert (e + 8) mod 16 are named together exactly 2 * 32 times, no expert more than 64 times, and one expert is named exactly 64 times by the tokens of every device.
All inputs are finite; a program needn't handle non-finite values.
Results may differ from the reference program's by a relative error of at most 0.0065.
Values may be sent and summed in bfloat16 or wider, within the bound.
No kernel may reach another device: no remote copies, remote signals or barrier semaphores. Data moves between devices by JAX's collectives and lax.ppermute only.
A program may use at most 128 MiB of HBM per device.

```python
import jax
import jax.numpy as jnp
from jax import lax

D = 2048
FF = 768
TOP = 4
EXPERTS = 16
TOK_DEV = 128
TOKENS = 4096
LOAD = 32
CAP = 64
N_DP = 2
N_EXPERT = 16


def block_routes(block_key, hot_expert):
    key_delta, key_rows, key_cols = jax.random.split(block_key, 3)
    half_count = EXPERTS // 2
    deltas = jax.random.randint(key_delta, (half_count,), -LOAD, LOAD + 1, dtype=jnp.int32)
    hot_delta = jnp.where(hot_expert < half_count, LOAD, -LOAD).astype(jnp.int32)
    deltas = jnp.where(jnp.arange(half_count, dtype=jnp.int32) == hot_expert % half_count, hot_delta, deltas)
    counts = jnp.concatenate([LOAD + deltas, LOAD - deltas]).astype(jnp.int32)
    run_ends = jnp.cumsum(counts)
    places = jnp.arange(TOK_DEV * TOP, dtype=jnp.int32)
    listing = jnp.sum((run_ends[None, :] <= places[:, None]).astype(jnp.int32), axis=1)
    layout = listing.reshape(TOP, TOK_DEV).T
    row_order = jax.random.permutation(key_rows, TOK_DEV)
    layout = layout[row_order]
    col_scores = jax.random.randint(key_cols, (TOK_DEV, TOP), 0, 1 << 20, dtype=jnp.int32) * TOP + jnp.arange(TOP, dtype=jnp.int32)[None, :]
    col_order = jnp.argsort(col_scores, axis=1, stable=True)
    return jnp.take_along_axis(layout, col_order, axis=1)


def draw_experts(key, part):
    key_hot, key_blocks = jax.random.split(jax.random.fold_in(key, 7))
    hot_expert = jax.random.randint(key_hot, (), 0, EXPERTS, dtype=jnp.int32)
    block_keys = jax.random.split(key_blocks, TOKENS // TOK_DEV)
    routed = jax.vmap(lambda block_key: block_routes(block_key, hot_expert))(block_keys)
    return routed.reshape(TOKENS, TOP).astype(jnp.int32)


def steps_of(stream_key, extent, cuts, least, top_value):
    factor_of, own = 1.0, jax.random.fold_in(stream_key, 6)
    for dim, blocks in cuts:
        steps = jnp.exp(jax.random.uniform(jax.random.fold_in(own, dim), (blocks,), jnp.float32, least / len(cuts), top_value / len(cuts)))
        factor_of = factor_of * jnp.repeat(steps, extent[dim] // blocks).reshape([-1 if axis == dim else 1 for axis in range(len(extent))])
    return factor_of


def bell_draw(rng, dims, width, most, cuts=(), held_as=jnp.bfloat16):
    drawn = jax.random.normal(rng, dims, jnp.float32) * width
    if len(cuts) > 0:
        drawn = steps_of(rng, dims, cuts, -0.22, 0.18) * drawn
    return jnp.clip(drawn, min=-most, max=most).astype(held_as)


def setup_inputs(seed: int = 0) -> dict:
    seeds = jax.random.split(jax.random.key(seed), 8)
    tokens = bell_draw(seeds[0], (TOKENS, D), 1.0, 6.0, ((0, 32),))
    cotangent = bell_draw(seeds[1], (TOKENS, D), 0.5, 3.0, ((0, 32),))
    experts = draw_experts(jax.random.fold_in(seeds[7], 71), 0)
    mixing = jnp.clip(0.1 + 0.79999997 * jax.random.uniform(seeds[3], (TOKENS, TOP), jnp.float32) ** steps_of(seeds[3], (TOKENS, TOP), ((0, 32),), -0.2, 0.2), 0.1, 0.9)
    gate_matrix = bell_draw(seeds[4], (EXPERTS, D, FF), D ** -0.5, 0.125, ((0, 16),))
    up_matrix = bell_draw(seeds[5], (EXPERTS, D, FF), D ** -0.5, 0.125, ((0, 16),))
    down_matrix = bell_draw(seeds[6], (EXPERTS, FF, D), FF ** -0.5, 0.21875, ((0, 16),))
    return dict(tokens=tokens, cotangent=cotangent, experts=experts, mixing=mixing, gate_matrix=gate_matrix, up_matrix=up_matrix, down_matrix=down_matrix)


def build_table(experts):
    blocks = TOKENS // TOK_DEV
    per_block = TOK_DEV * TOP
    routed = experts.reshape(blocks, per_block)
    labels = jnp.arange(EXPERTS, dtype=jnp.int32)
    onehot = (routed[:, :, None] == labels[None, None, :]).astype(jnp.int32)
    position = jnp.sum(onehot * (jnp.cumsum(onehot, axis=1) - 1), axis=2)
    column = jnp.arange(blocks, dtype=jnp.int32)[:, None] * CAP + position
    pair_ids = jnp.arange(TOKENS * TOP, dtype=jnp.int32).reshape(blocks, per_block)
    empty_table = jnp.full((EXPERTS, blocks * CAP), TOKENS * TOP, dtype=jnp.int32)
    return empty_table.at[routed, column].set(pair_ids)


def round_back(values):
    rounded = lax.optimization_barrier(values.astype(jnp.bfloat16))
    return rounded.astype(jnp.float32)


def reference(tokens, cotangent, experts, mixing, gate_matrix, up_matrix, down_matrix):
    table = build_table(experts)
    flat_mixing = mixing.reshape(TOKENS * TOP)
    group_shape = (N_DP, N_EXPERT, 2, LOAD)

    def one_expert(accumulated, expert_items):
        table_row, weight_gate, weight_up, weight_down = expert_items
        live_rows = table_row < TOKENS * TOP
        safe_index = jnp.where(live_rows, table_row, 0)
        token_ids = safe_index // TOP
        inputs = jnp.where(live_rows[:, None], tokens[token_ids], jnp.zeros((), jnp.bfloat16))
        weight_row = jnp.where(live_rows, flat_mixing[safe_index], jnp.zeros((), jnp.float32))
        scaled = (weight_row[:, None] * cotangent[token_ids].astype(jnp.float32)).astype(jnp.bfloat16)
        pre_gate = jnp.dot(inputs, weight_gate, preferred_element_type=jnp.float32)
        pre_up = jnp.dot(inputs, weight_up, preferred_element_type=jnp.float32)
        sigmoid_gate = jax.nn.sigmoid(pre_gate)
        activated = pre_gate * sigmoid_gate
        hidden = (activated * pre_up).astype(jnp.bfloat16)
        hidden_cot = jnp.dot(scaled, weight_down.T, preferred_element_type=jnp.float32)
        gate_cot = (hidden_cot * pre_up * sigmoid_gate * (1.0 + pre_gate * (1.0 - sigmoid_gate))).astype(jnp.bfloat16)
        up_cot = (hidden_cot * activated).astype(jnp.bfloat16)
        pair_cot = (jnp.dot(gate_cot, weight_gate.T, preferred_element_type=jnp.float32)
                    + jnp.dot(up_cot, weight_up.T, preferred_element_type=jnp.float32)).astype(jnp.bfloat16)
        accumulated = accumulated.at[token_ids].add(
            jnp.where(live_rows[:, None], pair_cot.astype(jnp.float32), jnp.zeros((), jnp.float32)))
        grouped_in = inputs.astype(jnp.float32).reshape(group_shape + (D,))
        grouped_gate = gate_cot.astype(jnp.float32).reshape(group_shape + (FF,))
        grouped_up = up_cot.astype(jnp.float32).reshape(group_shape + (FF,))
        grouped_hidden = hidden.astype(jnp.float32).reshape(group_shape + (FF,))
        grouped_cot = scaled.astype(jnp.float32).reshape(group_shape + (D,))
        gate_part = jnp.einsum("djsrk,djsrf->dskf", grouped_in, grouped_gate)
        up_part = jnp.einsum("djsrk,djsrf->dskf", grouped_in, grouped_up)
        down_part = jnp.einsum("djsrf,djsrk->dsfk", grouped_hidden, grouped_cot)
        gate_sum = jnp.sum(gate_part[:, 0], axis=0) + jnp.sum(round_back(gate_part[:, 1]), axis=0)
        up_sum = jnp.sum(up_part[:, 0], axis=0) + jnp.sum(round_back(up_part[:, 1]), axis=0)
        down_sum = jnp.sum(down_part[:, 0], axis=0) + jnp.sum(round_back(down_part[:, 1]), axis=0)
        return accumulated, (gate_sum, up_sum, down_sum)

    zero_start = jnp.zeros((TOKENS, D), jnp.float32)
    summed, expert_grads = lax.scan(one_expert, zero_start, (table, gate_matrix, up_matrix, down_matrix))
    return summed.astype(jnp.bfloat16), expert_grads[0], expert_grads[1], expert_grads[2]
```

```python
import functools

import jax
import jax.numpy as jnp
from jax import lax
from jax.experimental import pallas as pl
from jax.experimental.pallas import tpu as pltpu
from jax.sharding import PartitionSpec as P

BF16 = jnp.bfloat16
F32 = jnp.float32
VMEM_BYTES = 56 * 1024 * 1024
PARAMS = pltpu.CompilerParams(vmem_limit_bytes=VMEM_BYTES)


def dot(left, right, dims):
    return lax.dot_general(left, right, (dims, ((), ())), preferred_element_type=F32)


def cost(flops, bytes_accessed):
    return pl.CostEstimate(flops=flops, transcendentals=0, bytes_accessed=bytes_accessed)


def slot_masks(ids_ref, meta, count, cap):
    top = meta.shape[0] // 2
    tokens = meta.shape[1]
    earlier = lax.broadcasted_iota(jnp.int32, (tokens, tokens), 0)
    later = lax.broadcasted_iota(jnp.int32, (tokens, tokens), 1)
    before = (earlier < later).astype(F32)
    slot = lax.broadcasted_iota(jnp.int32, (cap, tokens), 0).astype(F32)
    named, weights = [], []
    for which in range(count):
        hit = meta[:top] == ids_ref[which].astype(F32)
        named.append(jnp.sum(jnp.where(hit, 1.0, 0.0), axis=0, keepdims=True))
        weights.append(jnp.sum(jnp.where(hit, meta[top:], 0.0), axis=0, keepdims=True))
    position = dot(jnp.concatenate(named, axis=0), before, ((1,), (0,)))
    onehot, slot_weight = [], []
    for which in range(count):
        here = (slot == position[which : which + 1]) & (named[which] > 0.5)
        onehot.append(jnp.where(here, 1.0, 0.0))
        slot_weight.append(jnp.sum(jnp.where(here, weights[which], 0.0), axis=1, keepdims=True))
    return jnp.concatenate(onehot, axis=0).astype(BF16), jnp.concatenate(slot_weight, axis=0)


def select_kernel(ids_ref, meta_ref, in_ref, cot_ref, *outs):
    count, (cap, width) = len(outs), outs[0].shape
    onehot, weight = slot_masks(ids_ref, meta_ref[...], count, cap)
    model = width // 2
    step = min(512, model)
    for start in range(0, model, step):
        rows = dot(onehot, in_ref[:, start : start + step], ((1,), (0,))).astype(BF16)
        cots = (dot(onehot, cot_ref[:, start : start + step], ((1,), (0,))) * weight).astype(BF16)
        for which in range(count):
            part = slice(which * cap, (which + 1) * cap)
            outs[which][:, start : start + step] = rows[part]
            outs[which][:, model + start : model + start + step] = cots[part]


def select(ids, meta, rows, cots, cap):
    count = ids.shape[0]
    tokens, model = rows.shape
    vmem = pl.BlockSpec(memory_space=pltpu.VMEM)
    return pl.pallas_call(
        select_kernel,
        out_shape=[jax.ShapeDtypeStruct((cap, 2 * model), BF16)] * count,
        in_specs=[pl.BlockSpec(memory_space=pltpu.SMEM), vmem, vmem, vmem],
        out_specs=[vmem] * count,
        compiler_params=PARAMS,
        cost_estimate=cost(4 * count * cap * tokens * model, 4 * model * (tokens + count * cap)),
        name="select",
    )(ids, meta, rows, cots)


def expert_kernel(count, *refs):
    ins = refs[:count]
    gate_ref, up_ref, down_ref = refs[count : count + 3]
    outs = refs[count + 3 : 2 * count + 3]
    all_ref, hidden_ref, gate_cot_ref, up_cot_ref, total = refs[2 * count + 3 :]
    cap, width = ins[0].shape
    model = width // 2
    step = pl.program_id(0)

    @pl.when(step == 0)
    def _():
        for which in range(count):
            all_ref[which * cap : (which + 1) * cap, :] = ins[which][...]

    rows = all_ref[:, :model]
    cots = all_ref[:, model:]
    pre_gate = dot(rows, gate_ref[...], ((1,), (0,)))
    pre_up = dot(rows, up_ref[...], ((1,), (0,)))
    hidden_cot = dot(cots, down_ref[...], ((1,), (1,)))
    sigmoid_gate = jax.nn.sigmoid(pre_gate)
    activated = pre_gate * sigmoid_gate
    hidden_ref[...] = (activated * pre_up).astype(BF16)
    gate_cot = (
        hidden_cot * pre_up * sigmoid_gate * (1.0 + pre_gate * (1.0 - sigmoid_gate))
    ).astype(BF16)
    up_cot = (hidden_cot * activated).astype(BF16)
    gate_cot_ref[...] = gate_cot
    up_cot_ref[...] = up_cot
    part = dot(gate_cot, gate_ref[...], ((1,), (1,))) + dot(up_cot, up_ref[...], ((1,), (1,)))

    @pl.when(step == 0)
    def _():
        total[...] = part

    @pl.when(step > 0)
    def _():
        total[...] += part

    @pl.when(step == pl.num_programs(0) - 1)
    def _():
        for which in range(count):
            outs[which][...] = total[which * cap : (which + 1) * cap, :].astype(BF16)


def expert(arrived, weight_gate, weight_up, weight_down):
    count = len(arrived)
    cap, width = arrived[0].shape
    model, units = weight_gate.shape
    block = min(256, units)
    rows = count * cap
    whole = lambda *shape: pl.BlockSpec(shape, lambda f: (0, 0))
    unit_block = pl.BlockSpec((rows, block), lambda f: (0, f))
    column_block = pl.BlockSpec((model, block), lambda f: (0, f))
    result = pl.pallas_call(
        functools.partial(expert_kernel, count),
        grid=(units // block,),
        in_specs=[whole(cap, width)] * count
        + [column_block, column_block, pl.BlockSpec((block, model), lambda f: (f, 0))],
        out_specs=[whole(cap, model)] * count + [whole(rows, width)] + [unit_block] * 3,
        out_shape=[jax.ShapeDtypeStruct((cap, model), BF16)] * count
        + [jax.ShapeDtypeStruct((rows, width), BF16)]
        + [jax.ShapeDtypeStruct((rows, units), BF16)] * 3,
        scratch_shapes=[pltpu.VMEM((rows, model), F32)],
        compiler_params=PARAMS,
        cost_estimate=cost(10 * rows * model * units, 6 * model * units + 10 * rows * model),
        name="expert",
    )(*arrived, weight_gate, weight_up, weight_down)
    return result[:count], result[count:]


def grads_kernel(count, add, half_ref, *refs):
    rows, cots, hiddens, gate_cots, up_cots = (
        refs[which * count : (which + 1) * count] for which in range(5)
    )
    rest = refs[5 * count :]
    outs = rest[-3:]
    totals = [0.0, 0.0, 0.0]
    for which in range(count):
        flipped = rows[which][...].T
        totals[0] += dot(flipped, gate_cots[which][...], ((1,), (0,)))
        totals[1] += dot(flipped, up_cots[which][...], ((1,), (0,)))
        totals[2] += dot(hiddens[which][...], cots[which][...], ((0,), (0,)))
    for which in range(3):
        value = totals[which]
        if add:
            value = value + rest[which][...].astype(F32)
        outs[which][...] = value.astype(outs[which].dtype)


def grads(half, saved, received):
    count = len(saved)
    rows, width = saved[0][0].shape
    units = saved[0][1].shape[1]
    model = width // 2
    steps = 4
    row_block, down_block = model // 2 // steps, model // steps
    add = received is not None
    in_specs = (
        [pl.BlockSpec((rows, row_block), lambda g, h: (0, h[0] * steps + g))] * count
        + [pl.BlockSpec((rows, down_block), lambda g, h: (0, steps + g))] * count
        + [pl.BlockSpec((rows, units // 2), lambda g, h: (0, h[0]))] * count
        + [pl.BlockSpec((rows, units), lambda g, h: (0, 0))] * (2 * count)
    )
    out_specs = [
        pl.BlockSpec((row_block, units), lambda g, h: (g, 0)),
        pl.BlockSpec((row_block, units), lambda g, h: (g, 0)),
        pl.BlockSpec((units // 2, down_block), lambda g, h: (0, g)),
    ]
    dtype = F32 if add else BF16
    args = (
        [part[0] for part in saved] * 2
        + [part[1] for part in saved]
        + [part[2] for part in saved]
        + [part[3] for part in saved]
    )
    if add:
        in_specs = in_specs + out_specs
        args = args + list(received)
    return pl.pallas_call(
        functools.partial(grads_kernel, count, add),
        grid_spec=pltpu.PrefetchScalarGridSpec(
            num_scalar_prefetch=1, grid=(steps,), in_specs=in_specs, out_specs=out_specs
        ),
        out_shape=[
            jax.ShapeDtypeStruct((model // 2, units), dtype),
            jax.ShapeDtypeStruct((model // 2, units), dtype),
            jax.ShapeDtypeStruct((units // 2, model), dtype),
        ],
        compiler_params=PARAMS,
        cost_estimate=cost(3 * count * rows * model * units, 8 * count * rows * model),
        name="grads",
    )(half, *args)


def expand_kernel(count, ids_ref, meta_ref, *refs):
    back, others, out = refs[:count], refs[count:-1], refs[-1]
    cap, model = back[0].shape
    onehot, _ = slot_masks(ids_ref, meta_ref[...], count, cap)
    spread = onehot.T
    step = min(512, model)
    for start in range(0, model, step):
        columns = slice(start, start + step)
        pairs = jnp.concatenate([ref[:, columns] for ref in back], axis=0)
        value = dot(spread, pairs, ((1,), (0,)))
        for other in others:
            value = value + other[:, columns].astype(F32)
        out[:, columns] = value.astype(BF16)


def expand(ids, meta, back, others):
    count = len(back)
    cap, model = back[0].shape
    tokens = meta.shape[1]
    vmem = pl.BlockSpec(memory_space=pltpu.VMEM)
    return pl.pallas_call(
        functools.partial(expand_kernel, count),
        out_shape=jax.ShapeDtypeStruct((tokens, model), BF16),
        in_specs=[pl.BlockSpec(memory_space=pltpu.SMEM)] + [vmem] * (1 + count + len(others)),
        out_specs=vmem,
        compiler_params=PARAMS,
        cost_estimate=cost(2 * count * cap * tokens * model, 2 * model * (tokens + count * cap)),
        name="expand",
    )(ids, meta, *back, *others)


def local(tokens, cotangent, experts, mixing, gate_matrix, up_matrix, down_matrix):
    expert_count = lax.axis_size("expert")
    inner = min(4, expert_count)
    outer = expert_count // inner
    tok_rows, top = experts.shape
    cap = 2 * tok_rows * top // expert_count

    def swap(value, mask):
        pairs = [(device, device ^ mask) for device in range(expert_count)]
        return lax.ppermute(value, "expert", pairs)

    ids = jnp.bitwise_xor(lax.axis_index("expert"), jnp.arange(inner)).astype(jnp.int32)
    meta = {0: jnp.concatenate([experts.astype(F32), mixing], axis=1).T}
    held = {0: (tokens, cotangent)}
    for plane in range(1, outer):
        low = plane & -plane
        meta[plane] = swap(meta[0], plane * inner)
        held[plane] = tuple(swap(part, low * inner) for part in held[plane ^ low])

    arrived = {}
    for plane in range(outer):
        sent = select(ids, meta[plane], *held[plane], cap)
        arrived[plane] = [sent[0]] + [swap(sent[which], which) for which in range(1, inner)]
    returned, saved = {}, []
    for plane in range(outer):
        pair_cot, kept = expert(arrived[plane], gate_matrix[0], up_matrix[0], down_matrix[0])
        returned[plane] = [pair_cot[0]] + [swap(pair_cot[which], which) for which in range(1, inner)]
        saved.append(kept)
    partial = [
        swap(expand(ids, meta[plane], returned[plane], []), plane * inner)
        for plane in range(1, outer)
    ]
    input_grad = expand(ids, meta[0], returned[0], partial)
    core = lax.axis_index("dp").astype(jnp.int32).reshape(1)
    other_half = grads(1 - core, saved, None)
    received = [lax.ppermute(part, "dp", [(0, 1), (1, 0)]) for part in other_half]
    gate_grad, up_grad, down_grad = grads(core, saved, received)
    return (input_grad, gate_grad[None], up_grad[None], down_grad[None])


def solution(mesh):
    return jax.shard_map(
        local,
        mesh=mesh,
        in_specs=(
            P(("dp", "expert"), None),
            P(("dp", "expert"), None),
            P(("dp", "expert"), None),
            P(("dp", "expert"), None),
            P("expert", None, None),
            P("expert", None, None),
            P("expert", None, None),
        ),
        out_specs=(
            P(("dp", "expert"), None),
            P("expert", "dp", None),
            P("expert", "dp", None),
            P("expert", "dp", None),
        ),
        check_vma=False,
    )
```

```python
import functools

import jax
import jax.numpy as jnp
from jax import lax
from jax.experimental import pallas as pl
from jax.experimental.pallas import tpu as pltpu
from jax.sharding import PartitionSpec as P

BF16 = jnp.bfloat16
F32 = jnp.float32
META = 16
COST = pl.CostEstimate(flops=1, transcendentals=0, bytes_accessed=1)
LONG = pl.CostEstimate(flops=1 << 37, transcendentals=0, bytes_accessed=1 << 27)
PARAMS = pltpu.CompilerParams(vmem_limit_bytes=56 * 1024 * 1024)
VMEM = pl.BlockSpec(memory_space=pltpu.VMEM)
SMEM = pl.BlockSpec(memory_space=pltpu.SMEM)
ANYWHERE = pl.BlockSpec(memory_space=pl.ANY)


def dot(left, right, dims=((1,), (0,))):
    return lax.dot_general(left, right, (dims, ((), ())), preferred_element_type=F32)


def array(shape, dtype=BF16):
    return jax.ShapeDtypeStruct(shape, dtype)


def pack_kernel(in_ref, cot_ref, experts_ref, mixing_ref, out_ref):
    tokens, model = in_ref.shape
    out_ref[:tokens, :] = in_ref[...]
    out_ref[tokens : 2 * tokens, :] = cot_ref[...]
    mixing = mixing_ref[...]
    high = mixing.astype(BF16).astype(F32)
    middle = (mixing - high).astype(BF16).astype(F32)
    low = mixing - high - middle
    filler = jnp.zeros((META - 4 * mixing.shape[0], tokens), F32)
    block = [experts_ref[...].astype(F32), high, middle, low]
    if filler.shape[0]:
        block.append(filler)
    out_ref[2 * tokens :, :tokens] = jnp.concatenate(block, axis=0).astype(BF16)
    out_ref[2 * tokens :, tokens:] = jnp.zeros((META, model - tokens), BF16)


def pack(tokens, cotangent, experts, mixing):
    rows, model = tokens.shape
    return pl.pallas_call(
        pack_kernel,
        out_shape=array((2 * rows + META, model)),
        in_specs=[VMEM] * 4,
        out_specs=VMEM,
        compiler_params=PARAMS,
        cost_estimate=COST,
        name="pack",
    )(tokens, cotangent, experts.T, mixing.T)


def slot_masks(ids_ref, block, count, cap, top):
    block = block.astype(F32)
    chosen, high, middle, low = (block[top * part : top * (part + 1)] for part in range(4))
    mixing = (high + middle) + low
    tokens = chosen.shape[1]
    earlier = lax.broadcasted_iota(jnp.int32, (tokens, tokens), 0)
    later = lax.broadcasted_iota(jnp.int32, (tokens, tokens), 1)
    before = (earlier < later).astype(F32)
    slot = lax.broadcasted_iota(jnp.int32, (cap, tokens), 0).astype(F32)
    named, weights = [], []
    for which in range(count):
        hit = chosen == ids_ref[which].astype(F32)
        named.append(jnp.sum(jnp.where(hit, 1.0, 0.0), axis=0, keepdims=True))
        weights.append(jnp.sum(jnp.where(hit, mixing, 0.0), axis=0, keepdims=True))
    position = dot(jnp.concatenate(named, axis=0), before)
    onehot, slot_weight = [], []
    for which in range(count):
        here = (slot == position[which : which + 1]) & (named[which] > 0.5)
        onehot.append(jnp.where(here, 1.0, 0.0))
        slot_weight.append(jnp.sum(jnp.where(here, weights[which], 0.0), axis=1, keepdims=True))
    return jnp.concatenate(onehot, axis=0), jnp.concatenate(slot_weight, axis=0)


def select_kernel(count, top, keep, ids_ref, packed_ref, *refs):
    onehot, weight = refs[-2:]
    outs = refs[-2 - keep - count : -2 - keep]
    cap = outs[0].shape[1]
    tokens = onehot.shape[1]

    @pl.when(pl.program_id(0) == 0)
    def _():
        block = packed_ref[2 * tokens :, :tokens]
        masks, slot_weight = slot_masks(ids_ref, block, count, cap, top)
        onehot[...] = masks.astype(BF16)
        weight[...] = jnp.broadcast_to(slot_weight, weight.shape)

    rows = dot(onehot[...], packed_ref[:tokens, :]).astype(BF16)
    cots = (dot(onehot[...], packed_ref[tokens : 2 * tokens, :]) * weight[:, :1]).astype(BF16)
    for which in range(count):
        part = slice(which * cap, (which + 1) * cap)
        outs[which][0] = rows[part]
        outs[which][1] = cots[part]
    if keep:
        refs[-3][...] = packed_ref[...]


def select(ids, packed, cap, top, keep, after):
    count = ids.shape[0]
    height, model = packed.shape
    tokens = (height - META) // 2
    step = min(512, model)
    packed_spec = pl.BlockSpec((height, step), lambda s: (0, s))
    return pl.pallas_call(
        functools.partial(select_kernel, count, top, int(keep)),
        grid=(model // step,),
        out_shape=[array((2, cap, model))] * count + [array(packed.shape)] * keep,
        in_specs=[SMEM, packed_spec] + [ANYWHERE] * len(after),
        out_specs=[pl.BlockSpec((2, cap, step), lambda s: (0, 0, s))] * count + [packed_spec] * keep,
        scratch_shapes=[
            pltpu.VMEM((count * cap, tokens), BF16),
            pltpu.VMEM((count * cap, 128), F32),
        ],
        compiler_params=PARAMS,
        cost_estimate=COST,
        name="select",
    )(ids, packed, *after)


def flip_kernel(gate_ref, up_ref, down_ref, _, both_ref, flipped_ref):
    units = gate_ref.shape[1]
    both_ref[:units, :] = gate_ref[...].T
    both_ref[units:, :] = up_ref[...].T
    flipped_ref[...] = down_ref[...].T


def flip(weight_gate, weight_up, weight_down, after):
    model, units = weight_gate.shape
    step = min(512, model)
    return pl.pallas_call(
        flip_kernel,
        grid=(model // step,),
        in_specs=[
            pl.BlockSpec((step, units), lambda s: (s, 0)),
            pl.BlockSpec((step, units), lambda s: (s, 0)),
            pl.BlockSpec((units, step), lambda s: (0, s)),
            ANYWHERE,
        ],
        out_specs=[
            pl.BlockSpec((2 * units, step), lambda s: (0, s)),
            pl.BlockSpec((step, units), lambda s: (s, 0)),
        ],
        out_shape=[array((2 * units, model)), array((model, units))],
        compiler_params=PARAMS,
        cost_estimate=COST,
        name="flip",
    )(weight_gate, weight_up, weight_down, after)


def expert_kernel(count, first_steps, *refs):
    ins = refs[:count]
    gate_ref, up_ref, down_ref, both_ref = refs[count : count + 4]
    outs = refs[-count - 6 : -6]
    rows_ref, cots_ref, pair_units_ref, hidden_ref, rows, cots = refs[-6:]
    cap = ins[0].shape[1]
    units = hidden_ref.shape[1]
    block = gate_ref.shape[1]
    step = pl.program_id(0)

    @pl.when(step == 0)
    def _():
        for which in range(count):
            rows[which * cap : (which + 1) * cap, :] = ins[which][0]
            cots[which * cap : (which + 1) * cap, :] = ins[which][1]

    @pl.when(step < first_steps)
    def _():
        pre_gate = dot(rows[...], gate_ref[...])
        pre_up = dot(rows[...], up_ref[...])
        hidden_cot = dot(cots[...], down_ref[...])
        sigmoid_gate = jax.nn.sigmoid(pre_gate)
        activated = pre_gate * sigmoid_gate
        start = pl.multiple_of(step * block, block)
        hidden_ref[:, pl.ds(start, block)] = (activated * pre_up).astype(BF16)
        pair_units_ref[:, pl.ds(start, block)] = (
            hidden_cot * pre_up * sigmoid_gate * (1.0 + pre_gate * (1.0 - sigmoid_gate))
        ).astype(BF16)
        pair_units_ref[:, pl.ds(units + start, block)] = (hidden_cot * activated).astype(BF16)

    @pl.when(step >= first_steps)
    def _():
        width = rows_ref.shape[1]
        start = pl.multiple_of((step - first_steps) * width, width)
        rows_ref[...] = rows[:, pl.ds(start, width)]
        cots_ref[...] = cots[:, pl.ds(start, width)]
        pair_cot = dot(pair_units_ref[...], both_ref[...]).astype(BF16)
        for which in range(count):
            outs[which][...] = pair_cot[which * cap : (which + 1) * cap]


def expert(arrived, weight_gate, weight_up, flipped_down, flipped_both, saved, place, places, after):
    count = len(arrived)
    _, cap, model = arrived[0].shape
    units = weight_gate.shape[1]
    block, width = min(256, units), min(512, model)
    first_steps, last_steps = units // block, model // width
    rows = count * cap
    early = lambda s: (0, jnp.minimum(s, first_steps - 1))
    late = lambda s: (0, jnp.maximum(s - first_steps, 0))
    late_rows = pl.BlockSpec((rows, width), lambda s: (place, jnp.maximum(s - first_steps, 0)))
    kept = [(rows, model), (rows, model), (rows, 2 * units), (rows, units)]
    result = pl.pallas_call(
        functools.partial(expert_kernel, count, first_steps),
        grid=(first_steps + last_steps,),
        in_specs=[pl.BlockSpec((2, cap, model), lambda s: (0, 0, 0))] * count
        + [pl.BlockSpec((model, block), early)] * 3
        + [pl.BlockSpec((2 * units, width), late)]
        + [ANYWHERE] * (len(saved) + len(after)),
        out_specs=[pl.BlockSpec((cap, width), late)] * count
        + [late_rows, late_rows]
        + [pl.BlockSpec(shape, lambda s: (place, 0)) for shape in kept[2:]],
        out_shape=[array((cap, model))] * count
        + [array((places * shape[0], shape[1])) for shape in kept],
        scratch_shapes=[pltpu.VMEM((rows, model), BF16)] * 2,
        input_output_aliases={count + 4 + which: count + which for which in range(len(saved))},
        compiler_params=PARAMS,
        cost_estimate=COST,
        name="expert",
    )(*arrived, weight_gate, weight_up, flipped_down, flipped_both, *saved, *after)
    return result[:count], result[count:]


def grads_kernel(half_ref, rows_ref, cots_ref, pair_units_ref, hidden_ref, *refs):
    flipped_hidden = refs[-1]
    units = hidden_ref.shape[1] * 2

    @pl.when(pl.program_id(0) == 0)
    def _():
        flipped_hidden[...] = hidden_ref[...].T

    both = dot(rows_ref[...].T, pair_units_ref[...])
    down = dot(flipped_hidden[...], cots_ref[...])
    height, width = both.shape[0], down.shape[1]
    rest = units // 2 - height
    fold = height // rest
    part = width // fold
    if len(refs) == 3:
        sent = refs[1]
        sent[:, : 2 * units] = both.astype(BF16)
        down = down.astype(BF16)
        sent[:, 2 * units : 2 * units + width] = down[:height]
        for which in range(fold):
            sent[which * rest : (which + 1) * rest, 2 * units + width :] = down[
                height:, which * part : (which + 1) * part
            ]
    else:
        other, _, gate_ref, up_ref, down_ref, _ = refs
        gate_ref[...] = both[:, :units] + other[:, :units].astype(F32)
        up_ref[...] = both[:, units:] + other[:, units : 2 * units].astype(F32)
        down_ref[:height, :] = down[:height] + other[:, 2 * units : 2 * units + width].astype(F32)
        for which in range(fold):
            columns = slice(which * part, (which + 1) * part)
            down_ref[height:, columns] = down[height:, columns] + other[
                which * rest : (which + 1) * rest, 2 * units + width :
            ].astype(F32)


def grads(half, saved, received, after):
    rows, model = saved[0].shape
    units = saved[3].shape[1]
    steps = 4
    row_block, down_block = model // 2 // steps, model // steps
    sent_width = 2 * units + (units // 2) * down_block // row_block
    in_specs = [
        pl.BlockSpec((rows, row_block), lambda g, h: (0, h[0] * steps + g)),
        pl.BlockSpec((rows, down_block), lambda g, h: (0, g)),
        pl.BlockSpec((rows, 2 * units), lambda g, h: (0, 0)),
        pl.BlockSpec((rows, units // 2), lambda g, h: (0, h[0])),
    ]
    sent_spec = pl.BlockSpec((row_block, sent_width), lambda g, h: (g, 0))
    one_spec = pl.BlockSpec((row_block, units), lambda g, h: (g, 0))
    down_spec = pl.BlockSpec((units // 2, down_block), lambda g, h: (0, g))
    if received:
        in_specs += [sent_spec]
        out_specs = [one_spec, one_spec, down_spec]
        out_shape = [array((model // 2, units), F32)] * 2 + [array((units // 2, model), F32)]
    else:
        out_specs = [sent_spec]
        out_shape = [array((model // 2, sent_width))]
    return pl.pallas_call(
        grads_kernel,
        grid_spec=pltpu.PrefetchScalarGridSpec(
            num_scalar_prefetch=1,
            grid=(steps,),
            in_specs=in_specs + [ANYWHERE],
            out_specs=out_specs,
            scratch_shapes=[pltpu.VMEM((units // 2, rows), BF16)],
        ),
        out_shape=out_shape,
        compiler_params=PARAMS,
        cost_estimate=LONG,
        name="grads",
    )(half, *saved, *received, after)


def expand_kernel(count, top, ids_ref, meta_ref, *refs):
    back, out = refs[:count], refs[-1]
    cap, model = back[0].shape
    onehot, _ = slot_masks(ids_ref, meta_ref[...], count, cap, top)
    spread = onehot.T.astype(BF16)
    step = min(512, model)
    for start in range(0, model, step):
        columns = slice(start, start + step)
        value = dot(spread, jnp.concatenate([ref[:, columns] for ref in back], axis=0))
        out[:, columns] = value.astype(out.dtype)


def expand(ids, packed, back, top, dtype, estimate, after):
    count = len(back)
    cap, model = back[0].shape
    tokens = (packed.shape[0] - META) // 2
    whole = lambda *shape: pl.BlockSpec(shape, lambda s: (0, 0))
    return pl.pallas_call(
        functools.partial(expand_kernel, count, top),
        grid=(1,),
        out_shape=array((tokens, model), dtype),
        in_specs=[SMEM, pl.BlockSpec((META, tokens), lambda s: (2 * tokens // META, 0))]
        + [whole(cap, model)] * count
        + [ANYWHERE],
        out_specs=whole(tokens, model),
        compiler_params=PARAMS,
        cost_estimate=estimate,
        name="expand",
    )(ids, packed, *back, after)


def total_kernel(count, own_ref, *refs):
    value = own_ref[...]
    for ref in refs[:count]:
        value = value + ref[...].astype(F32)
    refs[-1][...] = value.astype(refs[-1].dtype)


def total(own, others, dtype, after):
    rows, model = own.shape
    step = min(512, model)
    spec = pl.BlockSpec((rows, step), lambda s: (0, s))
    return pl.pallas_call(
        functools.partial(total_kernel, len(others)),
        grid=(model // step,),
        out_shape=array(own.shape, dtype),
        in_specs=[spec] * (1 + len(others)) + [ANYWHERE],
        out_specs=spec,
        compiler_params=PARAMS,
        cost_estimate=COST,
        name="total",
    )(own, *others, after)


def local(tokens, cotangent, experts, mixing, gate_matrix, up_matrix, down_matrix):
    expert_count = lax.axis_size("expert")
    inner = min(4, expert_count)
    outer = expert_count // inner
    tok_rows, top = experts.shape
    cap = 2 * tok_rows * top // expert_count
    weight_gate, weight_up, weight_down = gate_matrix[0], up_matrix[0], down_matrix[0]

    def swap(value, mask):
        pairs = [(device, device ^ mask) for device in range(expert_count)]
        return lax.ppermute(value, "expert", pairs)

    def swap_inner(values):
        return [values[0]] + [swap(values[which], which) for which in range(1, inner)]

    ids = jnp.bitwise_xor(lax.axis_index("expert"), jnp.arange(inner)).astype(jnp.int32)
    order = list(range(2, outer)) + [1] if outer > 1 else []
    places = [0] + order
    packed = {0: pack(tokens, cotangent, experts, mixing)}
    arrived, returned, partial, kept = {}, {}, [], {}
    saved = []

    def fetch(plane):
        low = plane & -plane
        source = plane ^ low
        packed[plane] = swap(kept[source] if source else packed[0], low * inner)

    def send(plane, after):
        onward = [other for other in order if other ^ (other & -other) == plane and plane]
        sent = list(select(ids, packed[plane], cap, top, bool(onward), after))
        if onward:
            kept[plane] = sent.pop()
        arrived[plane] = swap_inner(sent)
        for other in onward:
            fetch(other)
        return sent[0]

    def work(plane, after):
        pair_cot, saved[:] = expert(
            arrived[plane], weight_gate, weight_up, flipped_down, flipped_both,
            saved, places.index(plane), outer, after,
        )
        returned[plane] = swap_inner(pair_cot)
        return pair_cot[0]

    def give_back(plane, after, estimate=COST):
        value = expand(ids, packed[plane], returned[plane], top, BF16, estimate, after)
        partial.append(swap(value, plane * inner))
        return value

    for plane in order:
        if plane & (plane - 1) == 0:
            fetch(plane)
    last = send(0, [])
    flipped_both, flipped_down = flip(weight_gate, weight_up, weight_down, last)
    last = work(0, [])
    own = expand(ids, packed[0], returned[0], top, F32, COST, last)
    last = own
    for plane in order[:2]:
        last = send(plane, [last])
    for which, plane in enumerate(order):
        last = work(plane, [last])
        if which + 2 < len(order):
            last = send(order[which + 2], [last])
        if which >= 1:
            last = give_back(order[which - 1], last)
    if len(partial) > 1:
        own = total(own, partial[:-1], F32, last)
        last = own
        del partial[:-1]
    core = lax.axis_index("dp").astype(jnp.int32).reshape(1)
    (other_half,) = grads(1 - core, saved, [], last)
    received = lax.ppermute(other_half, "dp", [(0, 1), (1, 0)])
    last = other_half
    if order:
        last = give_back(order[-1], last, LONG)
    gate_grad, up_grad, down_grad = grads(core, saved, [received], last)
    input_grad = total(own, partial, BF16, gate_grad)
    return (input_grad, gate_grad[None], up_grad[None], down_grad[None])


def solution(mesh):
    return jax.shard_map(
        local,
        mesh=mesh,
        in_specs=(
            P(("dp", "expert"), None),
            P(("dp", "expert"), None),
            P(("dp", "expert"), None),
            P(("dp", "expert"), None),
            P("expert", None, None),
            P("expert", None, None),
            P("expert", None, None),
        ),
        out_specs=(
            P(("dp", "expert"), None),
            P("expert", "dp", None),
            P("expert", "dp", None),
            P("expert", "dp", None),
        ),
        check_vma=False,
    )
```

```python
import functools

import jax
import jax.numpy as jnp
from jax import lax
from jax.experimental import pallas as pl
from jax.experimental.pallas import tpu as pltpu
from jax.sharding import PartitionSpec as P

BF16 = jnp.bfloat16
F32 = jnp.float32
META = 16
COST = pl.CostEstimate(flops=1, transcendentals=0, bytes_accessed=1)
LONG = pl.CostEstimate(flops=1 << 37, transcendentals=0, bytes_accessed=1 << 27)
VMEM = pl.BlockSpec(memory_space=pltpu.VMEM)
SMEM = pl.BlockSpec(memory_space=pltpu.SMEM)
ANYWHERE = pl.BlockSpec(memory_space=pl.ANY)


def params(mebibytes):
    return pltpu.CompilerParams(vmem_limit_bytes=mebibytes << 20)


def dot(left, right, dims=((1,), (0,))):
    return lax.dot_general(left, right, (dims, ((), ())), preferred_element_type=F32)


def array(shape, dtype=BF16):
    return jax.ShapeDtypeStruct(shape, dtype)


def resident(*shape):
    return pltpu.VMEM(shape, BF16)


def pack_kernel(in_ref, cot_ref, experts_ref, mixing_ref, out_ref):
    tokens, model = in_ref.shape
    out_ref[:tokens, :] = in_ref[...]
    out_ref[tokens : 2 * tokens, :] = cot_ref[...]
    mixing = mixing_ref[...]
    high = mixing.astype(BF16).astype(F32)
    middle = (mixing - high).astype(BF16).astype(F32)
    low = mixing - high - middle
    filler = jnp.zeros((META - 4 * mixing.shape[0], tokens), F32)
    block = [experts_ref[...].astype(F32), high, middle, low]
    if filler.shape[0]:
        block.append(filler)
    out_ref[2 * tokens :, :tokens] = jnp.concatenate(block, axis=0).astype(BF16)
    out_ref[2 * tokens :, tokens:] = jnp.zeros((META, model - tokens), BF16)


def pack(tokens, cotangent, experts, mixing):
    rows, model = tokens.shape
    return pl.pallas_call(
        pack_kernel,
        out_shape=array((2 * rows + META, model)),
        in_specs=[VMEM] * 4,
        out_specs=VMEM,
        compiler_params=params(12),
        cost_estimate=COST,
        name="pack",
    )(tokens, cotangent, experts.T, mixing.T)


def slot_masks(ids_ref, block, count, cap, top):
    block = block.astype(F32)
    chosen, high, middle, low = (block[top * part : top * (part + 1)] for part in range(4))
    mixing = (high + middle) + low
    tokens = chosen.shape[1]
    earlier = lax.broadcasted_iota(jnp.int32, (tokens, tokens), 0)
    later = lax.broadcasted_iota(jnp.int32, (tokens, tokens), 1)
    before = (earlier < later).astype(F32)
    slot = lax.broadcasted_iota(jnp.int32, (cap, tokens), 0).astype(F32)
    named, weights = [], []
    for which in range(count):
        hit = chosen == ids_ref[which].astype(F32)
        named.append(jnp.sum(jnp.where(hit, 1.0, 0.0), axis=0, keepdims=True))
        weights.append(jnp.sum(jnp.where(hit, mixing, 0.0), axis=0, keepdims=True))
    position = dot(jnp.concatenate(named, axis=0), before)
    onehot, slot_weight = [], []
    for which in range(count):
        here = (slot == position[which : which + 1]) & (named[which] > 0.5)
        onehot.append(jnp.where(here, 1.0, 0.0))
        slot_weight.append(jnp.sum(jnp.where(here, weights[which], 0.0), axis=1, keepdims=True))
    return jnp.concatenate(onehot, axis=0), jnp.concatenate(slot_weight, axis=0)


def select_kernel(count, top, keep, ids_ref, packed_ref, *refs):
    outs = refs[-keep - count : len(refs) - keep]
    cap = outs[0].shape[1]
    height, model = packed_ref.shape
    tokens = (height - META) // 2
    masks, weight = slot_masks(ids_ref, packed_ref[2 * tokens :, :tokens], count, cap, top)
    onehot = masks.astype(BF16)
    step = min(512, model)
    for start in range(0, model, step):
        columns = slice(start, start + step)
        rows = dot(onehot, packed_ref[:tokens, columns]).astype(BF16)
        cots = (dot(onehot, packed_ref[tokens : 2 * tokens, columns]) * weight).astype(BF16)
        for which in range(count):
            part = slice(which * cap, (which + 1) * cap)
            outs[which][0, :, columns] = rows[part]
            outs[which][1, :, columns] = cots[part]
    if keep:
        refs[-1][...] = packed_ref[...]


def select(ids, packed, cap, top, keep, after):
    count = ids.shape[0] - 2
    model = packed.shape[1]
    return pl.pallas_call(
        functools.partial(select_kernel, count, top, int(keep)),
        out_shape=[array((2, cap, model))] * count + [array(packed.shape)] * keep,
        in_specs=[SMEM, VMEM] + [ANYWHERE] * len(after),
        out_specs=[VMEM] * (count + keep),
        compiler_params=params(14),
        cost_estimate=COST,
        name="select",
    )(ids, packed, *after)


def flip_kernel(gate_in, up_in, down_in, _, gate_ref, up_ref, both_ref, flipped_ref, down, sems):
    copies = [
        pltpu.make_async_copy(source, target, sems.at[which])
        for which, (source, target) in enumerate(
            ((gate_in, gate_ref), (up_in, up_ref), (down_in, down))
        )
    ]
    for copy in copies:
        copy.start()
    model, units = gate_ref.shape
    step = min(512, model)
    for which, source in enumerate((gate_ref, up_ref)):
        copies[which].wait()
        for start in range(0, model, step):
            both_ref[which * units : (which + 1) * units, start : start + step] = source[
                start : start + step, :
            ].T
    copies[2].wait()
    for start in range(0, model, step):
        flipped_ref[start : start + step, :] = down[:, start : start + step].T


def flip(weight_gate, weight_up, weight_down, after):
    model, units = weight_gate.shape
    return pl.pallas_call(
        flip_kernel,
        in_specs=[ANYWHERE] * 4,
        out_specs=[VMEM] * 4,
        out_shape=[
            resident(model, units),
            resident(model, units),
            resident(2 * units, model),
            resident(model, units),
        ],
        scratch_shapes=[pltpu.VMEM((units, model), BF16), pltpu.SemaphoreType.DMA((3,))],
        compiler_params=params(12),
        cost_estimate=COST,
        name="flip",
    )(weight_gate, weight_up, weight_down, after)


def expert_kernel(count, place, *refs):
    ins = refs[:count]
    gate_ref, up_ref, both_ref, flipped_ref = refs[count : count + 4]
    outs = refs[-count - 4 : -4]
    rows_ref, cots_ref, pair_units_ref, hidden_ref = refs[-4:]
    cap = ins[0].shape[1]
    model, units = gate_ref.shape
    begin = place * count * cap
    here = slice(begin, begin + count * cap)
    for which in range(count):
        part = slice(begin + which * cap, begin + (which + 1) * cap)
        rows_ref[part, :] = ins[which][0]
        cots_ref[part, :] = ins[which][1]
    block = min(256, units)
    for start in range(0, units, block):
        columns = slice(start, start + block)
        pre_gate = dot(rows_ref[here, :], gate_ref[:, columns])
        pre_up = dot(rows_ref[here, :], up_ref[:, columns])
        hidden_cot = dot(cots_ref[here, :], flipped_ref[:, columns])
        sigmoid_gate = jax.nn.sigmoid(pre_gate)
        activated = pre_gate * sigmoid_gate
        hidden_ref[here, columns] = (activated * pre_up).astype(BF16)
        pair_units_ref[here, columns] = (
            hidden_cot * pre_up * sigmoid_gate * (1.0 + pre_gate * (1.0 - sigmoid_gate))
        ).astype(BF16)
        pair_units_ref[here, units + start : units + start + block] = (
            hidden_cot * activated
        ).astype(BF16)
    block = min(512, model)
    for start in range(0, model, block):
        columns = slice(start, start + block)
        pair_cot = dot(pair_units_ref[here, :], both_ref[:, columns]).astype(BF16)
        for which in range(count):
            outs[which][:, columns] = pair_cot[which * cap : (which + 1) * cap]


def expert(arrived, weights, saved, place, places, after):
    count = len(arrived)
    _, cap, model = arrived[0].shape
    units = weights[0].shape[1]
    total_rows = places * count * cap
    result = pl.pallas_call(
        functools.partial(expert_kernel, count, place),
        in_specs=[VMEM] * (count + 4 + len(saved)) + [ANYWHERE] * len(after),
        out_specs=[VMEM] * (count + 4),
        out_shape=[array((cap, model))] * count
        + [
            resident(total_rows, model),
            resident(total_rows, model),
            resident(total_rows, 2 * units),
            resident(total_rows, units),
        ],
        input_output_aliases={count + 4 + which: count + which for which in range(len(saved))},
        compiler_params=params(14),
        cost_estimate=COST,
        name="expert",
    )(*arrived, *weights, *saved, *after)
    return result[:count], result[count:]


def grads_kernel(add, ids_ref, rows_ref, cots_ref, pair_units_ref, hidden_ref, *refs):
    rows, units = hidden_ref.shape
    model = rows_ref.shape[1]
    half = ids_ref[ids_ref.shape[0] - 2 + (not add)]
    steps = 4
    height, width = model // 2 // steps, model // steps
    rest = units // 2 - height
    fold = height // rest
    part = width // fold
    if add:
        other, _, gate_out, up_out, down_out, gate_ref, up_ref, down_ref, sems = refs
    else:
        _, sent_out, sent_ref, sems = refs
    own_units = pl.ds(pl.multiple_of(half * (units // 2), 128), units // 2)
    flipped_hidden = hidden_ref[:, own_units].T
    copies = []
    for step in range(steps):
        at = slice(step * height, (step + 1) * height)
        across = slice(step * width, (step + 1) * width)
        own_rows = pl.ds(pl.multiple_of(half * (model // 2) + step * height, 128), height)
        both = dot(rows_ref[:, own_rows].T, pair_units_ref[...])
        down = dot(flipped_hidden, cots_ref[:, across])
        if add:
            gate_ref[at, :] = both[:, :units] + other[at, :units].astype(F32)
            up_ref[at, :] = both[:, units:] + other[at, units : 2 * units].astype(F32)
            down_ref[:height, across] = down[:height] + other[
                at, 2 * units : 2 * units + width
            ].astype(F32)
            for which in range(fold):
                columns = slice(which * part, (which + 1) * part)
                lower = slice(step * height + which * rest, step * height + (which + 1) * rest)
                target = slice(step * width + which * part, step * width + (which + 1) * part)
                down_ref[height:, target] = down[height:, columns] + other[
                    lower, 2 * units + width :
                ].astype(F32)
            moves = [
                (gate_ref.at[at], gate_out.at[at]),
                (up_ref.at[at], up_out.at[at]),
                (down_ref.at[:, across], down_out.at[:, across]),
            ]
        else:
            sent_ref[at, : 2 * units] = both.astype(BF16)
            down = down.astype(BF16)
            sent_ref[at, 2 * units : 2 * units + width] = down[:height]
            for which in range(fold):
                lower = slice(step * height + which * rest, step * height + (which + 1) * rest)
                sent_ref[lower, 2 * units + width :] = down[
                    height:, which * part : (which + 1) * part
                ]
            moves = [(sent_ref.at[at], sent_out.at[at])]
        for which, (source, target) in enumerate(moves):
            copy = pltpu.make_async_copy(source, target, sems.at[step, which])
            copy.start()
            copies.append(copy)
    for copy in copies:
        copy.wait()


def grads(ids, saved, received, after):
    _, model = saved[0].shape
    units = saved[3].shape[1]
    add = bool(received)
    if add:
        shapes = [(model // 2, units), (model // 2, units), (units // 2, model)]
        dtype = F32
    else:
        shapes = [(model // 2, 2 * units + units // 2 * 2)]
        dtype = BF16
    return pl.pallas_call(
        functools.partial(grads_kernel, add),
        in_specs=[SMEM] + [VMEM] * (4 + len(received)) + [ANYWHERE],
        out_specs=[ANYWHERE] * len(shapes),
        out_shape=[array(shape, dtype) for shape in shapes],
        scratch_shapes=[pltpu.VMEM(shape, dtype) for shape in shapes]
        + [pltpu.SemaphoreType.DMA((4, len(shapes)))],
        compiler_params=params(26),
        cost_estimate=LONG,
        name="grads",
    )(ids, *saved, *received, after)


def expand_kernel(count, top, ids_ref, meta_ref, *refs):
    back, out = refs[:count], refs[-1]
    cap, model = back[0].shape
    onehot, _ = slot_masks(ids_ref, meta_ref[...], count, cap, top)
    spread = onehot.T.astype(BF16)
    step = min(512, model)
    for start in range(0, model, step):
        columns = slice(start, start + step)
        value = dot(spread, jnp.concatenate([ref[:, columns] for ref in back], axis=0))
        out[:, columns] = value.astype(out.dtype)


def expand(ids, packed, back, top, dtype, estimate, after):
    count = len(back)
    cap, model = back[0].shape
    tokens = (packed.shape[0] - META) // 2
    whole = lambda *shape: pl.BlockSpec(shape, lambda s: (0, 0))
    return pl.pallas_call(
        functools.partial(expand_kernel, count, top),
        grid=(1,),
        out_shape=array((tokens, model), dtype),
        in_specs=[SMEM, pl.BlockSpec((META, tokens), lambda s: (2 * tokens // META, 0))]
        + [whole(cap, model)] * count
        + [ANYWHERE],
        out_specs=whole(tokens, model),
        compiler_params=params(12),
        cost_estimate=estimate,
        name="expand",
    )(ids, packed, *back, after)


def total_kernel(count, own_ref, *refs):
    value = own_ref[...]
    for ref in refs[:count]:
        value = value + ref[...].astype(F32)
    refs[-1][...] = value.astype(refs[-1].dtype)


def total(own, others, dtype, after):
    return pl.pallas_call(
        functools.partial(total_kernel, len(others)),
        out_shape=array(own.shape, dtype),
        in_specs=[VMEM] * (1 + len(others)) + [ANYWHERE],
        out_specs=VMEM,
        compiler_params=params(16),
        cost_estimate=COST,
        name="total",
    )(own, *others, after)


def local(tokens, cotangent, experts, mixing, gate_matrix, up_matrix, down_matrix):
    expert_count = lax.axis_size("expert")
    inner = min(4, expert_count)
    outer = expert_count // inner
    tok_rows, top = experts.shape
    cap = 2 * tok_rows * top // expert_count
    weight_gate, weight_up, weight_down = gate_matrix[0], up_matrix[0], down_matrix[0]

    def swap(value, mask):
        pairs = [(device, device ^ mask) for device in range(expert_count)]
        return lax.ppermute(value, "expert", pairs)

    def swap_inner(values):
        return [values[0]] + [swap(values[which], which) for which in range(1, inner)]

    core = lax.axis_index("dp").astype(jnp.int32)
    plane_ids = jnp.bitwise_xor(lax.axis_index("expert").astype(jnp.int32), jnp.arange(inner, dtype=jnp.int32))
    ids = jnp.concatenate([plane_ids, jnp.stack([core, 1 - core])])
    order = list(range(2, outer)) + [1] if outer > 1 else []
    places = [0] + order
    packed = {0: pack(tokens, cotangent, experts, mixing)}
    arrived, returned, partial, kept = {}, {}, [], {}
    saved = []

    def fetch(plane):
        low = plane & -plane
        source = plane ^ low
        packed[plane] = swap(kept[source] if source else packed[0], low * inner)

    def send(plane, after):
        onward = [other for other in order if other ^ (other & -other) == plane and plane]
        sent = list(select(ids, packed[plane], cap, top, bool(onward), after))
        if onward:
            kept[plane] = sent.pop()
        arrived[plane] = swap_inner(sent)
        for other in onward:
            fetch(other)
        return sent[0]

    def work(plane, after):
        pair_cot, saved[:] = expert(
            arrived[plane], weights, saved, places.index(plane), outer, after
        )
        returned[plane] = swap_inner(pair_cot)
        return pair_cot[0]

    def give_back(plane, after, estimate=COST):
        value = expand(ids, packed[plane], returned[plane], top, BF16, estimate, after)
        partial.append(swap(value, plane * inner))
        return value

    for plane in order:
        if plane & (plane - 1) == 0:
            fetch(plane)
    last = send(0, [])
    weights = flip(weight_gate, weight_up, weight_down, last)
    last = work(0, [])
    for plane in order[:2]:
        last = send(plane, [last, packed[order[-1]]])
        if plane == order[0]:
            own = expand(ids, packed[0], returned[0], top, F32, COST, last)
            last = own
    if not order:
        own = expand(ids, packed[0], returned[0], top, F32, COST, last)
    for which, plane in enumerate(order):
        last = work(plane, [last])
        if which + 2 < len(order):
            last = send(order[which + 2], [last])
        if which >= 1:
            last = give_back(order[which - 1], last)
    if len(partial) > 1:
        own = total(own, partial[:-1], F32, last)
        last = own
        del partial[:-1]
    (other_half,) = grads(ids, saved, [], last)
    received = lax.ppermute(other_half, "dp", [(0, 1), (1, 0)])
    last = other_half
    if order:
        last = give_back(order[-1], last, LONG)
    gate_grad, up_grad, down_grad = grads(ids, saved, [received], last)
    input_grad = total(own, partial, BF16, gate_grad)
    return (input_grad, gate_grad[None], up_grad[None], down_grad[None])


def solution(mesh):
    return jax.shard_map(
        local,
        mesh=mesh,
        in_specs=(
            P(("dp", "expert"), None),
            P(("dp", "expert"), None),
            P(("dp", "expert"), None),
            P(("dp", "expert"), None),
            P("expert", None, None),
            P("expert", None, None),
            P("expert", None, None),
        ),
        out_specs=(
            P(("dp", "expert"), None),
            P("expert", "dp", None),
            P("expert", "dp", None),
            P("expert", "dp", None),
        ),
        check_vma=False,
    )
```

```python
import functools

import jax
import jax.numpy as jnp
from jax import lax
from jax.experimental import pallas as pl
from jax.experimental.pallas import tpu as pltpu
from jax.sharding import PartitionSpec as P

BF16 = jnp.bfloat16
F32 = jnp.float32
META = 16
PARAMS = pltpu.CompilerParams(vmem_limit_bytes=8 << 20)
LARGE = pltpu.CompilerParams(vmem_limit_bytes=18 << 20)
COST = pl.CostEstimate(flops=1, transcendentals=0, bytes_accessed=1)
LONG = pl.CostEstimate(flops=1 << 37, transcendentals=0, bytes_accessed=1 << 27)
VMEM = pl.BlockSpec(memory_space=pltpu.VMEM)
SMEM = pl.BlockSpec(memory_space=pltpu.SMEM)
ANYWHERE = pl.BlockSpec(memory_space=pl.ANY)
HBM = pl.BlockSpec(memory_space=pltpu.HBM)


def dot(left, right, dims=((1,), (0,))):
    return lax.dot_general(left, right, (dims, ((), ())), preferred_element_type=F32)


def array(shape, dtype=BF16):
    return jax.ShapeDtypeStruct(shape, dtype)


def in_hbm(*values):
    return [pltpu.with_memory_space_constraint(value, pltpu.HBM) for value in values]


def in_vmem(*values):
    return [pltpu.with_memory_space_constraint(value, pltpu.VMEM) for value in values]


def resident(*shape, dtype=BF16):
    return pltpu.VMEM(shape, dtype)


def pack_kernel(in_ref, cot_ref, experts_ref, mixing_ref, out_ref, block_ref, sems):
    tokens, model = in_ref.shape
    targets = [out_ref.at[part * tokens : (part + 1) * tokens] for part in range(2)]
    copies = [
        pltpu.make_async_copy(source, target, sems.at[which])
        for which, (source, target) in enumerate(zip((in_ref, cot_ref), targets))
    ]
    for copy in copies:
        copy.start()
    mixing = mixing_ref[...]
    high = mixing.astype(BF16).astype(F32)
    middle = (mixing - high).astype(BF16).astype(F32)
    low = mixing - high - middle
    block = [experts_ref[...].astype(F32), high, middle, low]
    if META > 4 * mixing.shape[0]:
        block.append(jnp.zeros((META - 4 * mixing.shape[0], tokens), F32))
    block_ref[:, :tokens] = jnp.concatenate(block, axis=0).astype(BF16)
    block_ref[:, tokens:] = jnp.zeros((META, model - tokens), BF16)
    copies.append(pltpu.make_async_copy(block_ref, out_ref.at[2 * tokens :], sems.at[2]))
    copies[2].start()
    for copy in copies:
        copy.wait()


def pack(tokens, cotangent, experts, mixing):
    rows, model = tokens.shape
    return pl.pallas_call(
        pack_kernel,
        out_shape=array((2 * rows + META, model)),
        in_specs=[HBM, HBM, VMEM, VMEM],
        out_specs=HBM,
        scratch_shapes=[pltpu.VMEM((META, model), BF16), pltpu.SemaphoreType.DMA((3,))],
        compiler_params=PARAMS,
        cost_estimate=COST,
        name="pack",
    )(*in_hbm(tokens, cotangent), experts.T, mixing.T)


def slot_masks(ids_ref, block, count, cap, top):
    block = block.astype(F32)
    chosen, high, middle, low = (block[top * part : top * (part + 1)] for part in range(4))
    mixing = (high + middle) + low
    tokens = chosen.shape[1]
    earlier = lax.broadcasted_iota(jnp.int32, (tokens, tokens), 0)
    later = lax.broadcasted_iota(jnp.int32, (tokens, tokens), 1)
    before = (earlier < later).astype(F32)
    slot = lax.broadcasted_iota(jnp.int32, (cap, tokens), 0).astype(F32)
    named, weights = [], []
    for which in range(count):
        hit = chosen == ids_ref[which].astype(F32)
        named.append(jnp.sum(jnp.where(hit, 1.0, 0.0), axis=0, keepdims=True))
        weights.append(jnp.sum(jnp.where(hit, mixing, 0.0), axis=0, keepdims=True))
    position = dot(jnp.concatenate(named, axis=0), before)
    onehot, slot_weight = [], []
    for which in range(count):
        here = (slot == position[which : which + 1]) & (named[which] > 0.5)
        onehot.append(jnp.where(here, 1.0, 0.0))
        slot_weight.append(jnp.sum(jnp.where(here, weights[which], 0.0), axis=1, keepdims=True))
    return jnp.concatenate(onehot, axis=0), jnp.concatenate(slot_weight, axis=0)


def select_kernel(count, top, keep, ids_ref, packed_ref, *refs):
    outs = refs[-keep - count : len(refs) - keep]
    cap = outs[0].shape[1]
    height, model = packed_ref.shape
    tokens = (height - META) // 2
    masks, weight = slot_masks(ids_ref, packed_ref[2 * tokens :, :tokens], count, cap, top)
    onehot = masks.astype(BF16)
    step = min(512, model)
    for start in range(0, model, step):
        columns = slice(start, start + step)
        rows = dot(onehot, packed_ref[:tokens, columns]).astype(BF16)
        cots = (dot(onehot, packed_ref[tokens : 2 * tokens, columns]) * weight).astype(BF16)
        for which in range(count):
            part = slice(which * cap, (which + 1) * cap)
            outs[which][0, :, columns] = rows[part]
            outs[which][1, :, columns] = cots[part]
    if keep:
        refs[-1][...] = packed_ref[...]


def select(ids, packed, cap, top, keep, after):
    count = ids.shape[0] - 2
    model = packed.shape[1]
    return pl.pallas_call(
        functools.partial(select_kernel, count, top, int(keep)),
        out_shape=[array((2, cap, model))] * count + [array(packed.shape)] * keep,
        in_specs=[SMEM, VMEM] + [ANYWHERE] * len(after),
        out_specs=[VMEM] * (count + keep),
        compiler_params=PARAMS,
        cost_estimate=COST,
        name="select",
    )(ids, packed, *after)


def flip_kernel(gate_in, up_in, down_in, _, gate_ref, up_ref, both_ref, flipped_ref, down, sems):
    copies = [
        pltpu.make_async_copy(source, target, sems.at[which])
        for which, (source, target) in enumerate(
            ((gate_in, gate_ref), (up_in, up_ref), (down_in, down))
        )
    ]
    for copy in copies:
        copy.start()
    model, units = gate_ref.shape
    step = min(512, model)
    for which, source in enumerate((gate_ref, up_ref)):
        copies[which].wait()
        for start in range(0, model, step):
            both_ref[which * units : (which + 1) * units, start : start + step] = source[
                start : start + step, :
            ].T
    copies[2].wait()
    for start in range(0, model, step):
        flipped_ref[start : start + step, :] = down[:, start : start + step].T


def flip(weight_gate, weight_up, weight_down, after):
    model, units = weight_gate.shape
    return pl.pallas_call(
        flip_kernel,
        in_specs=[HBM] * 3 + [ANYWHERE],
        out_specs=[VMEM] * 4,
        out_shape=[
            resident(model, units),
            resident(model, units),
            resident(2 * units, model),
            resident(model, units),
        ],
        scratch_shapes=[pltpu.VMEM((units, model), BF16), pltpu.SemaphoreType.DMA((3,))],
        compiler_params=PARAMS,
        cost_estimate=COST,
        name="flip",
    )(*in_hbm(weight_gate, weight_up, weight_down), after)


def expert_kernel(count, *refs):
    ins = refs[:count]
    gate_ref, up_ref, both_ref, flipped_ref = refs[count : count + 4]
    outs = refs[-count - 4 : -4]
    rows_ref, cots_ref, pair_units_ref, hidden_ref = refs[-4:]
    cap = ins[0].shape[1]
    model, units = gate_ref.shape
    for which in range(count):
        part = slice(which * cap, (which + 1) * cap)
        rows_ref[part, :] = ins[which][0]
        cots_ref[part, :] = ins[which][1]
    block = min(256, units)
    for start in range(0, units, block):
        columns = slice(start, start + block)
        pre_gate = dot(rows_ref[...], gate_ref[:, columns])
        pre_up = dot(rows_ref[...], up_ref[:, columns])
        hidden_cot = dot(cots_ref[...], flipped_ref[:, columns])
        sigmoid_gate = jax.nn.sigmoid(pre_gate)
        activated = pre_gate * sigmoid_gate
        hidden_ref[:, columns] = (activated * pre_up).astype(BF16)
        pair_units_ref[:, columns] = (
            hidden_cot * pre_up * sigmoid_gate * (1.0 + pre_gate * (1.0 - sigmoid_gate))
        ).astype(BF16)
        pair_units_ref[:, units + start : units + start + block] = (
            hidden_cot * activated
        ).astype(BF16)
    block = min(512, model)
    for start in range(0, model, block):
        columns = slice(start, start + block)
        pair_cot = dot(pair_units_ref[...], both_ref[:, columns]).astype(BF16)
        for which in range(count):
            outs[which][:, columns] = pair_cot[which * cap : (which + 1) * cap]


def expert(arrived, weights, after):
    count = len(arrived)
    _, cap, model = arrived[0].shape
    units = weights[0].shape[1]
    rows = count * cap
    result = pl.pallas_call(
        functools.partial(expert_kernel, count),
        in_specs=[VMEM] * (count + 4) + [ANYWHERE] * len(after),
        out_specs=[VMEM] * (count + 4),
        out_shape=[array((cap, model))] * count
        + [
            resident(rows, model),
            resident(rows, model),
            resident(rows, 2 * units),
            resident(rows, units),
        ],
        compiler_params=PARAMS,
        cost_estimate=COST,
        name="expert",
    )(*arrived, *in_vmem(*weights), *after)
    return result[:count], result[count:]


STEPS = 4


def gather_kernel(first, rows_ref, cots_ref, pair_units_ref, hidden_ref, *refs):
    both_ref, down_ref = refs[-2:]
    model, units = rows_ref.shape[1], hidden_ref.shape[1]
    block = model // (2 * STEPS)
    for start in range(0, model, block):
        part = slice(start, start + block)
        value = dot(rows_ref[:, part].T, pair_units_ref[...])
        both_ref[part, :] = value if first else both_ref[part, :] + value
    block = min(256, units)
    for start in range(0, units, block):
        part = slice(start, start + block)
        value = dot(hidden_ref[:, part].T, cots_ref[...])
        down_ref[part, :] = value if first else down_ref[part, :] + value


def gather(kept, sums, after):
    model, units = kept[0].shape[1], kept[3].shape[1]
    return pl.pallas_call(
        functools.partial(gather_kernel, not sums),
        in_specs=[VMEM] * (4 + len(sums)) + [ANYWHERE],
        out_specs=[VMEM] * 2,
        out_shape=[resident(model, 2 * units, dtype=F32), resident(units, model, dtype=F32)],
        input_output_aliases={4 + which: which for which in range(len(sums))},
        compiler_params=PARAMS,
        cost_estimate=COST,
        name="gather",
    )(*in_vmem(*kept), *in_vmem(*sums), after)


def lend_kernel(ids_ref, rows_ref, cots_ref, pair_units_ref, hidden_ref, both_ref, down_ref, *refs):
    sent_ref = refs[-1]
    model, units = rows_ref.shape[1], hidden_ref.shape[1]
    half = ids_ref[ids_ref.shape[0] - 1]
    height, width = model // 2 // STEPS, model // STEPS
    rest = units // 2 - height
    fold = height // rest
    part = width // fold
    units_half = pl.multiple_of(half * (units // 2), 128)
    flipped_hidden = hidden_ref[:, pl.ds(units_half, units // 2)].T
    for step in range(STEPS):
        at = slice(step * height, (step + 1) * height)
        across = slice(step * width, (step + 1) * width)
        begin = pl.multiple_of(half * (model // 2) + step * height, 128)
        both = dot(rows_ref[:, pl.ds(begin, height)].T, pair_units_ref[...])
        sent_ref[at, : 2 * units] = (both + both_ref[pl.ds(begin, height), :]).astype(BF16)
        down = dot(flipped_hidden, cots_ref[:, across]) + down_ref[
            pl.ds(units_half, units // 2), across
        ]
        down = down.astype(BF16)
        sent_ref[at, 2 * units : 2 * units + width] = down[:height]
        for which in range(fold):
            lower = slice(step * height + which * rest, step * height + (which + 1) * rest)
            sent_ref[lower, 2 * units + width :] = down[height:, which * part : (which + 1) * part]


def lend(ids, kept, sums, after):
    model, units = kept[0].shape[1], kept[3].shape[1]
    return pl.pallas_call(
        lend_kernel,
        in_specs=[SMEM] + [VMEM] * 6 + [ANYWHERE],
        out_specs=VMEM,
        out_shape=array((model // 2, 2 * units + units // 2 * 2)),
        compiler_params=LARGE,
        cost_estimate=LONG,
        name="lend",
    )(ids, *in_vmem(*kept), *in_vmem(*sums), after)


def finish_kernel(ids_ref, both_ref, down_ref, other, _, gate_out, up_out, down_out, token, gate_ref, up_ref, own_ref, sems):
    model, units = both_ref.shape[0], down_ref.shape[0]
    half = ids_ref[ids_ref.shape[0] - 2]
    height, width = model // 2 // STEPS, model // STEPS
    rest = units // 2 - height
    fold = height // rest
    part = width // fold
    token[...] = jnp.zeros(token.shape, F32)
    units_half = pl.multiple_of(half * (units // 2), 128)
    copies = []
    for step in range(STEPS):
        at = slice(step * height, (step + 1) * height)
        across = slice(step * width, (step + 1) * width)
        begin = pl.multiple_of(half * (model // 2) + step * height, 128)
        both = both_ref[pl.ds(begin, height), :] + other[at, : 2 * units].astype(F32)
        gate_ref[at, :] = both[:, :units]
        up_ref[at, :] = both[:, units:]
        own_ref[:height, across] = down_ref[pl.ds(units_half, height), across] + other[
            at, 2 * units : 2 * units + width
        ].astype(F32)
        lowest = pl.multiple_of(units_half + height, 128)
        for which in range(fold):
            lower = slice(step * height + which * rest, step * height + (which + 1) * rest)
            target = slice(step * width + which * part, step * width + (which + 1) * part)
            own_ref[height:, target] = down_ref[pl.ds(lowest, rest), target] + other[
                lower, 2 * units + width :
            ].astype(F32)
        moves = (
            (gate_ref.at[at], gate_out.at[at]),
            (up_ref.at[at], up_out.at[at]),
            (own_ref.at[:, across], down_out.at[:, across]),
        )
        for which, (source, target) in enumerate(moves):
            copy = pltpu.make_async_copy(source, target, sems.at[step, which])
            copy.start()
            copies.append(copy)
    for copy in copies:
        copy.wait()


def finish(ids, sums, received, after):
    model, units = sums[0].shape[0], sums[1].shape[0]
    shapes = [(model // 2, units), (model // 2, units), (units // 2, model)]
    return pl.pallas_call(
        finish_kernel,
        in_specs=[SMEM] + [VMEM] * 3 + [ANYWHERE],
        out_specs=[HBM] * 3 + [VMEM],
        out_shape=[array(shape, F32) for shape in shapes] + [array((8, 128), F32)],
        scratch_shapes=[pltpu.VMEM(shape, F32) for shape in shapes]
        + [pltpu.SemaphoreType.DMA((STEPS, 3))],
        compiler_params=LARGE,
        cost_estimate=LONG,
        name="finish",
    )(ids, *in_vmem(*sums), received, after)


def expand_kernel(count, top, ids_ref, meta_ref, *refs):
    back, out = refs[:count], refs[-1]
    cap, model = back[0].shape
    onehot, _ = slot_masks(ids_ref, meta_ref[...], count, cap, top)
    spread = onehot.T.astype(BF16)
    step = min(512, model)
    for start in range(0, model, step):
        columns = slice(start, start + step)
        value = dot(spread, jnp.concatenate([ref[:, columns] for ref in back], axis=0))
        out[:, columns] = value.astype(out.dtype)


def expand(ids, packed, back, top, dtype, estimate, after):
    count = len(back)
    cap, model = back[0].shape
    tokens = (packed.shape[0] - META) // 2
    whole = lambda *shape: pl.BlockSpec(shape, lambda s: (0, 0))
    return pl.pallas_call(
        functools.partial(expand_kernel, count, top),
        grid=(1,),
        out_shape=array((tokens, model), dtype),
        in_specs=[SMEM, pl.BlockSpec((META, tokens), lambda s: (2 * tokens // META, 0))]
        + [whole(cap, model)] * count
        + [ANYWHERE],
        out_specs=whole(tokens, model),
        compiler_params=PARAMS,
        cost_estimate=estimate,
        name="expand",
    )(ids, packed, *back, after)


def total_kernel(count, own_ref, *refs):
    value = own_ref[...]
    for ref in refs[:count]:
        value = value + ref[...].astype(F32)
    refs[-1][...] = value.astype(refs[-1].dtype)


def total(own, others, dtype, after):
    return pl.pallas_call(
        functools.partial(total_kernel, len(others)),
        out_shape=array(own.shape, dtype),
        in_specs=[VMEM] * (1 + len(others)) + [ANYWHERE],
        out_specs=VMEM,
        compiler_params=PARAMS,
        cost_estimate=COST,
        name="total",
    )(own, *others, after)


def local(tokens, cotangent, experts, mixing, gate_matrix, up_matrix, down_matrix):
    expert_count = lax.axis_size("expert")
    inner = min(4, expert_count)
    outer = expert_count // inner
    tok_rows, top = experts.shape
    cap = 2 * tok_rows * top // expert_count
    weight_gate, weight_up, weight_down = gate_matrix[0], up_matrix[0], down_matrix[0]

    def swap(value, mask):
        pairs = [(device, device ^ mask) for device in range(expert_count)]
        return lax.ppermute(value, "expert", pairs)

    def swap_inner(values):
        return [values[0]] + [swap(values[which], which) for which in range(1, inner)]

    core = lax.axis_index("dp").astype(jnp.int32)
    plane_ids = jnp.bitwise_xor(lax.axis_index("expert").astype(jnp.int32), jnp.arange(inner, dtype=jnp.int32))
    ids = jnp.concatenate([plane_ids, jnp.stack([core, 1 - core])])
    order = list(range(2, outer)) + [1] if outer > 1 else []
    packed = {0: pack(tokens, cotangent, experts, mixing)}
    arrived, returned, partial, kept = {}, {}, [], {}
    saved, sums = {}, []

    def fetch(plane):
        low = plane & -plane
        source = plane ^ low
        packed[plane] = swap(kept[source] if source else packed[0], low * inner)

    def send(plane, after):
        onward = [other for other in order if other ^ (other & -other) == plane and plane]
        sent = list(select(ids, packed[plane], cap, top, bool(onward), after))
        if onward:
            kept[plane] = sent.pop()
        arrived[plane] = swap_inner(sent)
        for other in onward:
            fetch(other)
        return sent[0]

    def work(plane, after):
        pair_cot, saved[plane] = expert(arrived[plane], weights, after)
        returned[plane] = swap_inner(pair_cot)
        return pair_cot[0]

    def add_up(plane, after):
        sums[:] = gather(saved[plane], sums, after)
        return sums[1]

    def give_back(plane, after, estimate=COST):
        value = expand(ids, packed[plane], returned[plane], top, BF16, estimate, after)
        partial.append(swap(value, plane * inner))
        return value

    for plane in order:
        if plane & (plane - 1) == 0:
            fetch(plane)
    last = send(0, [])
    weights = flip(weight_gate, weight_up, weight_down, last)
    last = work(0, [])
    if order:
        last = add_up(0, last)
    own = expand(ids, packed[0], returned[0], top, F32, COST, last)
    last = own
    for plane in order[:2]:
        last = send(plane, [last, packed[order[-1]]])
    for which, plane in enumerate(order):
        last = work(plane, [last])
        if which + 2 < len(order):
            last = send(order[which + 2], [last])
        if which + 1 < len(order):
            last = add_up(plane, last)
        if which >= 1:
            last = give_back(order[which - 1], last)
    final = order[-1] if order else 0
    other_half = lend(ids, saved[final], sums, last)
    received = lax.ppermute(other_half, "dp", [(0, 1), (1, 0)])
    last = add_up(final, other_half)
    if len(partial) > 1:
        own = total(own, partial[:-1], F32, last)
        last = own
        del partial[:-1]
    if order:
        last = give_back(order[-1], last, LONG)
    gate_grad, up_grad, down_grad, token = finish(ids, sums, received, last)
    input_grad = total(own, partial, BF16, token)
    return (input_grad, gate_grad[None], up_grad[None], down_grad[None])


def solution(mesh):
    return jax.shard_map(
        local,
        mesh=mesh,
        in_specs=(
            P(("dp", "expert"), None),
            P(("dp", "expert"), None),
            P(("dp", "expert"), None),
            P(("dp", "expert"), None),
            P("expert", None, None),
            P("expert", None, None),
            P("expert", None, None),
        ),
        out_specs=(
            P(("dp", "expert"), None),
            P("expert", "dp", None),
            P("expert", "dp", None),
            P("expert", "dp", None),
        ),
        check_vma=False,
    )
```

```python
import functools

import jax
import jax.numpy as jnp
from jax import lax
from jax.experimental import pallas as pl
from jax.experimental.pallas import tpu as pltpu
from jax.sharding import PartitionSpec as P

BF16 = jnp.bfloat16
F32 = jnp.float32
META = 16
OWN_HALF, OTHER_HALF, XOR_IDS = 0, 1, 2
PARAMS = pltpu.CompilerParams(vmem_limit_bytes=14 << 20)
COST = pl.CostEstimate(flops=1, transcendentals=0, bytes_accessed=1)
LONG = pl.CostEstimate(flops=1 << 37, transcendentals=0, bytes_accessed=1 << 27)
VMEM = pl.BlockSpec(memory_space=pltpu.VMEM)
SMEM = pl.BlockSpec(memory_space=pltpu.SMEM)
ANYWHERE = pl.BlockSpec(memory_space=pl.ANY)
HBM = pl.BlockSpec(memory_space=pltpu.HBM)


def dot(left, right, dims=((1,), (0,))):
    return lax.dot_general(left, right, (dims, ((), ())), preferred_element_type=F32)


def array(shape, dtype=BF16):
    return jax.ShapeDtypeStruct(shape, dtype)


def in_hbm(*values):
    return [pltpu.with_memory_space_constraint(value, pltpu.HBM) for value in values]


def in_vmem(*values):
    return [pltpu.with_memory_space_constraint(value, pltpu.VMEM) for value in values]


def resident(*shape):
    return pltpu.VMEM(shape, BF16)


def pack_kernel(in_ref, cot_ref, experts_ref, mixing_ref, out_ref, block_ref, sems):
    tokens, model = in_ref.shape
    targets = [out_ref.at[part * tokens : (part + 1) * tokens] for part in range(2)]
    copies = [
        pltpu.make_async_copy(source, target, sems.at[which])
        for which, (source, target) in enumerate(zip((in_ref, cot_ref), targets))
    ]
    for copy in copies:
        copy.start()
    mixing = mixing_ref[...]
    high = mixing.astype(BF16).astype(F32)
    middle = (mixing - high).astype(BF16).astype(F32)
    low = mixing - high - middle
    block = [experts_ref[...].astype(F32), high, middle, low]
    if META > 4 * mixing.shape[0]:
        block.append(jnp.zeros((META - 4 * mixing.shape[0], tokens), F32))
    block_ref[:, :tokens] = jnp.concatenate(block, axis=0).astype(BF16)
    block_ref[:, tokens:] = jnp.zeros((META, model - tokens), BF16)
    copies.append(pltpu.make_async_copy(block_ref, out_ref.at[2 * tokens :], sems.at[2]))
    copies[2].start()
    for copy in copies:
        copy.wait()


def pack(tokens, cotangent, experts, mixing):
    rows, model = tokens.shape
    return pl.pallas_call(
        pack_kernel,
        out_shape=array((2 * rows + META, model)),
        in_specs=[HBM, HBM, VMEM, VMEM],
        out_specs=HBM,
        scratch_shapes=[pltpu.VMEM((META, model), BF16), pltpu.SemaphoreType.DMA((3,))],
        compiler_params=PARAMS,
        cost_estimate=COST,
        name="pack",
    )(*in_hbm(tokens, cotangent), experts.T, mixing.T)


def slot_masks(ids_ref, first, block, count, cap, top):
    block = block.astype(F32)
    chosen, high, middle, low = (block[top * part : top * (part + 1)] for part in range(4))
    mixing = (high + middle) + low
    tokens = chosen.shape[1]
    earlier = lax.broadcasted_iota(jnp.int32, (tokens, tokens), 0)
    later = lax.broadcasted_iota(jnp.int32, (tokens, tokens), 1)
    before = (earlier < later).astype(F32)
    slot = lax.broadcasted_iota(jnp.int32, (cap, tokens), 0).astype(F32)
    named, weights = [], []
    for which in range(count):
        hit = chosen == ids_ref[first + which].astype(F32)
        named.append(jnp.sum(jnp.where(hit, 1.0, 0.0), axis=0, keepdims=True))
        weights.append(jnp.sum(jnp.where(hit, mixing, 0.0), axis=0, keepdims=True))
    position = dot(jnp.concatenate(named, axis=0), before)
    onehot, slot_weight = [], []
    for which in range(count):
        here = (slot == position[which : which + 1]) & (named[which] > 0.5)
        onehot.append(jnp.where(here, 1.0, 0.0))
        slot_weight.append(jnp.sum(jnp.where(here, weights[which], 0.0), axis=1, keepdims=True))
    return jnp.concatenate(onehot, axis=0), jnp.concatenate(slot_weight, axis=0)


def select_kernel(count, top, keep, ids_ref, packed_ref, *refs):
    outs = refs[-keep - count : len(refs) - keep]
    cap = outs[0].shape[1]
    height, model = packed_ref.shape
    tokens = (height - META) // 2
    masks, weight = slot_masks(ids_ref, XOR_IDS, packed_ref[2 * tokens :, :tokens], count, cap, top)
    onehot = masks.astype(BF16)
    step = min(512, model)
    for start in range(0, model, step):
        columns = slice(start, start + step)
        rows = dot(onehot, packed_ref[:tokens, columns]).astype(BF16)
        cots = (dot(onehot, packed_ref[tokens : 2 * tokens, columns]) * weight).astype(BF16)
        for which in range(count):
            part = slice(which * cap, (which + 1) * cap)
            outs[which][0, :, columns] = rows[part]
            outs[which][1, :, columns] = cots[part]
    if keep:
        refs[-1][...] = packed_ref[...]


def select(ids, packed, cap, top, keep, after):
    count = (ids.shape[0] - XOR_IDS) // 2
    model = packed.shape[1]
    return pl.pallas_call(
        functools.partial(select_kernel, count, top, int(keep)),
        out_shape=[array((2, cap, model))] * count + [array(packed.shape)] * keep,
        in_specs=[SMEM, VMEM] + [ANYWHERE] * len(after),
        out_specs=[VMEM] * (count + keep),
        compiler_params=PARAMS,
        cost_estimate=COST,
        name="select",
    )(ids, packed, *after)


def flip_kernel(gate_in, up_in, down_in, _, gate_ref, up_ref, both_ref, flipped_ref, down, sems):
    copies = [
        pltpu.make_async_copy(source, target, sems.at[which])
        for which, (source, target) in enumerate(
            ((gate_in, gate_ref), (up_in, up_ref), (down_in, down))
        )
    ]
    for copy in copies:
        copy.start()
    model, units = gate_ref.shape
    step = min(512, model)
    for which, source in enumerate((gate_ref, up_ref)):
        copies[which].wait()
        for start in range(0, model, step):
            both_ref[which * units : (which + 1) * units, start : start + step] = source[
                start : start + step, :
            ].T
    copies[2].wait()
    for start in range(0, model, step):
        flipped_ref[start : start + step, :] = down[:, start : start + step].T


def flip(weight_gate, weight_up, weight_down, after):
    model, units = weight_gate.shape
    return pl.pallas_call(
        flip_kernel,
        in_specs=[HBM] * 3 + [ANYWHERE],
        out_specs=[VMEM] * 4,
        out_shape=[
            resident(model, units),
            resident(model, units),
            resident(2 * units, model),
            resident(model, units),
        ],
        scratch_shapes=[pltpu.VMEM((units, model), BF16), pltpu.SemaphoreType.DMA((3,))],
        compiler_params=PARAMS,
        cost_estimate=COST,
        name="flip",
    )(*in_hbm(weight_gate, weight_up, weight_down), after)


def expert_kernel(count, place, ids_ref, *refs):
    ins = refs[:count]
    gate_ref, up_ref, both_ref, flipped_ref = refs[count : count + 4]
    out_ref, rows_ref, cots_ref, pair_units_ref, hidden_ref = refs[-5:]
    cap = ins[0].shape[1]
    model, units = gate_ref.shape
    begin = place * count * cap
    here = slice(begin, begin + count * cap)
    for which in range(count):
        part = slice(begin + which * cap, begin + (which + 1) * cap)
        rows_ref[part, :] = ins[which][0]
        cots_ref[part, :] = ins[which][1]
    block = min(256, units)
    for start in range(0, units, block):
        columns = slice(start, start + block)
        pre_gate = dot(rows_ref[here, :], gate_ref[:, columns])
        pre_up = dot(rows_ref[here, :], up_ref[:, columns])
        hidden_cot = dot(cots_ref[here, :], flipped_ref[:, columns])
        sigmoid_gate = jax.nn.sigmoid(pre_gate)
        activated = pre_gate * sigmoid_gate
        hidden_ref[here, columns] = (activated * pre_up).astype(BF16)
        pair_units_ref[here, columns] = (
            hidden_cot * pre_up * sigmoid_gate * (1.0 + pre_gate * (1.0 - sigmoid_gate))
        ).astype(BF16)
        pair_units_ref[here, units + start : units + start + block] = (
            hidden_cot * activated
        ).astype(BF16)
    block = min(512, model)
    for start in range(0, model, block):
        columns = slice(start, start + block)
        pair_cot = dot(pair_units_ref[here, :], both_ref[:, columns]).astype(BF16)
        for which in range(count):
            chip = lax.rem(ids_ref[XOR_IDS + which], count)
            out_ref[chip, :, columns] = pair_cot[which * cap : (which + 1) * cap]


def expert(ids, arrived, weights, saved, place, places, after):
    count = len(arrived)
    _, cap, model = arrived[0].shape
    units = weights[0].shape[1]
    total_rows = places * count * cap
    result = pl.pallas_call(
        functools.partial(expert_kernel, count, place),
        in_specs=[SMEM] + [VMEM] * (count + 4 + len(saved)) + [ANYWHERE] * len(after),
        out_specs=[VMEM] * 5,
        out_shape=[
            array((count, cap, model)),
            resident(total_rows, model),
            resident(total_rows, model),
            resident(total_rows, 2 * units),
            resident(total_rows, units),
        ],
        input_output_aliases={count + 5 + which: 1 + which for which in range(len(saved))},
        compiler_params=PARAMS,
        cost_estimate=COST,
        name="expert",
    )(ids, *arrived, *in_vmem(*weights, *saved), *after)
    return result[0], result[1:]


STEPS = 4


def grads_kernel(add, ids_ref, rows_ref, cots_ref, pair_units_ref, hidden_ref, *refs):
    units, model = hidden_ref.shape[1], rows_ref.shape[1]
    half = ids_ref[OWN_HALF if add else OTHER_HALF]
    height, width = model // 2 // STEPS, model // STEPS
    rest = units // 2 - height
    fold = height // rest
    part = width // fold
    if add:
        other_in, _, gate_out, up_out, down_out, token, gate_ref, up_ref, down_ref, other_ref, sems, other_sems = refs
        token[...] = jnp.zeros(token.shape, F32)
    else:
        _, sent_out, sent_ref, sems = refs
    own_units = pl.ds(pl.multiple_of(half * (units // 2), 128), units // 2)
    flipped_hidden = hidden_ref[:, own_units].T

    def fetch(step):
        at = slice(step * height, (step + 1) * height)
        slot = step % 2
        return pltpu.make_async_copy(other_in.at[at], other_ref.at[slot], other_sems.at[slot])

    def moves(step):
        at = slice(step * height, (step + 1) * height)
        across = slice(step * width, (step + 1) * width)
        slot = step % 2
        if add:
            pairs = (
                (gate_ref.at[slot], gate_out.at[at]),
                (up_ref.at[slot], up_out.at[at]),
                (down_ref.at[slot], down_out.at[:, across]),
            )
        else:
            pairs = ((sent_ref.at[slot], sent_out.at[at]),)
        return [
            pltpu.make_async_copy(source, target, sems.at[slot, which])
            for which, (source, target) in enumerate(pairs)
        ]

    if add:
        fetch(0).start()
    for step in range(STEPS):
        slot = step % 2
        across = slice(step * width, (step + 1) * width)
        own_rows = pl.ds(pl.multiple_of(half * (model // 2) + step * height, 128), height)
        both = dot(rows_ref[:, own_rows].T, pair_units_ref[...])
        down = dot(flipped_hidden, cots_ref[:, across])
        if step >= 2:
            for copy in moves(step - 2):
                copy.wait()
        if add:
            fetch(step).wait()
            if step + 1 < STEPS:
                fetch(step + 1).start()
            gate_ref[slot] = both[:, :units] + other_ref[slot, :, :units].astype(F32)
            up_ref[slot] = both[:, units:] + other_ref[slot, :, units : 2 * units].astype(F32)
            down_ref[slot, :height, :] = down[:height] + other_ref[
                slot, :, 2 * units : 2 * units + width
            ].astype(F32)
            for which in range(fold):
                columns = slice(which * part, (which + 1) * part)
                lower = slice(which * rest, (which + 1) * rest)
                down_ref[slot, height:, columns] = down[height:, columns] + other_ref[
                    slot, lower, 2 * units + width :
                ].astype(F32)
        else:
            sent_ref[slot, :, : 2 * units] = both.astype(BF16)
            down = down.astype(BF16)
            sent_ref[slot, :, 2 * units : 2 * units + width] = down[:height]
            for which in range(fold):
                lower = slice(which * rest, (which + 1) * rest)
                sent_ref[slot, lower, 2 * units + width :] = down[
                    height:, which * part : (which + 1) * part
                ]
        for copy in moves(step):
            copy.start()
    for step in range(STEPS - 2, STEPS):
        for copy in moves(step):
            copy.wait()


def grads(ids, saved, received, after):
    model, units = saved[0].shape[1], saved[3].shape[1]
    height = model // 2 // STEPS
    sent_width = 3 * units
    add = bool(received)
    if add:
        shapes = [(model // 2, units), (model // 2, units), (units // 2, model)]
        stages = [(2, height, units), (2, height, units), (2, units // 2, model // STEPS)]
        dtype = F32
    else:
        shapes, stages, dtype = [(model // 2, sent_width)], [(2, height, sent_width)], BF16
    scratch = [pltpu.VMEM(shape, dtype) for shape in stages]
    if add:
        scratch.append(pltpu.VMEM((2, height, sent_width), BF16))
    scratch.append(pltpu.SemaphoreType.DMA((2, len(shapes))))
    if add:
        scratch.append(pltpu.SemaphoreType.DMA((2,)))
    return pl.pallas_call(
        functools.partial(grads_kernel, add),
        in_specs=[SMEM] + [VMEM] * 4 + [ANYWHERE] * (1 + add),
        out_specs=[HBM] * len(shapes) + [VMEM] * add,
        out_shape=[array(shape, dtype) for shape in shapes] + [array((8, 128), F32)] * add,
        scratch_shapes=scratch,
        compiler_params=PARAMS,
        cost_estimate=LONG,
        name="grads",
    )(ids, *in_vmem(*saved), *received, after)


def expand_kernel(top, ids_ref, meta_ref, back, _, out):
    count, cap, model = back.shape
    onehot, _ = slot_masks(ids_ref, XOR_IDS + count, meta_ref[...], count, cap, top)
    spread = onehot.T.astype(BF16)
    step = min(512, model)
    for start in range(0, model, step):
        columns = slice(start, start + step)
        pairs = jnp.concatenate([back[which, :, columns] for which in range(count)], axis=0)
        out[:, columns] = dot(spread, pairs).astype(out.dtype)


def expand(ids, packed, back, top, dtype, estimate, after):
    count, cap, model = back.shape
    tokens = (packed.shape[0] - META) // 2
    whole = lambda *shape: pl.BlockSpec(shape, lambda s: (0,) * len(shape))
    return pl.pallas_call(
        functools.partial(expand_kernel, top),
        grid=(1,),
        out_shape=array((tokens, model), dtype),
        in_specs=[
            SMEM,
            pl.BlockSpec((META, tokens), lambda s: (2 * tokens // META, 0)),
            whole(count, cap, model),
            ANYWHERE,
        ],
        out_specs=whole(tokens, model),
        compiler_params=PARAMS,
        cost_estimate=estimate,
        name="expand",
    )(ids, packed, back, after)


def total_kernel(count, own_ref, *refs):
    value = own_ref[...]
    for ref in refs[:count]:
        value = value + ref[...].astype(F32)
    refs[-1][...] = value.astype(refs[-1].dtype)


def total(own, others, dtype, after):
    return pl.pallas_call(
        functools.partial(total_kernel, len(others)),
        out_shape=array(own.shape, dtype),
        in_specs=[VMEM] * (1 + len(others)) + [ANYWHERE],
        out_specs=VMEM,
        compiler_params=PARAMS,
        cost_estimate=COST,
        name="total",
    )(own, *others, after)


def local(tokens, cotangent, experts, mixing, gate_matrix, up_matrix, down_matrix):
    expert_count = lax.axis_size("expert")
    inner = min(4, expert_count)
    outer = expert_count // inner
    tok_rows, top = experts.shape
    cap = 2 * tok_rows * top // expert_count
    weight_gate, weight_up, weight_down = gate_matrix[0], up_matrix[0], down_matrix[0]

    def swap(value, mask):
        pairs = [(device, device ^ mask) for device in range(expert_count)]
        return lax.ppermute(value, "expert", pairs)

    def swap_inner(values):
        return [values[0]] + [swap(values[which], which) for which in range(1, inner)]

    core = lax.axis_index("dp").astype(jnp.int32)
    plane_ids = jnp.bitwise_xor(lax.axis_index("expert").astype(jnp.int32), jnp.arange(inner, dtype=jnp.int32))
    ids = jnp.concatenate([jnp.stack([core, 1 - core]), plane_ids, jnp.sort(plane_ids)])
    order = list(range(2, outer)) + [1] if outer > 1 else []
    places = [0] + order
    packed = {0: pack(tokens, cotangent, experts, mixing)}
    arrived, returned, partial, kept = {}, {}, [], {}
    saved = []

    chips = [list(range(first, first + inner)) for first in range(0, expert_count, inner)]

    def fetch(plane):
        low = plane & -plane
        source = plane ^ low
        packed[plane] = swap(kept[source] if source else packed[0], low * inner)

    def send(plane, after):
        onward = [other for other in order if other ^ (other & -other) == plane and plane]
        sent = list(select(ids, packed[plane], cap, top, bool(onward), after))
        if onward:
            kept[plane] = sent.pop()
        arrived[plane] = swap_inner(sent)
        for other in onward:
            fetch(other)
        return sent[0]

    def work(plane, after):
        pair_cot, saved[:] = expert(
            ids, arrived[plane], weights, saved, places.index(plane), outer, after
        )
        returned[plane] = lax.all_to_all(
            pair_cot, "expert", split_axis=0, concat_axis=0, axis_index_groups=chips, tiled=True
        )
        return pair_cot

    def give_back(plane, after, estimate=COST):
        value = expand(ids, packed[plane], returned[plane], top, BF16, estimate, after)
        partial.append(swap(value, plane * inner))
        return value

    for plane in order:
        if plane & (plane - 1) == 0:
            fetch(plane)
    last = send(0, [])
    weights = flip(weight_gate, weight_up, weight_down, last)
    last = work(0, [])
    own = expand(ids, packed[0], returned[0], top, F32, COST, last)
    last = own
    for plane in order[:2]:
        last = send(plane, [last, packed[order[-1]]])
    for which, plane in enumerate(order):
        last = work(plane, [last])
        if which + 2 < len(order):
            last = send(order[which + 2], [last])
        if which >= 1:
            last = give_back(order[which - 1], last)
    (other_half,) = grads(ids, saved, [], last)
    received = lax.ppermute(other_half, "dp", [(0, 1), (1, 0)])
    last = other_half
    if order:
        last = give_back(order[-1], last, LONG)
    gate_grad, up_grad, down_grad, token = grads(ids, saved, [received], last)
    input_grad = total(own, partial, BF16, token)
    return (input_grad, gate_grad[None], up_grad[None], down_grad[None])


def solution(mesh):
    return jax.shard_map(
        local,
        mesh=mesh,
        in_specs=(
            P(("dp", "expert"), None),
            P(("dp", "expert"), None),
            P(("dp", "expert"), None),
            P(("dp", "expert"), None),
            P("expert", None, None),
            P("expert", None, None),
            P("expert", None, None),
        ),
        out_specs=(
            P(("dp", "expert"), None),
            P("expert", "dp", None),
            P("expert", "dp", None),
            P("expert", "dp", None),
        ),
        check_vma=False,
    )
```

```python
import functools

import jax
import jax.numpy as jnp
from jax import lax
from jax.experimental import pallas as pl
from jax.experimental.pallas import tpu as pltpu
from jax.sharding import PartitionSpec as P

BF16 = jnp.bfloat16
F32 = jnp.float32
META = 16
PARAMS = pltpu.CompilerParams(vmem_limit_bytes=8 << 20)
LARGE = pltpu.CompilerParams(vmem_limit_bytes=15 << 20)
COST = pl.CostEstimate(flops=1, transcendentals=0, bytes_accessed=1)
LONG = pl.CostEstimate(flops=1 << 37, transcendentals=0, bytes_accessed=1 << 27)
VMEM = pl.BlockSpec(memory_space=pltpu.VMEM)
SMEM = pl.BlockSpec(memory_space=pltpu.SMEM)
ANYWHERE = pl.BlockSpec(memory_space=pl.ANY)
HBM = pl.BlockSpec(memory_space=pltpu.HBM)


def dot(left, right, dims=((1,), (0,))):
    return lax.dot_general(left, right, (dims, ((), ())), preferred_element_type=F32)


def array(shape, dtype=BF16):
    return jax.ShapeDtypeStruct(shape, dtype)


def in_hbm(*values):
    return [pltpu.with_memory_space_constraint(value, pltpu.HBM) for value in values]


def in_vmem(*values):
    return [pltpu.with_memory_space_constraint(value, pltpu.VMEM) for value in values]


def resident(*shape, dtype=BF16):
    return pltpu.VMEM(shape, dtype)


def pack_kernel(in_ref, cot_ref, experts_ref, mixing_ref, out_ref, block_ref, sems):
    tokens, model = in_ref.shape
    targets = [out_ref.at[part * tokens : (part + 1) * tokens] for part in range(2)]
    copies = [
        pltpu.make_async_copy(source, target, sems.at[which])
        for which, (source, target) in enumerate(zip((in_ref, cot_ref), targets))
    ]
    for copy in copies:
        copy.start()
    mixing = mixing_ref[...]
    high = mixing.astype(BF16).astype(F32)
    middle = (mixing - high).astype(BF16).astype(F32)
    low = mixing - high - middle
    block = [experts_ref[...].astype(F32), high, middle, low]
    if META > 4 * mixing.shape[0]:
        block.append(jnp.zeros((META - 4 * mixing.shape[0], tokens), F32))
    block_ref[:, :tokens] = jnp.concatenate(block, axis=0).astype(BF16)
    block_ref[:, tokens:] = jnp.zeros((META, model - tokens), BF16)
    copies.append(pltpu.make_async_copy(block_ref, out_ref.at[2 * tokens :], sems.at[2]))
    copies[2].start()
    for copy in copies:
        copy.wait()


def pack(tokens, cotangent, experts, mixing):
    rows, model = tokens.shape
    return pl.pallas_call(
        pack_kernel,
        out_shape=array((2 * rows + META, model)),
        in_specs=[HBM, HBM, VMEM, VMEM],
        out_specs=HBM,
        scratch_shapes=[pltpu.VMEM((META, model), BF16), pltpu.SemaphoreType.DMA((3,))],
        compiler_params=PARAMS,
        cost_estimate=COST,
        name="pack",
    )(*in_hbm(tokens, cotangent), experts.T, mixing.T)


def slot_masks(ids_ref, block, count, cap, top):
    block = block.astype(F32)
    chosen, high, middle, low = (block[top * part : top * (part + 1)] for part in range(4))
    mixing = (high + middle) + low
    tokens = chosen.shape[1]
    earlier = lax.broadcasted_iota(jnp.int32, (tokens, tokens), 0)
    later = lax.broadcasted_iota(jnp.int32, (tokens, tokens), 1)
    before = (earlier < later).astype(F32)
    slot = lax.broadcasted_iota(jnp.int32, (cap, tokens), 0).astype(F32)
    named, weights = [], []
    for which in range(count):
        hit = chosen == ids_ref[which].astype(F32)
        named.append(jnp.sum(jnp.where(hit, 1.0, 0.0), axis=0, keepdims=True))
        weights.append(jnp.sum(jnp.where(hit, mixing, 0.0), axis=0, keepdims=True))
    position = dot(jnp.concatenate(named, axis=0), before)
    onehot, slot_weight = [], []
    for which in range(count):
        here = (slot == position[which : which + 1]) & (named[which] > 0.5)
        onehot.append(jnp.where(here, 1.0, 0.0))
        slot_weight.append(jnp.sum(jnp.where(here, weights[which], 0.0), axis=1, keepdims=True))
    return jnp.concatenate(onehot, axis=0), jnp.concatenate(slot_weight, axis=0)


def select_kernel(count, top, keep, ids_ref, packed_ref, *refs):
    outs = refs[-keep - count : len(refs) - keep]
    cap = outs[0].shape[1]
    height, model = packed_ref.shape
    tokens = (height - META) // 2
    masks, weight = slot_masks(ids_ref, packed_ref[2 * tokens :, :tokens], count, cap, top)
    onehot = masks.astype(BF16)
    step = min(512, model)
    for start in range(0, model, step):
        columns = slice(start, start + step)
        rows = dot(onehot, packed_ref[:tokens, columns]).astype(BF16)
        cots = (dot(onehot, packed_ref[tokens : 2 * tokens, columns]) * weight).astype(BF16)
        for which in range(count):
            part = slice(which * cap, (which + 1) * cap)
            outs[which][0, :, columns] = rows[part]
            outs[which][1, :, columns] = cots[part]
    if keep:
        refs[-1][...] = packed_ref[...]


def select(ids, packed, cap, top, keep, after):
    count = ids.shape[0] - 2
    model = packed.shape[1]
    return pl.pallas_call(
        functools.partial(select_kernel, count, top, int(keep)),
        out_shape=[array((2, cap, model))] * count + [array(packed.shape)] * keep,
        in_specs=[SMEM, VMEM] + [ANYWHERE] * len(after),
        out_specs=[VMEM] * (count + keep),
        compiler_params=PARAMS,
        cost_estimate=COST,
        name="select",
    )(ids, packed, *after)


def flip_kernel(gate_in, up_in, down_in, _, gate_ref, up_ref, both_ref, flipped_ref, down, sems):
    copies = [
        pltpu.make_async_copy(source, target, sems.at[which])
        for which, (source, target) in enumerate(
            ((gate_in, gate_ref), (up_in, up_ref), (down_in, down))
        )
    ]
    for copy in copies:
        copy.start()
    model, units = gate_ref.shape
    step = min(512, model)
    for which, source in enumerate((gate_ref, up_ref)):
        copies[which].wait()
        for start in range(0, model, step):
            both_ref[which * units : (which + 1) * units, start : start + step] = source[
                start : start + step, :
            ].T
    copies[2].wait()
    for start in range(0, model, step):
        flipped_ref[start : start + step, :] = down[:, start : start + step].T


def flip(weight_gate, weight_up, weight_down, after):
    model, units = weight_gate.shape
    return pl.pallas_call(
        flip_kernel,
        in_specs=[HBM] * 3 + [ANYWHERE],
        out_specs=[VMEM] * 4,
        out_shape=[
            resident(model, units),
            resident(model, units),
            resident(2 * units, model),
            resident(model, units),
        ],
        scratch_shapes=[pltpu.VMEM((units, model), BF16), pltpu.SemaphoreType.DMA((3,))],
        compiler_params=PARAMS,
        cost_estimate=COST,
        name="flip",
    )(*in_hbm(weight_gate, weight_up, weight_down), after)


def expert_kernel(count, *refs):
    ins = refs[:count]
    gate_ref, up_ref, both_ref, flipped_ref = refs[count : count + 4]
    outs = refs[-count - 4 : -4]
    rows_ref, cots_ref, pair_units_ref, hidden_ref = refs[-4:]
    cap = ins[0].shape[1]
    model, units = gate_ref.shape
    for which in range(count):
        part = slice(which * cap, (which + 1) * cap)
        rows_ref[part, :] = ins[which][0]
        cots_ref[part, :] = ins[which][1]
    block = min(256, units)
    for start in range(0, units, block):
        columns = slice(start, start + block)
        pre_gate = dot(rows_ref[...], gate_ref[:, columns])
        pre_up = dot(rows_ref[...], up_ref[:, columns])
        hidden_cot = dot(cots_ref[...], flipped_ref[:, columns])
        sigmoid_gate = jax.nn.sigmoid(pre_gate)
        activated = pre_gate * sigmoid_gate
        hidden_ref[:, columns] = (activated * pre_up).astype(BF16)
        pair_units_ref[:, columns] = (
            hidden_cot * pre_up * sigmoid_gate * (1.0 + pre_gate * (1.0 - sigmoid_gate))
        ).astype(BF16)
        pair_units_ref[:, units + start : units + start + block] = (
            hidden_cot * activated
        ).astype(BF16)
    block = min(512, model)
    for start in range(0, model, block):
        columns = slice(start, start + block)
        pair_cot = dot(pair_units_ref[...], both_ref[:, columns]).astype(BF16)
        for which in range(count):
            outs[which][:, columns] = pair_cot[which * cap : (which + 1) * cap]


def expert(arrived, weights, after):
    count = len(arrived)
    _, cap, model = arrived[0].shape
    units = weights[0].shape[1]
    rows = count * cap
    result = pl.pallas_call(
        functools.partial(expert_kernel, count),
        in_specs=[VMEM] * (count + 4) + [ANYWHERE] * len(after),
        out_specs=[VMEM] * (count + 4),
        out_shape=[array((cap, model))] * count
        + [
            resident(rows, model),
            resident(rows, model),
            resident(rows, 2 * units),
            resident(rows, units),
        ],
        compiler_params=PARAMS,
        cost_estimate=COST,
        name="expert",
    )(*arrived, *in_vmem(*weights), *after)
    return result[:count], result[count:]


STEPS = 4


def grads_kernel(planes, add, ids_ref, *refs):
    saved = [refs[4 * which : 4 * which + 4] for which in range(planes)]
    refs = refs[4 * planes :]
    model, units = saved[0][0].shape[1], saved[0][3].shape[1]
    half = ids_ref[ids_ref.shape[0] - (2 if add else 1)]
    height, width = model // 2 // STEPS, model // STEPS
    rest = units // 2 - height
    fold = height // rest
    part = width // fold
    if add:
        other_in, _, gate_out, up_out, down_out, token, gate_ref, up_ref, down_ref, other_ref, sems, other_sems = refs
        token[...] = jnp.zeros(token.shape, F32)
    else:
        _, sent_out, sent_ref, sems = refs
    own_units = pl.ds(pl.multiple_of(half * (units // 2), 128), units // 2)
    flipped_hidden = [kept[3][:, own_units].T for kept in saved]

    def fetch(step):
        at = slice(step * height, (step + 1) * height)
        slot = step % 2
        return pltpu.make_async_copy(other_in.at[at], other_ref.at[slot], other_sems.at[slot])

    def moves(step):
        at = slice(step * height, (step + 1) * height)
        across = slice(step * width, (step + 1) * width)
        slot = step % 2
        if add:
            pairs = (
                (gate_ref.at[slot], gate_out.at[at]),
                (up_ref.at[slot], up_out.at[at]),
                (down_ref.at[slot], down_out.at[:, across]),
            )
        else:
            pairs = ((sent_ref.at[slot], sent_out.at[at]),)
        return [
            pltpu.make_async_copy(source, target, sems.at[slot, which])
            for which, (source, target) in enumerate(pairs)
        ]

    if add:
        fetch(0).start()
    for step in range(STEPS):
        slot = step % 2
        across = slice(step * width, (step + 1) * width)
        own_rows = pl.ds(pl.multiple_of(half * (model // 2) + step * height, 128), height)
        both, down = 0.0, 0.0
        for flipped, (rows_ref, cots_ref, pair_units_ref, _) in zip(flipped_hidden, saved):
            both = both + dot(rows_ref[:, own_rows].T, pair_units_ref[...])
            down = down + dot(flipped, cots_ref[:, across])
        if step >= 2:
            for copy in moves(step - 2):
                copy.wait()
        if add:
            fetch(step).wait()
            if step + 1 < STEPS:
                fetch(step + 1).start()
            gate_ref[slot] = both[:, :units] + other_ref[slot, :, :units].astype(F32)
            up_ref[slot] = both[:, units:] + other_ref[slot, :, units : 2 * units].astype(F32)
            down_ref[slot, :height, :] = down[:height] + other_ref[
                slot, :, 2 * units : 2 * units + width
            ].astype(F32)
            for which in range(fold):
                columns = slice(which * part, (which + 1) * part)
                lower = slice(which * rest, (which + 1) * rest)
                down_ref[slot, height:, columns] = down[height:, columns] + other_ref[
                    slot, lower, 2 * units + width :
                ].astype(F32)
        else:
            sent_ref[slot, :, : 2 * units] = both.astype(BF16)
            down = down.astype(BF16)
            sent_ref[slot, :, 2 * units : 2 * units + width] = down[:height]
            for which in range(fold):
                lower = slice(which * rest, (which + 1) * rest)
                sent_ref[slot, lower, 2 * units + width :] = down[
                    height:, which * part : (which + 1) * part
                ]
        for copy in moves(step):
            copy.start()
    for step in range(STEPS - 2, STEPS):
        for copy in moves(step):
            copy.wait()


def grads(ids, saved, received, after):
    model, units = saved[0][0].shape[1], saved[0][3].shape[1]
    height = model // 2 // STEPS
    sent_width = 3 * units
    add = bool(received)
    if add:
        shapes = [(model // 2, units), (model // 2, units), (units // 2, model)]
        stages = [(2, height, units), (2, height, units), (2, units // 2, model // STEPS)]
        dtype = F32
    else:
        shapes, stages, dtype = [(model // 2, sent_width)], [(2, height, sent_width)], BF16
    scratch = [pltpu.VMEM(shape, dtype) for shape in stages]
    if add:
        scratch.append(pltpu.VMEM((2, height, sent_width), BF16))
    scratch.append(pltpu.SemaphoreType.DMA((2, len(shapes))))
    if add:
        scratch.append(pltpu.SemaphoreType.DMA((2,)))
    return pl.pallas_call(
        functools.partial(grads_kernel, len(saved), add),
        in_specs=[SMEM] + [VMEM] * (4 * len(saved)) + [ANYWHERE] * (1 + add),
        out_specs=[HBM] * len(shapes) + [VMEM] * add,
        out_shape=[array(shape, dtype) for shape in shapes] + [array((8, 128), F32)] * add,
        scratch_shapes=scratch,
        compiler_params=LARGE,
        cost_estimate=LONG,
        name="grads",
    )(ids, *in_vmem(*(part for kept in saved for part in kept)), *received, after)


def expand_kernel(count, top, ids_ref, meta_ref, *refs):
    back, out = refs[:count], refs[-1]
    cap, model = back[0].shape
    onehot, _ = slot_masks(ids_ref, meta_ref[...], count, cap, top)
    spread = onehot.T.astype(BF16)
    step = min(512, model)
    for start in range(0, model, step):
        columns = slice(start, start + step)
        value = dot(spread, jnp.concatenate([ref[:, columns] for ref in back], axis=0))
        out[:, columns] = value.astype(out.dtype)


def expand(ids, packed, back, top, dtype, estimate, after):
    count = len(back)
    cap, model = back[0].shape
    tokens = (packed.shape[0] - META) // 2
    whole = lambda *shape: pl.BlockSpec(shape, lambda s: (0, 0))
    return pl.pallas_call(
        functools.partial(expand_kernel, count, top),
        grid=(1,),
        out_shape=array((tokens, model), dtype),
        in_specs=[SMEM, pl.BlockSpec((META, tokens), lambda s: (2 * tokens // META, 0))]
        + [whole(cap, model)] * count
        + [ANYWHERE],
        out_specs=whole(tokens, model),
        compiler_params=PARAMS,
        cost_estimate=estimate,
        name="expand",
    )(ids, packed, *back, after)


def total_kernel(count, own_ref, *refs):
    value = own_ref[...]
    for ref in refs[:count]:
        value = value + ref[...].astype(F32)
    refs[-1][...] = value.astype(refs[-1].dtype)


def total(own, others, dtype, after):
    return pl.pallas_call(
        functools.partial(total_kernel, len(others)),
        out_shape=array(own.shape, dtype),
        in_specs=[VMEM] * (1 + len(others)) + [ANYWHERE],
        out_specs=VMEM,
        compiler_params=PARAMS,
        cost_estimate=COST,
        name="total",
    )(own, *others, after)


def local(tokens, cotangent, experts, mixing, gate_matrix, up_matrix, down_matrix):
    expert_count = lax.axis_size("expert")
    inner = min(4, expert_count)
    outer = expert_count // inner
    tok_rows, top = experts.shape
    cap = 2 * tok_rows * top // expert_count
    weight_gate, weight_up, weight_down = gate_matrix[0], up_matrix[0], down_matrix[0]

    def swap(value, mask):
        pairs = [(device, device ^ mask) for device in range(expert_count)]
        return lax.ppermute(value, "expert", pairs)

    def swap_inner(values):
        return [values[0]] + [swap(values[which], which) for which in range(1, inner)]

    core = lax.axis_index("dp").astype(jnp.int32)
    plane_ids = jnp.bitwise_xor(lax.axis_index("expert").astype(jnp.int32), jnp.arange(inner, dtype=jnp.int32))
    ids = jnp.concatenate([plane_ids, jnp.stack([core, 1 - core])])
    order = list(range(2, outer)) + [1] if outer > 1 else []
    packed = {0: pack(tokens, cotangent, experts, mixing)}
    arrived, returned, partial, kept = {}, {}, [], {}
    saved = {}

    def fetch(plane):
        low = plane & -plane
        source = plane ^ low
        packed[plane] = swap(kept[source] if source else packed[0], low * inner)

    def send(plane, after):
        onward = [other for other in order if other ^ (other & -other) == plane and plane]
        sent = list(select(ids, packed[plane], cap, top, bool(onward), after))
        if onward:
            kept[plane] = sent.pop()
        arrived[plane] = swap_inner(sent)
        for other in onward:
            fetch(other)
        return sent[0]

    def work(plane, after):
        pair_cot, saved[plane] = expert(arrived[plane], weights, after)
        returned[plane] = swap_inner(pair_cot)
        return pair_cot[0]

    def give_back(plane, after, estimate=COST):
        value = expand(ids, packed[plane], returned[plane], top, BF16, estimate, after)
        partial.append(swap(value, plane * inner))
        return value

    for plane in order:
        if plane & (plane - 1) == 0:
            fetch(plane)
    last = send(0, [])
    weights = flip(weight_gate, weight_up, weight_down, last)
    last = work(0, [])
    own = expand(ids, packed[0], returned[0], top, F32, COST, last)
    last = own
    for plane in order[:2]:
        last = send(plane, [last, packed[order[-1]]])
    for which, plane in enumerate(order):
        if which + 1 == len(order) and which >= 1:
            last = give_back(order[which - 1], last)
        last = work(plane, [last])
        if 1 <= which and which + 1 < len(order):
            last = give_back(order[which - 1], last)
            last = send(order[which + 1], [last])
    kept = [saved[plane] for plane in [0] + order]
    (other_half,) = grads(ids, kept, [], last)
    received = lax.ppermute(other_half, "dp", [(0, 1), (1, 0)])
    last = other_half
    if order:
        last = give_back(order[-1], last, LONG)
    gate_grad, up_grad, down_grad, token = grads(ids, kept, [received], last)
    input_grad = total(own, partial, BF16, token)
    return (input_grad, gate_grad[None], up_grad[None], down_grad[None])


def solution(mesh):
    return jax.shard_map(
        local,
        mesh=mesh,
        in_specs=(
            P(("dp", "expert"), None),
            P(("dp", "expert"), None),
            P(("dp", "expert"), None),
            P(("dp", "expert"), None),
            P("expert", None, None),
            P("expert", None, None),
            P("expert", None, None),
        ),
        out_specs=(
            P(("dp", "expert"), None),
            P("expert", "dp", None),
            P("expert", "dp", None),
            P("expert", "dp", None),
        ),
        check_vma=False,
    )
```

```python
import functools

import jax
import jax.numpy as jnp
from jax import lax
from jax.experimental import pallas as pl
from jax.experimental.pallas import tpu as pltpu
from jax.sharding import PartitionSpec as P

BF16 = jnp.bfloat16
F32 = jnp.float32
META = 16
PARAMS = pltpu.CompilerParams(vmem_limit_bytes=8 << 20)
LARGE = pltpu.CompilerParams(vmem_limit_bytes=15 << 20)
COST = pl.CostEstimate(flops=1, transcendentals=0, bytes_accessed=1)
LONG = pl.CostEstimate(flops=1 << 37, transcendentals=0, bytes_accessed=1 << 27)
VMEM = pl.BlockSpec(memory_space=pltpu.VMEM)
SMEM = pl.BlockSpec(memory_space=pltpu.SMEM)
ANYWHERE = pl.BlockSpec(memory_space=pl.ANY)
HBM = pl.BlockSpec(memory_space=pltpu.HBM)


def dot(left, right, dims=((1,), (0,))):
    return lax.dot_general(left, right, (dims, ((), ())), preferred_element_type=F32)


def array(shape, dtype=BF16):
    return jax.ShapeDtypeStruct(shape, dtype)


def in_hbm(*values):
    return [pltpu.with_memory_space_constraint(value, pltpu.HBM) for value in values]


def in_vmem(*values):
    return [pltpu.with_memory_space_constraint(value, pltpu.VMEM) for value in values]


def resident(*shape, dtype=BF16):
    return pltpu.VMEM(shape, dtype)


def pack_kernel(in_ref, experts_ref, mixing_ref, out_ref, block_ref, sems):
    tokens, model = in_ref.shape
    rows = pltpu.make_async_copy(in_ref, out_ref.at[:tokens], sems.at[0])
    rows.start()
    mixing = mixing_ref[...]
    high = mixing.astype(BF16).astype(F32)
    middle = (mixing - high).astype(BF16).astype(F32)
    low = mixing - high - middle
    block = [experts_ref[...].astype(F32), high, middle, low]
    if META > 4 * mixing.shape[0]:
        block.append(jnp.zeros((META - 4 * mixing.shape[0], tokens), F32))
    block_ref[:, :tokens] = jnp.concatenate(block, axis=0).astype(BF16)
    block_ref[:, tokens:] = jnp.zeros((META, model - tokens), BF16)
    routing = pltpu.make_async_copy(block_ref, out_ref.at[tokens:], sems.at[1])
    routing.start()
    rows.wait()
    routing.wait()


def pack(tokens, experts, mixing):
    rows, model = tokens.shape
    return pl.pallas_call(
        pack_kernel,
        out_shape=array((rows + META, model)),
        in_specs=[HBM, VMEM, VMEM],
        out_specs=HBM,
        scratch_shapes=[pltpu.VMEM((META, model), BF16), pltpu.SemaphoreType.DMA((2,))],
        compiler_params=PARAMS,
        cost_estimate=COST,
        name="pack",
    )(*in_hbm(tokens), experts.T, mixing.T)


def slot_masks(ids_ref, block, count, cap, top):
    block = block.astype(F32)
    chosen, high, middle, low = (block[top * part : top * (part + 1)] for part in range(4))
    mixing = (high + middle) + low
    tokens = chosen.shape[1]
    earlier = lax.broadcasted_iota(jnp.int32, (tokens, tokens), 0)
    later = lax.broadcasted_iota(jnp.int32, (tokens, tokens), 1)
    before = (earlier < later).astype(F32)
    slot = lax.broadcasted_iota(jnp.int32, (cap, tokens), 0).astype(F32)
    named, weights = [], []
    for which in range(count):
        hit = chosen == ids_ref[which].astype(F32)
        named.append(jnp.sum(jnp.where(hit, 1.0, 0.0), axis=0, keepdims=True))
        weights.append(jnp.sum(jnp.where(hit, mixing, 0.0), axis=0, keepdims=True))
    position = dot(jnp.concatenate(named, axis=0), before)
    onehot, slot_weight = [], []
    for which in range(count):
        here = (slot == position[which : which + 1]) & (named[which] > 0.5)
        onehot.append(jnp.where(here, 1.0, 0.0))
        slot_weight.append(jnp.sum(jnp.where(here, weights[which], 0.0), axis=1, keepdims=True))
    return jnp.concatenate(onehot, axis=0), jnp.concatenate(slot_weight, axis=0)


def select_kernel(count, cap, top, parts, copied, ids_ref, *refs):
    packed_ref, cots_ref = refs[:2]
    sources = refs[2 : 2 + copied]
    targets, sems = refs[-1 - copied : -1], refs[-1]
    outs = refs[-1 - copied - count : -1 - copied]
    copies = [
        pltpu.make_async_copy(source, target, sems.at[which])
        for which, (source, target) in enumerate(zip(sources, targets))
    ]
    for copy in copies:
        copy.start()
    model = packed_ref.shape[1]
    tokens = packed_ref.shape[0] - META
    masks, weight = slot_masks(ids_ref, packed_ref[tokens:, :tokens], count, cap, top)
    onehot = masks.astype(BF16)
    step = min(512, model)
    for start in range(0, model, step):
        columns = slice(start, start + step)
        for place, part in enumerate(parts):
            if part == "rows":
                value = dot(onehot, packed_ref[:tokens, columns])
            else:
                value = dot(onehot, cots_ref[:, columns]) * weight
            value = value.astype(BF16)
            for which in range(count):
                outs[which][place, :, columns] = value[which * cap : (which + 1) * cap]
    for copy in copies:
        copy.wait()


def select(ids, packed, cots, cap, top, parts, copied, after):
    count = ids.shape[0] - 2
    model = packed.shape[1]
    result = pl.pallas_call(
        functools.partial(select_kernel, count, cap, top, parts, len(copied)),
        out_shape=[array((len(parts), cap, model))] * count
        + [array(value.shape) for value in copied],
        in_specs=[SMEM, VMEM, VMEM if "cots" in parts else ANYWHERE]
        + [ANYWHERE] * (len(copied) + len(after)),
        out_specs=[VMEM] * count + [HBM] * len(copied),
        scratch_shapes=[pltpu.SemaphoreType.DMA((max(1, len(copied)),))],
        compiler_params=PARAMS,
        cost_estimate=COST,
        name="select",
    )(ids, packed, cots, *copied, *after)
    return result[:count], result[count:]


def flip_kernel(gate_in, up_in, down_in, _, gate_ref, up_ref, both_ref, flipped_ref, down, sems):
    copies = [
        pltpu.make_async_copy(source, target, sems.at[which])
        for which, (source, target) in enumerate(
            ((gate_in, gate_ref), (up_in, up_ref), (down_in, down))
        )
    ]
    for copy in copies:
        copy.start()
    model, units = gate_ref.shape
    step = min(512, model)
    for which, source in enumerate((gate_ref, up_ref)):
        copies[which].wait()
        for start in range(0, model, step):
            both_ref[which * units : (which + 1) * units, start : start + step] = source[
                start : start + step, :
            ].T
    copies[2].wait()
    for start in range(0, model, step):
        flipped_ref[start : start + step, :] = down[:, start : start + step].T


def flip(weight_gate, weight_up, weight_down, after):
    model, units = weight_gate.shape
    return pl.pallas_call(
        flip_kernel,
        in_specs=[HBM] * 3 + [ANYWHERE],
        out_specs=[VMEM] * 4,
        out_shape=[
            resident(model, units),
            resident(model, units),
            resident(2 * units, model),
            resident(model, units),
        ],
        scratch_shapes=[pltpu.VMEM((units, model), BF16), pltpu.SemaphoreType.DMA((3,))],
        compiler_params=PARAMS,
        cost_estimate=COST,
        name="flip",
    )(*in_hbm(weight_gate, weight_up, weight_down), after)


def begin_kernel(count, *refs):
    ins = refs[:count]
    gate_ref, up_ref = refs[count : count + 2]
    rows_ref, pre_gate_ref, pre_up_ref = refs[-3:]
    cap = ins[0].shape[1]
    for which in range(count):
        rows_ref[which * cap : (which + 1) * cap, :] = ins[which][0]
    pre_gate_ref[...] = dot(rows_ref[...], gate_ref[...])
    pre_up_ref[...] = dot(rows_ref[...], up_ref[...])


def begin(arrived, weights, after):
    count = len(arrived)
    _, cap, model = arrived[0].shape
    units = weights[0].shape[1]
    rows = count * cap
    return pl.pallas_call(
        functools.partial(begin_kernel, count),
        in_specs=[VMEM] * (count + 2) + [ANYWHERE] * len(after),
        out_specs=[VMEM] * 3,
        out_shape=[resident(rows, model)] + [resident(rows, units, dtype=F32)] * 2,
        compiler_params=PARAMS,
        cost_estimate=COST,
        name="begin",
    )(*arrived, *in_vmem(*weights[:2]), *after)


def expert_kernel(count, begun, *refs):
    ins = refs[:count]
    gate_ref, up_ref, both_ref, flipped_ref = refs[count : count + 4]
    cap = ins[0].shape[1]
    model, units = gate_ref.shape
    if begun:
        pre_gate_ref, pre_up_ref = refs[count + 4 : count + 6]
        outs, (cots_ref, pair_units_ref, hidden_ref) = refs[-count - 3 : -3], refs[-3:]
    else:
        outs = refs[-count - 4 : -4]
        rows_ref, cots_ref, pair_units_ref, hidden_ref = refs[-4:]
    for which in range(count):
        part = slice(which * cap, (which + 1) * cap)
        if not begun:
            rows_ref[part, :] = ins[which][0]
        cots_ref[part, :] = ins[which][0 if begun else 1]
    block = min(256, units)
    for start in range(0, units, block):
        columns = slice(start, start + block)
        if begun:
            pre_gate, pre_up = pre_gate_ref[:, columns], pre_up_ref[:, columns]
        else:
            pre_gate = dot(rows_ref[...], gate_ref[:, columns])
            pre_up = dot(rows_ref[...], up_ref[:, columns])
        hidden_cot = dot(cots_ref[...], flipped_ref[:, columns])
        sigmoid_gate = jax.nn.sigmoid(pre_gate)
        activated = pre_gate * sigmoid_gate
        hidden_ref[:, columns] = (activated * pre_up).astype(BF16)
        pair_units_ref[:, columns] = (
            hidden_cot * pre_up * sigmoid_gate * (1.0 + pre_gate * (1.0 - sigmoid_gate))
        ).astype(BF16)
        pair_units_ref[:, units + start : units + start + block] = (
            hidden_cot * activated
        ).astype(BF16)
    block = min(512, model)
    for start in range(0, model, block):
        columns = slice(start, start + block)
        pair_cot = dot(pair_units_ref[...], both_ref[:, columns]).astype(BF16)
        for which in range(count):
            outs[which][:, columns] = pair_cot[which * cap : (which + 1) * cap]


def expert(arrived, weights, begun, after):
    count = len(arrived)
    _, cap, model = arrived[0].shape
    units = weights[0].shape[1]
    rows = count * cap
    kept = [resident(rows, model)] * (1 if begun else 2)
    kept += [resident(rows, 2 * units), resident(rows, units)]
    result = pl.pallas_call(
        functools.partial(expert_kernel, count, bool(begun)),
        in_specs=[VMEM] * (count + 4 + len(begun[1:])) + [ANYWHERE] * len(after),
        out_specs=[VMEM] * (count + len(kept)),
        out_shape=[array((cap, model))] * count + kept,
        compiler_params=PARAMS,
        cost_estimate=COST,
        name="expert",
    )(*arrived, *in_vmem(*weights, *begun[1:]), *after)
    return result[:count], list(begun[:1]) + list(result[count:])


STEPS = 4


def grads_kernel(planes, add, ids_ref, *refs):
    saved = [refs[4 * which : 4 * which + 4] for which in range(planes)]
    refs = refs[4 * planes :]
    model, units = saved[0][0].shape[1], saved[0][3].shape[1]
    half = ids_ref[ids_ref.shape[0] - (2 if add else 1)]
    height, width = model // 2 // STEPS, model // STEPS
    rest = units // 2 - height
    fold = height // rest
    part = width // fold
    if add:
        other_in, _, gate_out, up_out, down_out, token, gate_ref, up_ref, down_ref, other_ref, sems, other_sems = refs
        token[...] = jnp.zeros(token.shape, F32)
    else:
        _, sent_out, sent_ref, sems = refs
    own_units = pl.ds(pl.multiple_of(half * (units // 2), 128), units // 2)
    flipped_hidden = [kept[3][:, own_units].T for kept in saved]

    def fetch(step):
        at = slice(step * height, (step + 1) * height)
        slot = step % 2
        return pltpu.make_async_copy(other_in.at[at], other_ref.at[slot], other_sems.at[slot])

    def moves(step):
        at = slice(step * height, (step + 1) * height)
        across = slice(step * width, (step + 1) * width)
        slot = step % 2
        if add:
            pairs = (
                (gate_ref.at[slot], gate_out.at[at]),
                (up_ref.at[slot], up_out.at[at]),
                (down_ref.at[slot], down_out.at[:, across]),
            )
        else:
            pairs = ((sent_ref.at[slot], sent_out.at[at]),)
        return [
            pltpu.make_async_copy(source, target, sems.at[slot, which])
            for which, (source, target) in enumerate(pairs)
        ]

    if add:
        fetch(0).start()
    for step in range(STEPS):
        slot = step % 2
        across = slice(step * width, (step + 1) * width)
        own_rows = pl.ds(pl.multiple_of(half * (model // 2) + step * height, 128), height)
        both, down = 0.0, 0.0
        for flipped, (rows_ref, cots_ref, pair_units_ref, _) in zip(flipped_hidden, saved):
            both = both + dot(rows_ref[:, own_rows].T, pair_units_ref[...])
            down = down + dot(flipped, cots_ref[:, across])
        if step >= 2:
            for copy in moves(step - 2):
                copy.wait()
        if add:
            fetch(step).wait()
            if step + 1 < STEPS:
                fetch(step + 1).start()
            gate_ref[slot] = both[:, :units] + other_ref[slot, :, :units].astype(F32)
            up_ref[slot] = both[:, units:] + other_ref[slot, :, units : 2 * units].astype(F32)
            down_ref[slot, :height, :] = down[:height] + other_ref[
                slot, :, 2 * units : 2 * units + width
            ].astype(F32)
            for which in range(fold):
                columns = slice(which * part, (which + 1) * part)
                lower = slice(which * rest, (which + 1) * rest)
                down_ref[slot, height:, columns] = down[height:, columns] + other_ref[
                    slot, lower, 2 * units + width :
                ].astype(F32)
        else:
            sent_ref[slot, :, : 2 * units] = both.astype(BF16)
            down = down.astype(BF16)
            sent_ref[slot, :, 2 * units : 2 * units + width] = down[:height]
            for which in range(fold):
                lower = slice(which * rest, (which + 1) * rest)
                sent_ref[slot, lower, 2 * units + width :] = down[
                    height:, which * part : (which + 1) * part
                ]
        for copy in moves(step):
            copy.start()
    for step in range(STEPS - 2, STEPS):
        for copy in moves(step):
            copy.wait()


def grads(ids, saved, received, after):
    model, units = saved[0][0].shape[1], saved[0][3].shape[1]
    height = model // 2 // STEPS
    sent_width = 3 * units
    add = bool(received)
    if add:
        shapes = [(model // 2, units), (model // 2, units), (units // 2, model)]
        stages = [(2, height, units), (2, height, units), (2, units // 2, model // STEPS)]
        dtype = F32
    else:
        shapes, stages, dtype = [(model // 2, sent_width)], [(2, height, sent_width)], BF16
    scratch = [pltpu.VMEM(shape, dtype) for shape in stages]
    if add:
        scratch.append(pltpu.VMEM((2, height, sent_width), BF16))
    scratch.append(pltpu.SemaphoreType.DMA((2, len(shapes))))
    if add:
        scratch.append(pltpu.SemaphoreType.DMA((2,)))
    return pl.pallas_call(
        functools.partial(grads_kernel, len(saved), add),
        in_specs=[SMEM] + [VMEM] * (4 * len(saved)) + [ANYWHERE] * (1 + add),
        out_specs=[HBM] * len(shapes) + [VMEM] * add,
        out_shape=[array(shape, dtype) for shape in shapes] + [array((8, 128), F32)] * add,
        scratch_shapes=scratch,
        compiler_params=LARGE,
        cost_estimate=LONG,
        name="grads",
    )(ids, *in_vmem(*(part for kept in saved for part in kept)), *received, after)


def expand_kernel(count, top, ids_ref, meta_ref, *refs):
    back, out = refs[:count], refs[-1]
    cap, model = back[0].shape
    onehot, _ = slot_masks(ids_ref, meta_ref[...], count, cap, top)
    spread = onehot.T.astype(BF16)
    step = min(512, model)
    for start in range(0, model, step):
        columns = slice(start, start + step)
        value = dot(spread, jnp.concatenate([ref[:, columns] for ref in back], axis=0))
        out[:, columns] = value.astype(out.dtype)


def expand(ids, packed, back, top, dtype, estimate, after):
    count = len(back)
    cap, model = back[0].shape
    tokens = packed.shape[0] - META
    whole = lambda *shape: pl.BlockSpec(shape, lambda s: (0, 0))
    return pl.pallas_call(
        functools.partial(expand_kernel, count, top),
        grid=(1,),
        out_shape=array((tokens, model), dtype),
        in_specs=[SMEM, pl.BlockSpec((META, tokens), lambda s: (tokens // META, 0))]
        + [whole(cap, model)] * count
        + [ANYWHERE],
        out_specs=whole(tokens, model),
        compiler_params=PARAMS,
        cost_estimate=estimate,
        name="expand",
    )(ids, packed, *back, after)


def total_kernel(count, own_ref, *refs):
    value = own_ref[...]
    for ref in refs[:count]:
        value = value + ref[...].astype(F32)
    refs[-1][...] = value.astype(refs[-1].dtype)


def total(own, others, dtype, after):
    return pl.pallas_call(
        functools.partial(total_kernel, len(others)),
        out_shape=array(own.shape, dtype),
        in_specs=[VMEM] * (1 + len(others)) + [ANYWHERE],
        out_specs=VMEM,
        compiler_params=PARAMS,
        cost_estimate=COST,
        name="total",
    )(own, *others, after)


def local(tokens, cotangent, experts, mixing, gate_matrix, up_matrix, down_matrix):
    expert_count = lax.axis_size("expert")
    inner = min(4, expert_count)
    outer = expert_count // inner
    tok_rows, top = experts.shape
    cap = 2 * tok_rows * top // expert_count
    weight_gate, weight_up, weight_down = gate_matrix[0], up_matrix[0], down_matrix[0]

    def swap(value, mask):
        pairs = [(device, device ^ mask) for device in range(expert_count)]
        return lax.ppermute(value, "expert", pairs)

    def swap_inner(values):
        return [values[0]] + [swap(values[which], which) for which in range(1, inner)]

    core = lax.axis_index("dp").astype(jnp.int32)
    plane_ids = jnp.bitwise_xor(lax.axis_index("expert").astype(jnp.int32), jnp.arange(inner, dtype=jnp.int32))
    ids = jnp.concatenate([plane_ids, jnp.stack([core, 1 - core])])
    order = list(range(2, outer)) + [1]
    packed = {0: pack(tokens, experts, mixing)}
    cots = {0: cotangent}
    arrived, returned, partial = {}, {}, []
    saved = {}

    def low_bit(plane):
        return plane & -plane

    def send(plane, parts, copied, after):
        sent, copies = select(ids, packed[plane], cots[plane], cap, top, parts, copied, after)
        arrived[plane] = swap_inner(sent)
        return sent[0], copies

    def onward(plane):
        return [other for other in order if other ^ low_bit(other) == plane]

    def forward(plane, kept, held):
        for other in onward(plane):
            held[other] = swap(kept, low_bit(other) * inner)

    def work(plane, begun, after):
        pair_cot, saved[plane] = expert(arrived[plane], weights, begun, after)
        returned[plane] = swap_inner(pair_cot)
        return pair_cot[0]

    def give_back(plane, after, estimate=COST):
        value = expand(ids, packed[plane], returned[plane], top, BF16, estimate, after)
        partial.append(swap(value, plane * inner))
        return value

    both = ("rows", "cots")
    first, final = order[0], order[-1]
    packed[first] = swap(packed[0], first * inner)
    last, _ = send(0, both, [], [])
    weights = flip(weight_gate, weight_up, weight_down, last)
    cots[first] = cotangent
    last, copies = send(first, both[:1], [packed[first], cotangent], [weights[3]])
    cots[first] = swap(copies[1], first * inner)
    forward(first, copies[0], packed)
    for plane in order[1:-1]:
        if plane == low_bit(plane):
            packed[plane] = swap(packed[0], plane * inner)
            cots[plane] = swap(cotangent, plane * inner)
    pieces = arrived[first]
    last = work(0, [], [last])
    begun = begin(pieces, weights, [last])
    last, copies = send(first, both[1:], [cots[first]], [begun[1]])
    forward(first, copies[0], cots)
    for which, plane in enumerate(order[1:-1]):
        copied = [packed[plane], cots[plane]] if onward(plane) else []
        if which == 0:
            copied += [packed[0], cotangent]
        last, copies = send(plane, both, copied, [last])
        if onward(plane):
            forward(plane, copies[0], packed)
            forward(plane, copies[1], cots)
        if which == 0:
            packed[final] = swap(copies[-2], final * inner)
            cots[final] = swap(copies[-1], final * inner)
        if which == 0:
            last = work(first, begun, [last])
            own = expand(ids, packed[0], returned[0], top, F32, COST, last)
            last = own
        last = work(plane, [], [last])
        last = give_back(order[which], last)
    last, _ = send(final, both, [], [last])
    last = give_back(order[-2], last)
    own = total(own, partial[:-1], F32, last)
    del partial[:-1]
    last = work(final, [], [own])
    kept = [saved[plane] for plane in [0] + order]
    (other_half,) = grads(ids, kept, [], last)
    received = lax.ppermute(other_half, "dp", [(0, 1), (1, 0)])
    last = other_half
    last = give_back(final, last, LONG)
    gate_grad, up_grad, down_grad, token = grads(ids, kept, [received], last)
    input_grad = total(own, partial, BF16, token)
    return (input_grad, gate_grad[None], up_grad[None], down_grad[None])


def solution(mesh):
    return jax.shard_map(
        local,
        mesh=mesh,
        in_specs=(
            P(("dp", "expert"), None),
            P(("dp", "expert"), None),
            P(("dp", "expert"), None),
            P(("dp", "expert"), None),
            P("expert", None, None),
            P("expert", None, None),
            P("expert", None, None),
        ),
        out_specs=(
            P(("dp", "expert"), None),
            P("expert", "dp", None),
            P("expert", "dp", None),
            P("expert", "dp", None),
        ),
        check_vma=False,
    )
```

```python
import functools

import jax
import jax.numpy as jnp
from jax import lax
from jax.experimental import pallas as pl
from jax.experimental.pallas import tpu as pltpu
from jax.sharding import PartitionSpec as P

BF16 = jnp.bfloat16
F32 = jnp.float32
META = 16
PARAMS = pltpu.CompilerParams(vmem_limit_bytes=8 << 20)
LARGE = pltpu.CompilerParams(vmem_limit_bytes=15 << 20)
VMEM = pl.BlockSpec(memory_space=pltpu.VMEM)
SMEM = pl.BlockSpec(memory_space=pltpu.SMEM)
ANYWHERE = pl.BlockSpec(memory_space=pl.ANY)
HBM = pl.BlockSpec(memory_space=pltpu.HBM)


def estimate(flops):
    return pl.CostEstimate(flops=flops, transcendentals=0, bytes_accessed=1)


def dot(left, right, dims=((1,), (0,))):
    return lax.dot_general(left, right, (dims, ((), ())), preferred_element_type=F32)


def array(shape, dtype=BF16):
    return jax.ShapeDtypeStruct(shape, dtype)


def in_hbm(*values):
    return [pltpu.with_memory_space_constraint(value, pltpu.HBM) for value in values]


def in_vmem(*values):
    return [pltpu.with_memory_space_constraint(value, pltpu.VMEM) for value in values]


def resident(*shape, dtype=BF16):
    return pltpu.VMEM(shape, dtype)


def pack_kernel(in_ref, experts_ref, mixing_ref, out_ref, block_ref, sems):
    tokens, model = in_ref.shape
    rows = pltpu.make_async_copy(in_ref, out_ref.at[:tokens], sems.at[0])
    rows.start()
    mixing = mixing_ref[...]
    high = mixing.astype(BF16).astype(F32)
    middle = (mixing - high).astype(BF16).astype(F32)
    low = mixing - high - middle
    block = [experts_ref[...].astype(F32), high, middle, low]
    if META > 4 * mixing.shape[0]:
        block.append(jnp.zeros((META - 4 * mixing.shape[0], tokens), F32))
    block_ref[:, :tokens] = jnp.concatenate(block, axis=0).astype(BF16)
    block_ref[:, tokens:] = jnp.zeros((META, model - tokens), BF16)
    routing = pltpu.make_async_copy(block_ref, out_ref.at[tokens:], sems.at[1])
    routing.start()
    rows.wait()
    routing.wait()


def pack(tokens, experts, mixing, flops=1):
    rows, model = tokens.shape
    return pl.pallas_call(
        pack_kernel,
        out_shape=array((rows + META, model)),
        in_specs=[HBM, VMEM, VMEM],
        out_specs=HBM,
        scratch_shapes=[pltpu.VMEM((META, model), BF16), pltpu.SemaphoreType.DMA((2,))],
        compiler_params=PARAMS,
        cost_estimate=estimate(flops),
        name="pack",
    )(*in_hbm(tokens), experts.T, mixing.T)


def slot_masks(ids_ref, block, count, cap, top):
    block = block.astype(F32)
    chosen, high, middle, low = (block[top * part : top * (part + 1)] for part in range(4))
    mixing = (high + middle) + low
    tokens = chosen.shape[1]
    earlier = lax.broadcasted_iota(jnp.int32, (tokens, tokens), 0)
    later = lax.broadcasted_iota(jnp.int32, (tokens, tokens), 1)
    before = (earlier < later).astype(F32)
    slot = lax.broadcasted_iota(jnp.int32, (cap, tokens), 0).astype(F32)
    named, weights = [], []
    for which in range(count):
        hit = chosen == ids_ref[which].astype(F32)
        named.append(jnp.sum(jnp.where(hit, 1.0, 0.0), axis=0, keepdims=True))
        weights.append(jnp.sum(jnp.where(hit, mixing, 0.0), axis=0, keepdims=True))
    position = dot(jnp.concatenate(named, axis=0), before)
    onehot, slot_weight = [], []
    for which in range(count):
        here = (slot == position[which : which + 1]) & (named[which] > 0.5)
        onehot.append(jnp.where(here, 1.0, 0.0))
        slot_weight.append(jnp.sum(jnp.where(here, weights[which], 0.0), axis=1, keepdims=True))
    return jnp.concatenate(onehot, axis=0), jnp.concatenate(slot_weight, axis=0)


def select_kernel(count, cap, top, parts, copied, ids_ref, *refs):
    packed_ref, cots_ref = refs[:2]
    sources = refs[2 : 2 + copied]
    targets, sems = refs[-1 - copied : -1], refs[-1]
    outs = refs[-1 - copied - count : -1 - copied]
    copies = [
        pltpu.make_async_copy(source, target, sems.at[which])
        for which, (source, target) in enumerate(zip(sources, targets))
    ]
    for copy in copies:
        copy.start()
    model = packed_ref.shape[1]
    tokens = packed_ref.shape[0] - META
    masks, weight = slot_masks(ids_ref, packed_ref[tokens:, :tokens], count, cap, top)
    onehot = masks.astype(BF16)
    step = min(512, model)
    for start in range(0, model, step):
        columns = slice(start, start + step)
        for place, part in enumerate(parts):
            if part == "rows":
                value = dot(onehot, packed_ref[:tokens, columns])
            else:
                value = dot(onehot, cots_ref[:, columns]) * weight
            value = value.astype(BF16)
            for which in range(count):
                outs[which][place, :, columns] = value[which * cap : (which + 1) * cap]
    for copy in copies:
        copy.wait()


def select(ids, packed, cots, cap, top, parts, copied, flops, after):
    count = ids.shape[0] - 2
    model = packed.shape[1]
    result = pl.pallas_call(
        functools.partial(select_kernel, count, cap, top, parts, len(copied)),
        out_shape=[array((len(parts), cap, model))] * count
        + [array(value.shape) for value in copied],
        in_specs=[SMEM, VMEM, VMEM if "cots" in parts else ANYWHERE]
        + [ANYWHERE] * (len(copied) + len(after)),
        out_specs=[VMEM] * count + [HBM] * len(copied),
        scratch_shapes=[pltpu.SemaphoreType.DMA((max(1, len(copied)),))],
        compiler_params=PARAMS,
        cost_estimate=estimate(flops),
        name="select",
    )(ids, packed, cots, *copied, *after)
    return result[:count], result[count:]


def flip_kernel(gate_in, up_in, down_in, _, gate_ref, up_ref, both_ref, flipped_ref, down, sems):
    copies = [
        pltpu.make_async_copy(source, target, sems.at[which])
        for which, (source, target) in enumerate(
            ((gate_in, gate_ref), (up_in, up_ref), (down_in, down))
        )
    ]
    for copy in copies:
        copy.start()
    model, units = gate_ref.shape
    step = min(512, model)
    for which, source in enumerate((gate_ref, up_ref)):
        copies[which].wait()
        for start in range(0, model, step):
            both_ref[which * units : (which + 1) * units, start : start + step] = source[
                start : start + step, :
            ].T
    copies[2].wait()
    for start in range(0, model, step):
        flipped_ref[start : start + step, :] = down[:, start : start + step].T


def flip(weight_gate, weight_up, weight_down, flops, after):
    model, units = weight_gate.shape
    return pl.pallas_call(
        flip_kernel,
        in_specs=[HBM] * 3 + [ANYWHERE],
        out_specs=[VMEM] * 4,
        out_shape=[
            resident(model, units),
            resident(model, units),
            resident(2 * units, model),
            resident(model, units),
        ],
        scratch_shapes=[pltpu.VMEM((units, model), BF16), pltpu.SemaphoreType.DMA((3,))],
        compiler_params=PARAMS,
        cost_estimate=estimate(flops),
        name="flip",
    )(*in_hbm(weight_gate, weight_up, weight_down), after)


def begin_kernel(count, *refs):
    ins = refs[:count]
    gate_ref, up_ref = refs[count : count + 2]
    rows_ref, pre_gate_ref, pre_up_ref = refs[-3:]
    cap = ins[0].shape[1]
    for which in range(count):
        rows_ref[which * cap : (which + 1) * cap, :] = ins[which][0]
    pre_gate_ref[...] = dot(rows_ref[...], gate_ref[...])
    pre_up_ref[...] = dot(rows_ref[...], up_ref[...])


def begin(arrived, weights, flops, after):
    count = len(arrived)
    _, cap, model = arrived[0].shape
    units = weights[0].shape[1]
    rows = count * cap
    return pl.pallas_call(
        functools.partial(begin_kernel, count),
        in_specs=[VMEM] * (count + 2) + [ANYWHERE] * len(after),
        out_specs=[VMEM] * 3,
        out_shape=[resident(rows, model)] + [resident(rows, units, dtype=F32)] * 2,
        compiler_params=PARAMS,
        cost_estimate=estimate(flops),
        name="begin",
    )(*arrived, *in_vmem(*weights[:2]), *after)


def expert_kernel(count, begun, *refs):
    ins = refs[:count]
    gate_ref, up_ref, both_ref, flipped_ref = refs[count : count + 4]
    cap = ins[0].shape[1]
    model, units = gate_ref.shape
    if begun:
        pre_gate_ref, pre_up_ref = refs[count + 4 : count + 6]
        outs, (cots_ref, pair_units_ref, hidden_ref) = refs[-count - 3 : -3], refs[-3:]
    else:
        outs = refs[-count - 4 : -4]
        rows_ref, cots_ref, pair_units_ref, hidden_ref = refs[-4:]
    for which in range(count):
        part = slice(which * cap, (which + 1) * cap)
        if not begun:
            rows_ref[part, :] = ins[which][0]
        cots_ref[part, :] = ins[which][0 if begun else 1]
    block = min(256, units)
    for start in range(0, units, block):
        columns = slice(start, start + block)
        if begun:
            pre_gate, pre_up = pre_gate_ref[:, columns], pre_up_ref[:, columns]
        else:
            pre_gate = dot(rows_ref[...], gate_ref[:, columns])
            pre_up = dot(rows_ref[...], up_ref[:, columns])
        hidden_cot = dot(cots_ref[...], flipped_ref[:, columns])
        sigmoid_gate = jax.nn.sigmoid(pre_gate)
        activated = pre_gate * sigmoid_gate
        hidden_ref[:, columns] = (activated * pre_up).astype(BF16)
        pair_units_ref[:, columns] = (
            hidden_cot * pre_up * sigmoid_gate * (1.0 + pre_gate * (1.0 - sigmoid_gate))
        ).astype(BF16)
        pair_units_ref[:, units + start : units + start + block] = (
            hidden_cot * activated
        ).astype(BF16)
    block = min(512, model)
    for start in range(0, model, block):
        columns = slice(start, start + block)
        pair_cot = dot(pair_units_ref[...], both_ref[:, columns]).astype(BF16)
        for which in range(count):
            outs[which][:, columns] = pair_cot[which * cap : (which + 1) * cap]


def expert(arrived, weights, begun, flops, after):
    count = len(arrived)
    _, cap, model = arrived[0].shape
    units = weights[0].shape[1]
    rows = count * cap
    kept = [resident(rows, model)] * (1 if begun else 2)
    kept += [resident(rows, 2 * units), resident(rows, units)]
    result = pl.pallas_call(
        functools.partial(expert_kernel, count, bool(begun)),
        in_specs=[VMEM] * (count + 4 + len(begun[1:])) + [ANYWHERE] * len(after),
        out_specs=[VMEM] * (count + len(kept)),
        out_shape=[array((cap, model))] * count + kept,
        compiler_params=PARAMS,
        cost_estimate=estimate(flops),
        name="expert",
    )(*arrived, *in_vmem(*weights, *begun[1:]), *after)
    return result[:count], list(begun[:1]) + list(result[count:])


STEPS = 4


def grads_kernel(planes, add, ids_ref, *refs):
    saved = [refs[4 * which : 4 * which + 4] for which in range(planes)]
    refs = refs[4 * planes :]
    model, units = saved[0][0].shape[1], saved[0][3].shape[1]
    half = ids_ref[ids_ref.shape[0] - (2 if add else 1)]
    height, width = model // 2 // STEPS, model // STEPS
    rest = units // 2 - height
    fold = height // rest
    part = width // fold
    if add:
        other_in, _, gate_out, up_out, down_out, token, gate_ref, up_ref, down_ref, other_ref, sems, other_sems = refs
        token[...] = jnp.zeros(token.shape, F32)
    else:
        _, sent_out, sent_ref, sems = refs
    own_units = pl.ds(pl.multiple_of(half * (units // 2), 128), units // 2)
    flipped_hidden = [kept[3][:, own_units].T for kept in saved]

    def fetch(step):
        at = slice(step * height, (step + 1) * height)
        slot = step % 2
        return pltpu.make_async_copy(other_in.at[at], other_ref.at[slot], other_sems.at[slot])

    def moves(step):
        at = slice(step * height, (step + 1) * height)
        across = slice(step * width, (step + 1) * width)
        slot = step % 2
        if add:
            pairs = (
                (gate_ref.at[slot], gate_out.at[at]),
                (up_ref.at[slot], up_out.at[at]),
                (down_ref.at[slot], down_out.at[:, across]),
            )
        else:
            pairs = ((sent_ref.at[slot], sent_out.at[at]),)
        return [
            pltpu.make_async_copy(source, target, sems.at[slot, which])
            for which, (source, target) in enumerate(pairs)
        ]

    if add:
        fetch(0).start()
    for step in range(STEPS):
        slot = step % 2
        across = slice(step * width, (step + 1) * width)
        own_rows = pl.ds(pl.multiple_of(half * (model // 2) + step * height, 128), height)
        both, down = 0.0, 0.0
        for flipped, (rows_ref, cots_ref, pair_units_ref, _) in zip(flipped_hidden, saved):
            both = both + dot(rows_ref[:, own_rows].T, pair_units_ref[...])
            down = down + dot(flipped, cots_ref[:, across])
        if step >= 2:
            for copy in moves(step - 2):
                copy.wait()
        if add:
            fetch(step).wait()
            if step + 1 < STEPS:
                fetch(step + 1).start()
            gate_ref[slot] = both[:, :units] + other_ref[slot, :, :units].astype(F32)
            up_ref[slot] = both[:, units:] + other_ref[slot, :, units : 2 * units].astype(F32)
            down_ref[slot, :height, :] = down[:height] + other_ref[
                slot, :, 2 * units : 2 * units + width
            ].astype(F32)
            for which in range(fold):
                columns = slice(which * part, (which + 1) * part)
                lower = slice(which * rest, (which + 1) * rest)
                down_ref[slot, height:, columns] = down[height:, columns] + other_ref[
                    slot, lower, 2 * units + width :
                ].astype(F32)
        else:
            sent_ref[slot, :, : 2 * units] = both.astype(BF16)
            down = down.astype(BF16)
            sent_ref[slot, :, 2 * units : 2 * units + width] = down[:height]
            for which in range(fold):
                lower = slice(which * rest, (which + 1) * rest)
                sent_ref[slot, lower, 2 * units + width :] = down[
                    height:, which * part : (which + 1) * part
                ]
        for copy in moves(step):
            copy.start()
    for step in range(STEPS - 2, STEPS):
        for copy in moves(step):
            copy.wait()


def grads(ids, saved, received, flops, after):
    model, units = saved[0][0].shape[1], saved[0][3].shape[1]
    height = model // 2 // STEPS
    sent_width = 3 * units
    add = bool(received)
    if add:
        shapes = [(model // 2, units), (model // 2, units), (units // 2, model)]
        stages = [(2, height, units), (2, height, units), (2, units // 2, model // STEPS)]
        dtype = F32
    else:
        shapes, stages, dtype = [(model // 2, sent_width)], [(2, height, sent_width)], BF16
    scratch = [pltpu.VMEM(shape, dtype) for shape in stages]
    if add:
        scratch.append(pltpu.VMEM((2, height, sent_width), BF16))
    scratch.append(pltpu.SemaphoreType.DMA((2, len(shapes))))
    if add:
        scratch.append(pltpu.SemaphoreType.DMA((2,)))
    return pl.pallas_call(
        functools.partial(grads_kernel, len(saved), add),
        in_specs=[SMEM] + [VMEM] * (4 * len(saved)) + [ANYWHERE] * (1 + add),
        out_specs=[HBM] * len(shapes) + [VMEM] * add,
        out_shape=[array(shape, dtype) for shape in shapes] + [array((8, 128), F32)] * add,
        scratch_shapes=scratch,
        compiler_params=LARGE,
        cost_estimate=estimate(flops),
        name="grads",
    )(ids, *in_vmem(*(part for kept in saved for part in kept)), *received, after)


def expand_kernel(count, top, ids_ref, meta_ref, *refs):
    back, out = refs[:count], refs[-1]
    cap, model = back[0].shape
    onehot, _ = slot_masks(ids_ref, meta_ref[...], count, cap, top)
    spread = onehot.T.astype(BF16)
    step = min(512, model)
    for start in range(0, model, step):
        columns = slice(start, start + step)
        value = dot(spread, jnp.concatenate([ref[:, columns] for ref in back], axis=0))
        out[:, columns] = value.astype(out.dtype)


def expand(ids, packed, back, top, dtype, flops, after):
    count = len(back)
    cap, model = back[0].shape
    tokens = packed.shape[0] - META
    whole = lambda *shape: pl.BlockSpec(shape, lambda s: (0, 0))
    return pl.pallas_call(
        functools.partial(expand_kernel, count, top),
        grid=(1,),
        out_shape=array((tokens, model), dtype),
        in_specs=[SMEM, pl.BlockSpec((META, tokens), lambda s: (tokens // META, 0))]
        + [whole(cap, model)] * count
        + [ANYWHERE],
        out_specs=whole(tokens, model),
        compiler_params=PARAMS,
        cost_estimate=estimate(flops),
        name="expand",
    )(ids, packed, *back, after)


def total_kernel(count, own_ref, *refs):
    value = own_ref[...]
    for ref in refs[:count]:
        value = value + ref[...].astype(F32)
    refs[-1][...] = value.astype(refs[-1].dtype)


def total(own, others, dtype, flops, after):
    return pl.pallas_call(
        functools.partial(total_kernel, len(others)),
        out_shape=array(own.shape, dtype),
        in_specs=[VMEM] * (1 + len(others)) + [ANYWHERE],
        out_specs=VMEM,
        compiler_params=PARAMS,
        cost_estimate=estimate(flops),
        name="total",
    )(own, *others, after)


FOUR_PLANES = (
    ("both", 0, 0),
    ("flip", 0, 0),
    ("rows", 2, 0),
    ("expert", 0, 0),
    ("begin", 2, 34),
    ("own", 0, 0),
    ("cots", 2, 0),
    ("both", 3, 0),
    ("expert", 2, 29),
    ("expert", 3, 0),
    ("both", 1, 0),
    ("expand", 2, 0),
    ("expand", 3, 0),
    ("total", 1, 0),
    ("expert", 1, 0),
    ("lend", 0, 37),
    ("expand", 1, 37),
    ("finish", 0, 37),
)
LATE = ()


def many_planes(outer):
    order = list(range(2, outer)) + [1]
    chain = [("both", 0, 0), ("flip", 0, 0), ("expert", 0, 0), ("own", 0, 0)]
    for plane in order:
        chain += [("both", plane, 0), ("expert", plane, 0)]
        chain += [("expand", plane, 0)]
    return chain + [("lend", 0, 0), ("finish", 0, 0)]


def local(tokens, cotangent, experts, mixing, gate_matrix, up_matrix, down_matrix):
    expert_count = lax.axis_size("expert")
    inner = min(4, expert_count)
    outer = expert_count // inner
    tok_rows, top = experts.shape
    cap = 2 * tok_rows * top // expert_count
    weight_gate, weight_up, weight_down = gate_matrix[0], up_matrix[0], down_matrix[0]

    def swap(value, mask):
        pairs = [(device, device ^ mask) for device in range(expert_count)]
        return lax.ppermute(value, "expert", pairs)

    def swap_inner(values):
        return [values[0]] + [swap(values[which], which) for which in range(1, inner)]

    core = lax.axis_index("dp").astype(jnp.int32)
    plane_ids = jnp.bitwise_xor(lax.axis_index("expert").astype(jnp.int32), jnp.arange(inner, dtype=jnp.int32))
    ids = jnp.concatenate([plane_ids, jnp.stack([core, 1 - core])])
    chain = FOUR_PLANES if outer == 4 else many_planes(outer)
    planes = [plane for kind, plane, _ in chain if kind == "expert"]
    packed = {0: pack(tokens, experts, mixing)}
    cots = {0: cotangent}
    arrived, returned, partial, saved, begun = {}, {}, [], {}, {}
    late = LATE if outer == 4 else ()
    late_planes = [plane for plane, _, _ in late]
    split = [plane for kind, plane, _ in chain if kind == "rows"]
    for plane in planes[1:]:
        if plane == plane & -plane and plane not in late_planes:
            packed[plane] = swap(packed[0], plane * inner)
            if plane not in split:
                cots[plane] = swap(cotangent, plane * inner)

    def send(kind, plane, flops, last):
        parts = ("rows", "cots") if kind == "both" else (kind,)
        onward = [other for other in planes if other ^ (other & -other) == plane and plane]
        copied = []
        if onward and "rows" in parts:
            copied.append(packed[plane])
        if onward and "cots" in parts:
            copied.append(cots[plane])
        if kind == "rows":
            copied.append(cotangent)
        waiting = [other for other, what, where in late if (what, where) == (kind, plane)]
        if waiting:
            copied += [packed[0], cotangent]
        value = cots.get(plane, cotangent)
        sent, copies = select(ids, packed[plane], value, cap, top, parts, copied, flops, last)
        copies = list(copies)
        arrived[plane, kind] = swap_inner(sent)
        for part, held in (("rows", packed), ("cots", cots)):
            if onward and part in parts:
                copy = copies.pop(0)
                for other in onward:
                    held[other] = swap(copy, (other & -other) * inner)
        if kind == "rows":
            cots[plane] = swap(copies.pop(0), plane * inner)
        for other in waiting:
            packed[other] = swap(copies[0], other * inner)
            cots[other] = swap(copies[1], other * inner)
        return sent[0]

    last, weights, own, received, results = None, None, None, None, None
    for kind, plane, size in chain:
        after = [] if last is None else [last]
        flops = 1 << size
        if kind in ("both", "rows", "cots"):
            last = send(kind, plane, flops, after)
        elif kind == "flip":
            weights = flip(weight_gate, weight_up, weight_down, flops, last)
            last = weights[3]
        elif kind == "begin":
            begun[plane] = begin(arrived[plane, "rows"], weights, flops, after)
            last = begun[plane][1]
        elif kind == "expert":
            pieces = arrived[plane, "cots" if plane in begun else "both"]
            pair_cot, saved[plane] = expert(pieces, weights, begun.get(plane, []), flops, after)
            returned[plane] = swap_inner(pair_cot)
            last = pair_cot[0]
        elif kind == "own":
            own = last = expand(ids, packed[0], returned[0], top, F32, flops, last)
        elif kind == "expand":
            last = expand(ids, packed[plane], returned[plane], top, BF16, flops, last)
            partial.append(swap(last, plane * inner))
        elif kind == "total":
            own = last = total(own, partial[:plane], F32, flops, last)
            del partial[:plane]
        elif kind == "lend":
            (last,) = grads(ids, [saved[other] for other in planes], [], flops, last)
            received = lax.ppermute(last, "dp", [(0, 1), (1, 0)])
        elif kind == "finish":
            kept = [saved[other] for other in planes]
            *results, last = grads(ids, kept, [received], flops, last)
    input_grad = total(own, partial, BF16, 1, last)
    return (input_grad, *(value[None] for value in results))


def solution(mesh):
    return jax.shard_map(
        local,
        mesh=mesh,
        in_specs=(
            P(("dp", "expert"), None),
            P(("dp", "expert"), None),
            P(("dp", "expert"), None),
            P(("dp", "expert"), None),
            P("expert", None, None),
            P("expert", None, None),
            P("expert", None, None),
        ),
        out_specs=(
            P(("dp", "expert"), None),
            P("expert", "dp", None),
            P("expert", "dp", None),
            P("expert", "dp", None),
        ),
        check_vma=False,
    )
```

```python
import functools

import jax
import jax.numpy as jnp
from jax import lax
from jax.experimental import pallas as pl
from jax.experimental.pallas import tpu as pltpu
from jax.sharding import PartitionSpec as P

BF16 = jnp.bfloat16
F32 = jnp.float32
META = 16
PARAMS = pltpu.CompilerParams(vmem_limit_bytes=8 << 20)
LARGE = pltpu.CompilerParams(vmem_limit_bytes=18 << 20)
VMEM = pl.BlockSpec(memory_space=pltpu.VMEM)
SMEM = pl.BlockSpec(memory_space=pltpu.SMEM)
ANYWHERE = pl.BlockSpec(memory_space=pl.ANY)
HBM = pl.BlockSpec(memory_space=pltpu.HBM)


def estimate(flops):
    return pl.CostEstimate(flops=flops, transcendentals=0, bytes_accessed=1)


def dot(left, right, dims=((1,), (0,))):
    return lax.dot_general(left, right, (dims, ((), ())), preferred_element_type=F32)


def array(shape, dtype=BF16):
    return jax.ShapeDtypeStruct(shape, dtype)


def in_hbm(*values):
    return [pltpu.with_memory_space_constraint(value, pltpu.HBM) for value in values]


def in_vmem(*values):
    return [pltpu.with_memory_space_constraint(value, pltpu.VMEM) for value in values]


def resident(*shape, dtype=BF16):
    return pltpu.VMEM(shape, dtype)


def pack_kernel(in_ref, experts_ref, mixing_ref, out_ref, block_ref, sems):
    tokens, model = in_ref.shape
    rows = pltpu.make_async_copy(in_ref, out_ref.at[:tokens], sems.at[0])
    rows.start()
    mixing = mixing_ref[...]
    high = mixing.astype(BF16).astype(F32)
    middle = (mixing - high).astype(BF16).astype(F32)
    low = mixing - high - middle
    block = [experts_ref[...].astype(F32), high, middle, low]
    if META > 4 * mixing.shape[0]:
        block.append(jnp.zeros((META - 4 * mixing.shape[0], tokens), F32))
    block_ref[:, :tokens] = jnp.concatenate(block, axis=0).astype(BF16)
    block_ref[:, tokens:] = jnp.zeros((META, model - tokens), BF16)
    routing = pltpu.make_async_copy(block_ref, out_ref.at[tokens:], sems.at[1])
    routing.start()
    rows.wait()
    routing.wait()


def pack(tokens, experts, mixing, flops=1):
    rows, model = tokens.shape
    return pl.pallas_call(
        pack_kernel,
        out_shape=array((rows + META, model)),
        in_specs=[HBM, VMEM, VMEM],
        out_specs=HBM,
        scratch_shapes=[pltpu.VMEM((META, model), BF16), pltpu.SemaphoreType.DMA((2,))],
        compiler_params=PARAMS,
        cost_estimate=estimate(flops),
        name="pack",
    )(*in_hbm(tokens), experts.T, mixing.T)


def slot_masks(ids_ref, block, count, cap, top):
    block = block.astype(F32)
    chosen, high, middle, low = (block[top * part : top * (part + 1)] for part in range(4))
    mixing = (high + middle) + low
    tokens = chosen.shape[1]
    earlier = lax.broadcasted_iota(jnp.int32, (tokens, tokens), 0)
    later = lax.broadcasted_iota(jnp.int32, (tokens, tokens), 1)
    before = (earlier < later).astype(F32)
    slot = lax.broadcasted_iota(jnp.int32, (cap, tokens), 0).astype(F32)
    named, weights = [], []
    for which in range(count):
        hit = chosen == ids_ref[which].astype(F32)
        named.append(jnp.sum(jnp.where(hit, 1.0, 0.0), axis=0, keepdims=True))
        weights.append(jnp.sum(jnp.where(hit, mixing, 0.0), axis=0, keepdims=True))
    position = dot(jnp.concatenate(named, axis=0), before)
    onehot, slot_weight = [], []
    for which in range(count):
        here = (slot == position[which : which + 1]) & (named[which] > 0.5)
        onehot.append(jnp.where(here, 1.0, 0.0))
        slot_weight.append(jnp.sum(jnp.where(here, weights[which], 0.0), axis=1, keepdims=True))
    return jnp.concatenate(onehot, axis=0), jnp.concatenate(slot_weight, axis=0)


def select_kernel(count, cap, top, parts, copied, ids_ref, *refs):
    packed_ref, cots_ref = refs[:2]
    sources = refs[2 : 2 + copied]
    targets, sems = refs[-1 - copied : -1], refs[-1]
    outs = refs[-1 - copied - count : -1 - copied]
    copies = [
        pltpu.make_async_copy(source, target, sems.at[which])
        for which, (source, target) in enumerate(zip(sources, targets))
    ]
    for copy in copies:
        copy.start()
    model = packed_ref.shape[1]
    tokens = packed_ref.shape[0] - META
    masks, weight = slot_masks(ids_ref, packed_ref[tokens:, :tokens], count, cap, top)
    onehot = masks.astype(BF16)
    step = min(512, model)
    for start in range(0, model, step):
        columns = slice(start, start + step)
        for place, part in enumerate(parts):
            if part == "rows":
                value = dot(onehot, packed_ref[:tokens, columns])
            else:
                value = dot(onehot, cots_ref[:, columns]) * weight
            value = value.astype(BF16)
            for which in range(count):
                outs[which][place, :, columns] = value[which * cap : (which + 1) * cap]
    for copy in copies:
        copy.wait()


def select(ids, packed, cots, cap, top, parts, copied, flops, after):
    count = ids.shape[0] - 2
    model = packed.shape[1]
    result = pl.pallas_call(
        functools.partial(select_kernel, count, cap, top, parts, len(copied)),
        out_shape=[array((len(parts), cap, model))] * count
        + [array(value.shape) for value in copied],
        in_specs=[SMEM, VMEM, VMEM if "cots" in parts else ANYWHERE]
        + [ANYWHERE] * (len(copied) + len(after)),
        out_specs=[VMEM] * count + [HBM] * len(copied),
        scratch_shapes=[pltpu.SemaphoreType.DMA((max(1, len(copied)),))],
        compiler_params=PARAMS,
        cost_estimate=estimate(flops),
        name="select",
    )(ids, packed, cots, *copied, *after)
    return result[:count], result[count:]


def flip_kernel(gate_in, up_in, down_in, _, gate_ref, up_ref, both_ref, flipped_ref, down, sems):
    copies = [
        pltpu.make_async_copy(source, target, sems.at[which])
        for which, (source, target) in enumerate(
            ((gate_in, gate_ref), (up_in, up_ref), (down_in, down))
        )
    ]
    for copy in copies:
        copy.start()
    model, units = gate_ref.shape
    step = min(512, model)
    for which, source in enumerate((gate_ref, up_ref)):
        copies[which].wait()
        for start in range(0, model, step):
            both_ref[which * units : (which + 1) * units, start : start + step] = source[
                start : start + step, :
            ].T
    copies[2].wait()
    for start in range(0, model, step):
        flipped_ref[start : start + step, :] = down[:, start : start + step].T


def flip(weight_gate, weight_up, weight_down, flops, after):
    model, units = weight_gate.shape
    return pl.pallas_call(
        flip_kernel,
        in_specs=[HBM] * 3 + [ANYWHERE],
        out_specs=[VMEM] * 4,
        out_shape=[
            resident(model, units),
            resident(model, units),
            resident(2 * units, model),
            resident(model, units),
        ],
        scratch_shapes=[pltpu.VMEM((units, model), BF16), pltpu.SemaphoreType.DMA((3,))],
        compiler_params=PARAMS,
        cost_estimate=estimate(flops),
        name="flip",
    )(*in_hbm(weight_gate, weight_up, weight_down), after)


def begin_kernel(count, *refs):
    ins = refs[:count]
    gate_ref, up_ref = refs[count : count + 2]
    rows_ref, pre_gate_ref, pre_up_ref = refs[-3:]
    cap = ins[0].shape[1]
    for which in range(count):
        rows_ref[which * cap : (which + 1) * cap, :] = ins[which][0]
    pre_gate_ref[...] = dot(rows_ref[...], gate_ref[...])
    pre_up_ref[...] = dot(rows_ref[...], up_ref[...])


def begin(arrived, weights, flops, after):
    count = len(arrived)
    _, cap, model = arrived[0].shape
    units = weights[0].shape[1]
    rows = count * cap
    return pl.pallas_call(
        functools.partial(begin_kernel, count),
        in_specs=[VMEM] * (count + 2) + [ANYWHERE] * len(after),
        out_specs=[VMEM] * 3,
        out_shape=[resident(rows, model)] + [resident(rows, units, dtype=F32)] * 2,
        compiler_params=PARAMS,
        cost_estimate=estimate(flops),
        name="begin",
    )(*arrived, *in_vmem(*weights[:2]), *after)


def expert_kernel(count, begun, *refs):
    ins = refs[:count]
    gate_ref, up_ref, both_ref, flipped_ref = refs[count : count + 4]
    cap = ins[0].shape[1]
    model, units = gate_ref.shape
    if begun:
        pre_gate_ref, pre_up_ref = refs[count + 4 : count + 6]
        outs, (cots_ref, pair_units_ref, hidden_ref) = refs[-count - 3 : -3], refs[-3:]
    else:
        outs = refs[-count - 4 : -4]
        rows_ref, cots_ref, pair_units_ref, hidden_ref = refs[-4:]
    for which in range(count):
        part = slice(which * cap, (which + 1) * cap)
        if not begun:
            rows_ref[part, :] = ins[which][0]
        cots_ref[part, :] = ins[which][0 if begun else 1]
    block = min(256, units)
    for start in range(0, units, block):
        columns = slice(start, start + block)
        if begun:
            pre_gate, pre_up = pre_gate_ref[:, columns], pre_up_ref[:, columns]
        else:
            pre_gate = dot(rows_ref[...], gate_ref[:, columns])
            pre_up = dot(rows_ref[...], up_ref[:, columns])
        hidden_cot = dot(cots_ref[...], flipped_ref[:, columns])
        sigmoid_gate = jax.nn.sigmoid(pre_gate)
        activated = pre_gate * sigmoid_gate
        hidden_ref[:, columns] = (activated * pre_up).astype(BF16)
        pair_units_ref[:, columns] = (
            hidden_cot * pre_up * sigmoid_gate * (1.0 + pre_gate * (1.0 - sigmoid_gate))
        ).astype(BF16)
        pair_units_ref[:, units + start : units + start + block] = (
            hidden_cot * activated
        ).astype(BF16)
    block = min(512, model)
    for start in range(0, model, block):
        columns = slice(start, start + block)
        pair_cot = dot(pair_units_ref[...], both_ref[:, columns]).astype(BF16)
        for which in range(count):
            outs[which][:, columns] = pair_cot[which * cap : (which + 1) * cap]


def expert(arrived, weights, begun, flops, after):
    count = len(arrived)
    _, cap, model = arrived[0].shape
    units = weights[0].shape[1]
    rows = count * cap
    kept = [resident(rows, model)] * (1 if begun else 2)
    kept += [resident(rows, 2 * units), resident(rows, units)]
    result = pl.pallas_call(
        functools.partial(expert_kernel, count, bool(begun)),
        in_specs=[VMEM] * (count + 4 + len(begun[1:])) + [ANYWHERE] * len(after),
        out_specs=[VMEM] * (count + len(kept)),
        out_shape=[array((cap, model))] * count + kept,
        compiler_params=PARAMS,
        cost_estimate=estimate(flops),
        name="expert",
    )(*arrived, *in_vmem(*weights, *begun[1:]), *after)
    return result[:count], list(begun[:1]) + list(result[count:])


STEPS = 4


def grads_kernel(planes, add, based, ids_ref, *refs):
    saved = [refs[4 * which : 4 * which + 4] for which in range(planes)]
    base = refs[4 * planes : 4 * planes + based]
    refs = refs[4 * planes + based :]
    model, units = saved[0][0].shape[1], saved[0][3].shape[1]
    half = ids_ref[ids_ref.shape[0] - (2 if add else 1)]
    height, width = model // 2 // STEPS, model // STEPS
    rest = units // 2 - height
    fold = height // rest
    part = width // fold
    if add:
        other_in, _, gate_out, up_out, down_out, token, gate_ref, up_ref, down_ref, other_ref, sems, other_sems = refs
        token[...] = jnp.zeros(token.shape, F32)
    else:
        _, sent_out, sent_ref, sems = refs
    own_units = pl.ds(pl.multiple_of(half * (units // 2), 128), units // 2)
    flipped_hidden = jnp.concatenate([kept[3][:, own_units].T for kept in saved], axis=1)
    pair_units = jnp.concatenate([kept[2][...] for kept in saved], axis=0)

    def fetch(step):
        at = slice(step * height, (step + 1) * height)
        slot = step % 2
        return pltpu.make_async_copy(other_in.at[at], other_ref.at[slot], other_sems.at[slot])

    def moves(step):
        at = slice(step * height, (step + 1) * height)
        across = slice(step * width, (step + 1) * width)
        slot = step % 2
        if add:
            pairs = (
                (gate_ref.at[slot], gate_out.at[at]),
                (up_ref.at[slot], up_out.at[at]),
                (down_ref.at[slot], down_out.at[:, across]),
            )
        else:
            pairs = ((sent_ref.at[slot], sent_out.at[at]),)
        return [
            pltpu.make_async_copy(source, target, sems.at[slot, which])
            for which, (source, target) in enumerate(pairs)
        ]

    if add:
        fetch(0).start()
    for step in range(STEPS):
        slot = step % 2
        across = slice(step * width, (step + 1) * width)
        own_rows = pl.ds(pl.multiple_of(half * (model // 2) + step * height, 128), height)
        flipped = jnp.concatenate([kept[0][:, own_rows].T for kept in saved], axis=1)
        both = dot(flipped, pair_units)
        down = dot(flipped_hidden, jnp.concatenate([kept[1][:, across] for kept in saved], axis=0))
        if based:
            both = both + base[0][step * height : (step + 1) * height, :]
            down = down + base[1][:, across]
        if step >= 2:
            for copy in moves(step - 2):
                copy.wait()
        if add:
            fetch(step).wait()
            if step + 1 < STEPS:
                fetch(step + 1).start()
            gate_ref[slot] = both[:, :units] + other_ref[slot, :, :units].astype(F32)
            up_ref[slot] = both[:, units:] + other_ref[slot, :, units : 2 * units].astype(F32)
            down_ref[slot, :height, :] = down[:height] + other_ref[
                slot, :, 2 * units : 2 * units + width
            ].astype(F32)
            for which in range(fold):
                columns = slice(which * part, (which + 1) * part)
                lower = slice(which * rest, (which + 1) * rest)
                down_ref[slot, height:, columns] = down[height:, columns] + other_ref[
                    slot, lower, 2 * units + width :
                ].astype(F32)
        else:
            sent_ref[slot, :, : 2 * units] = both.astype(BF16)
            down = down.astype(BF16)
            sent_ref[slot, :, 2 * units : 2 * units + width] = down[:height]
            for which in range(fold):
                lower = slice(which * rest, (which + 1) * rest)
                sent_ref[slot, lower, 2 * units + width :] = down[
                    height:, which * part : (which + 1) * part
                ]
        for copy in moves(step):
            copy.start()
    for step in range(STEPS - 2, STEPS):
        for copy in moves(step):
            copy.wait()


def grads(ids, saved, base, received, flops, after):
    model, units = saved[0][0].shape[1], saved[0][3].shape[1]
    height = model // 2 // STEPS
    sent_width = 3 * units
    add = bool(received)
    if add:
        shapes = [(model // 2, units), (model // 2, units), (units // 2, model)]
        stages = [(2, height, units), (2, height, units), (2, units // 2, model // STEPS)]
        dtype = F32
    else:
        shapes, stages, dtype = [(model // 2, sent_width)], [(2, height, sent_width)], BF16
    scratch = [pltpu.VMEM(shape, dtype) for shape in stages]
    if add:
        scratch.append(pltpu.VMEM((2, height, sent_width), BF16))
    scratch.append(pltpu.SemaphoreType.DMA((2, len(shapes))))
    if add:
        scratch.append(pltpu.SemaphoreType.DMA((2,)))
    return pl.pallas_call(
        functools.partial(grads_kernel, len(saved), add, len(base)),
        in_specs=[SMEM] + [VMEM] * (4 * len(saved) + len(base)) + [ANYWHERE] * (1 + add),
        out_specs=[HBM] * len(shapes) + [VMEM] * add,
        out_shape=[array(shape, dtype) for shape in shapes] + [array((8, 128), F32)] * add,
        scratch_shapes=scratch,
        compiler_params=LARGE,
        cost_estimate=estimate(flops),
        name="grads",
    )(ids, *in_vmem(*(part for kept in saved for part in kept), *base), *received, after)


def part_kernel(planes, ids_ref, *refs):
    saved = [refs[4 * which : 4 * which + 4] for which in range(planes)]
    both_ref, down_ref = refs[-2:]
    model, units = saved[0][0].shape[1], saved[0][3].shape[1]
    half = ids_ref[ids_ref.shape[0] - 1]
    height, width = model // 2 // STEPS, model // STEPS
    own_units = pl.ds(pl.multiple_of(half * (units // 2), 128), units // 2)
    flipped_hidden = jnp.concatenate([kept[3][:, own_units].T for kept in saved], axis=1)
    pair_units = jnp.concatenate([kept[2][...] for kept in saved], axis=0)
    for step in range(STEPS):
        across = slice(step * width, (step + 1) * width)
        own_rows = pl.ds(pl.multiple_of(half * (model // 2) + step * height, 128), height)
        flipped = jnp.concatenate([kept[0][:, own_rows].T for kept in saved], axis=1)
        both_ref[step * height : (step + 1) * height, :] = dot(flipped, pair_units)
        down_ref[:, across] = dot(
            flipped_hidden, jnp.concatenate([kept[1][:, across] for kept in saved], axis=0)
        )


def part(ids, saved, flops, after):
    model, units = saved[0][0].shape[1], saved[0][3].shape[1]
    return pl.pallas_call(
        functools.partial(part_kernel, len(saved)),
        in_specs=[SMEM] + [VMEM] * (4 * len(saved)) + [ANYWHERE],
        out_specs=[VMEM] * 2,
        out_shape=[
            resident(model // 2, 2 * units, dtype=F32),
            resident(units // 2, model, dtype=F32),
        ],
        compiler_params=PARAMS,
        cost_estimate=estimate(flops),
        name="part",
    )(ids, *in_vmem(*(part for kept in saved for part in kept)), after)


def expand_kernel(count, top, ids_ref, meta_ref, *refs):
    back, out = refs[:count], refs[-1]
    cap, model = back[0].shape
    onehot, _ = slot_masks(ids_ref, meta_ref[...], count, cap, top)
    spread = onehot.T.astype(BF16)
    step = min(512, model)
    for start in range(0, model, step):
        columns = slice(start, start + step)
        value = dot(spread, jnp.concatenate([ref[:, columns] for ref in back], axis=0))
        out[:, columns] = value.astype(out.dtype)


def expand(ids, packed, back, top, dtype, flops, after):
    count = len(back)
    cap, model = back[0].shape
    tokens = packed.shape[0] - META
    whole = lambda *shape: pl.BlockSpec(shape, lambda s: (0, 0))
    return pl.pallas_call(
        functools.partial(expand_kernel, count, top),
        grid=(1,),
        out_shape=array((tokens, model), dtype),
        in_specs=[SMEM, pl.BlockSpec((META, tokens), lambda s: (tokens // META, 0))]
        + [whole(cap, model)] * count
        + [ANYWHERE],
        out_specs=whole(tokens, model),
        compiler_params=PARAMS,
        cost_estimate=estimate(flops),
        name="expand",
    )(ids, packed, *back, after)


def total_kernel(count, own_ref, *refs):
    value = own_ref[...]
    for ref in refs[:count]:
        value = value + ref[...].astype(F32)
    refs[-1][...] = value.astype(refs[-1].dtype)


def total(own, others, dtype, flops, after):
    return pl.pallas_call(
        functools.partial(total_kernel, len(others)),
        out_shape=array(own.shape, dtype),
        in_specs=[VMEM] * (1 + len(others)) + [ANYWHERE],
        out_specs=VMEM,
        compiler_params=PARAMS,
        cost_estimate=estimate(flops),
        name="total",
    )(own, *others, after)


FOUR_PLANES = (
    ("both", 0, 0),
    ("flip", 0, 0),
    ("rows", 2, 0),
    ("expert", 0, 0),
    ("begin", 2, 34),
    ("own", 0, 0),
    ("cots", 2, 0),
    ("both", 3, 0),
    ("expert", 2, 29),
    ("expert", 3, 0),
    ("both", 1, 0),
    ("expand", 2, 0),
    ("expand", 3, 0),
    ("total", 1, 0),
    ("expert", 1, 0),
    ("lend", 0, 37),
    ("expand", 1, 37),
    ("finish", 0, 37),
)
LATE = ()


def many_planes(outer):
    order = list(range(2, outer)) + [1]
    chain = [("both", 0, 0), ("flip", 0, 0), ("expert", 0, 0), ("own", 0, 0)]
    for plane in order:
        chain += [("both", plane, 0), ("expert", plane, 0)]
        chain += [("expand", plane, 0)]
    return chain + [("lend", 0, 0), ("finish", 0, 0)]


def local(tokens, cotangent, experts, mixing, gate_matrix, up_matrix, down_matrix):
    expert_count = lax.axis_size("expert")
    inner = min(4, expert_count)
    outer = expert_count // inner
    tok_rows, top = experts.shape
    cap = 2 * tok_rows * top // expert_count
    weight_gate, weight_up, weight_down = gate_matrix[0], up_matrix[0], down_matrix[0]

    def swap(value, mask):
        pairs = [(device, device ^ mask) for device in range(expert_count)]
        return lax.ppermute(value, "expert", pairs)

    def swap_inner(values):
        return [values[0]] + [swap(values[which], which) for which in range(1, inner)]

    core = lax.axis_index("dp").astype(jnp.int32)
    plane_ids = jnp.bitwise_xor(lax.axis_index("expert").astype(jnp.int32), jnp.arange(inner, dtype=jnp.int32))
    ids = jnp.concatenate([plane_ids, jnp.stack([core, 1 - core])])
    chain = FOUR_PLANES if outer == 4 else many_planes(outer)
    planes = [plane for kind, plane, _ in chain if kind == "expert"]
    packed = {0: pack(tokens, experts, mixing)}
    cots = {0: cotangent}
    arrived, returned, partial, saved, begun = {}, {}, [], {}, {}
    late = LATE if outer == 4 else ()
    late_planes = [plane for plane, _, _ in late]
    split = [plane for kind, plane, _ in chain if kind == "rows"]
    for plane in planes[1:]:
        if plane == plane & -plane and plane not in late_planes:
            packed[plane] = swap(packed[0], plane * inner)
            if plane not in split:
                cots[plane] = swap(cotangent, plane * inner)

    def send(kind, plane, flops, last):
        parts = ("rows", "cots") if kind == "both" else (kind,)
        onward = [other for other in planes if other ^ (other & -other) == plane and plane]
        copied = []
        if onward and "rows" in parts:
            copied.append(packed[plane])
        if onward and "cots" in parts:
            copied.append(cots[plane])
        if kind == "rows":
            copied.append(cotangent)
        waiting = [other for other, what, where in late if (what, where) == (kind, plane)]
        if waiting:
            copied += [packed[0], cotangent]
        value = cots.get(plane, cotangent)
        sent, copies = select(ids, packed[plane], value, cap, top, parts, copied, flops, last)
        copies = list(copies)
        arrived[plane, kind] = swap_inner(sent)
        for part, held in (("rows", packed), ("cots", cots)):
            if onward and part in parts:
                copy = copies.pop(0)
                for other in onward:
                    held[other] = swap(copy, (other & -other) * inner)
        if kind == "rows":
            cots[plane] = swap(copies.pop(0), plane * inner)
        for other in waiting:
            packed[other] = swap(copies[0], other * inner)
            cots[other] = swap(copies[1], other * inner)
        return sent[0]

    last, weights, own, received, results = None, None, None, None, None
    base, based = [], []
    for kind, plane, size in chain:
        after = [] if last is None else [last]
        flops = 1 << size
        if kind in ("both", "rows", "cots"):
            last = send(kind, plane, flops, after)
        elif kind == "flip":
            weights = flip(weight_gate, weight_up, weight_down, flops, last)
            last = weights[3]
        elif kind == "begin":
            begun[plane] = begin(arrived[plane, "rows"], weights, flops, after)
            last = begun[plane][1]
        elif kind == "expert":
            pieces = arrived[plane, "cots" if plane in begun else "both"]
            pair_cot, saved[plane] = expert(pieces, weights, begun.get(plane, []), flops, after)
            returned[plane] = swap_inner(pair_cot)
            last = pair_cot[0]
        elif kind == "own":
            own = last = expand(ids, packed[0], returned[0], top, F32, flops, last)
        elif kind == "expand":
            last = expand(ids, packed[plane], returned[plane], top, BF16, flops, last)
            partial.append(swap(last, plane * inner))
        elif kind == "total":
            own = last = total(own, partial[:plane], F32, flops, last)
            del partial[:plane]
        elif kind == "part":
            based = list(saved)
            base = part(ids, [saved[other] for other in based], flops, last)
            last = base[1]
        elif kind == "lend":
            rest = [saved[other] for other in planes if other not in based]
            (last,) = grads(ids, rest, base, [], flops, last)
            received = lax.ppermute(last, "dp", [(0, 1), (1, 0)])
        elif kind == "finish":
            kept = [saved[other] for other in planes]
            *results, last = grads(ids, kept, [], [received], flops, last)
    input_grad = total(own, partial, BF16, 1, last)
    return (input_grad, *(value[None] for value in results))


def solution(mesh):
    return jax.shard_map(
        local,
        mesh=mesh,
        in_specs=(
            P(("dp", "expert"), None),
            P(("dp", "expert"), None),
            P(("dp", "expert"), None),
            P(("dp", "expert"), None),
            P("expert", None, None),
            P("expert", None, None),
            P("expert", None, None),
        ),
        out_specs=(
            P(("dp", "expert"), None),
            P("expert", "dp", None),
            P("expert", "dp", None),
            P("expert", "dp", None),
        ),
        check_vma=False,
    )
```

```python
import functools

import jax
import jax.numpy as jnp
from jax import lax
from jax.experimental import pallas as pl
from jax.experimental.pallas import tpu as pltpu
from jax.sharding import PartitionSpec as P

BF16 = jnp.bfloat16
F32 = jnp.float32
META = 16
PARAMS = pltpu.CompilerParams(vmem_limit_bytes=8 << 20)
LARGE = pltpu.CompilerParams(vmem_limit_bytes=18 << 20)
VMEM = pl.BlockSpec(memory_space=pltpu.VMEM)
SMEM = pl.BlockSpec(memory_space=pltpu.SMEM)
ANYWHERE = pl.BlockSpec(memory_space=pl.ANY)
HBM = pl.BlockSpec(memory_space=pltpu.HBM)


def estimate(flops):
    return pl.CostEstimate(flops=flops, transcendentals=0, bytes_accessed=1)


def dot(left, right, dims=((1,), (0,))):
    return lax.dot_general(left, right, (dims, ((), ())), preferred_element_type=F32)


def array(shape, dtype=BF16):
    return jax.ShapeDtypeStruct(shape, dtype)


def in_hbm(*values):
    return [pltpu.with_memory_space_constraint(value, pltpu.HBM) for value in values]


def in_vmem(*values):
    return [pltpu.with_memory_space_constraint(value, pltpu.VMEM) for value in values]


def resident(*shape, dtype=BF16):
    return pltpu.VMEM(shape, dtype)


def pack_kernel(in_ref, experts_ref, mixing_ref, out_ref, block_ref, sems):
    tokens, model = in_ref.shape
    rows = pltpu.make_async_copy(in_ref, out_ref.at[:tokens], sems.at[0])
    rows.start()
    mixing = mixing_ref[...]
    high = mixing.astype(BF16).astype(F32)
    middle = (mixing - high).astype(BF16).astype(F32)
    low = mixing - high - middle
    block = [experts_ref[...].astype(F32), high, middle, low]
    if META > 4 * mixing.shape[0]:
        block.append(jnp.zeros((META - 4 * mixing.shape[0], tokens), F32))
    block_ref[:, :tokens] = jnp.concatenate(block, axis=0).astype(BF16)
    block_ref[:, tokens:] = jnp.zeros((META, model - tokens), BF16)
    routing = pltpu.make_async_copy(block_ref, out_ref.at[tokens:], sems.at[1])
    routing.start()
    rows.wait()
    routing.wait()


def pack(tokens, experts, mixing, flops=1):
    rows, model = tokens.shape
    return pl.pallas_call(
        pack_kernel,
        out_shape=array((rows + META, model)),
        in_specs=[HBM, VMEM, VMEM],
        out_specs=HBM,
        scratch_shapes=[pltpu.VMEM((META, model), BF16), pltpu.SemaphoreType.DMA((2,))],
        compiler_params=PARAMS,
        cost_estimate=estimate(flops),
        name="pack",
    )(*in_hbm(tokens), experts.T, mixing.T)


def slot_masks(ids_ref, block, count, cap, top):
    block = block.astype(F32)
    chosen, high, middle, low = (block[top * part : top * (part + 1)] for part in range(4))
    mixing = (high + middle) + low
    tokens = chosen.shape[1]
    earlier = lax.broadcasted_iota(jnp.int32, (tokens, tokens), 0)
    later = lax.broadcasted_iota(jnp.int32, (tokens, tokens), 1)
    before = (earlier < later).astype(F32)
    slot = lax.broadcasted_iota(jnp.int32, (cap, tokens), 0).astype(F32)
    named, weights = [], []
    for which in range(count):
        hit = chosen == ids_ref[which].astype(F32)
        named.append(jnp.sum(jnp.where(hit, 1.0, 0.0), axis=0, keepdims=True))
        weights.append(jnp.sum(jnp.where(hit, mixing, 0.0), axis=0, keepdims=True))
    position = dot(jnp.concatenate(named, axis=0), before)
    onehot, slot_weight = [], []
    for which in range(count):
        here = (slot == position[which : which + 1]) & (named[which] > 0.5)
        onehot.append(jnp.where(here, 1.0, 0.0))
        slot_weight.append(jnp.sum(jnp.where(here, weights[which], 0.0), axis=1, keepdims=True))
    return jnp.concatenate(onehot, axis=0), jnp.concatenate(slot_weight, axis=0)


def select_kernel(count, cap, top, parts, copied, ids_ref, *refs):
    packed_ref, cots_ref = refs[:2]
    sources = refs[2 : 2 + copied]
    targets, sems = refs[-1 - copied : -1], refs[-1]
    outs = refs[-1 - copied - count : -1 - copied]
    copies = [
        pltpu.make_async_copy(source, target, sems.at[which])
        for which, (source, target) in enumerate(zip(sources, targets))
    ]
    for copy in copies:
        copy.start()
    model = packed_ref.shape[1]
    tokens = packed_ref.shape[0] - META
    masks, weight = slot_masks(ids_ref, packed_ref[tokens:, :tokens], count, cap, top)
    onehot = masks.astype(BF16)
    step = min(512, model)
    for start in range(0, model, step):
        columns = slice(start, start + step)
        for place, part in enumerate(parts):
            if part == "rows":
                value = dot(onehot, packed_ref[:tokens, columns])
            else:
                value = dot(onehot, cots_ref[:, columns]) * weight
            value = value.astype(BF16)
            for which in range(count):
                outs[which][place, :, columns] = value[which * cap : (which + 1) * cap]
    for copy in copies:
        copy.wait()


def select(ids, packed, cots, cap, top, parts, copied, flops, after):
    count = ids.shape[0] - 2
    model = packed.shape[1]
    result = pl.pallas_call(
        functools.partial(select_kernel, count, cap, top, parts, len(copied)),
        out_shape=[array((len(parts), cap, model))] * count
        + [array(value.shape) for value in copied],
        in_specs=[SMEM, VMEM, VMEM if "cots" in parts else ANYWHERE]
        + [ANYWHERE] * (len(copied) + len(after)),
        out_specs=[VMEM] * count + [HBM] * len(copied),
        scratch_shapes=[pltpu.SemaphoreType.DMA((max(1, len(copied)),))],
        compiler_params=PARAMS,
        cost_estimate=estimate(flops),
        name="select",
    )(ids, packed, cots, *copied, *after)
    return result[:count], result[count:]


def flip_kernel(gate_in, up_in, down_in, _, gate_ref, up_ref, both_ref, flipped_ref, down, sems):
    copies = [
        pltpu.make_async_copy(source, target, sems.at[which])
        for which, (source, target) in enumerate(
            ((gate_in, gate_ref), (up_in, up_ref), (down_in, down))
        )
    ]
    for copy in copies:
        copy.start()
    model, units = gate_ref.shape
    step = min(512, model)
    for which, source in enumerate((gate_ref, up_ref)):
        copies[which].wait()
        for start in range(0, model, step):
            both_ref[which * units : (which + 1) * units, start : start + step] = source[
                start : start + step, :
            ].T
    copies[2].wait()
    for start in range(0, model, step):
        flipped_ref[start : start + step, :] = down[:, start : start + step].T


def flip(weight_gate, weight_up, weight_down, flops, after):
    model, units = weight_gate.shape
    return pl.pallas_call(
        flip_kernel,
        in_specs=[HBM] * 3 + [ANYWHERE],
        out_specs=[VMEM] * 4,
        out_shape=[
            resident(model, units),
            resident(model, units),
            resident(2 * units, model),
            resident(model, units),
        ],
        scratch_shapes=[pltpu.VMEM((units, model), BF16), pltpu.SemaphoreType.DMA((3,))],
        compiler_params=PARAMS,
        cost_estimate=estimate(flops),
        name="flip",
    )(*in_hbm(weight_gate, weight_up, weight_down), after)


def begin_kernel(count, *refs):
    ins = refs[:count]
    gate_ref, up_ref = refs[count : count + 2]
    rows_ref, pre_gate_ref, pre_up_ref = refs[-3:]
    cap = ins[0].shape[1]
    for which in range(count):
        rows_ref[which * cap : (which + 1) * cap, :] = ins[which][0]
    pre_gate_ref[...] = dot(rows_ref[...], gate_ref[...])
    pre_up_ref[...] = dot(rows_ref[...], up_ref[...])


def begin(arrived, weights, flops, after):
    count = len(arrived)
    _, cap, model = arrived[0].shape
    units = weights[0].shape[1]
    rows = count * cap
    return pl.pallas_call(
        functools.partial(begin_kernel, count),
        in_specs=[VMEM] * (count + 2) + [ANYWHERE] * len(after),
        out_specs=[VMEM] * 3,
        out_shape=[resident(rows, model)] + [resident(rows, units, dtype=F32)] * 2,
        compiler_params=PARAMS,
        cost_estimate=estimate(flops),
        name="begin",
    )(*arrived, *in_vmem(*weights[:2]), *after)


def expert_kernel(count, begun, *refs):
    ins = refs[:count]
    gate_ref, up_ref, both_ref, flipped_ref = refs[count : count + 4]
    cap = ins[0].shape[1]
    model, units = gate_ref.shape
    if begun:
        pre_gate_ref, pre_up_ref = refs[count + 4 : count + 6]
        outs, (cots_ref, pair_units_ref, hidden_ref) = refs[-count - 3 : -3], refs[-3:]
    else:
        outs = refs[-count - 4 : -4]
        rows_ref, cots_ref, pair_units_ref, hidden_ref = refs[-4:]
    for which in range(count):
        part = slice(which * cap, (which + 1) * cap)
        if not begun:
            rows_ref[part, :] = ins[which][0]
        cots_ref[part, :] = ins[which][0 if begun else 1]
    block = min(256, units)
    for start in range(0, units, block):
        columns = slice(start, start + block)
        if begun:
            pre_gate, pre_up = pre_gate_ref[:, columns], pre_up_ref[:, columns]
        else:
            pre_gate = dot(rows_ref[...], gate_ref[:, columns])
            pre_up = dot(rows_ref[...], up_ref[:, columns])
        hidden_cot = dot(cots_ref[...], flipped_ref[:, columns])
        sigmoid_gate = jax.nn.sigmoid(pre_gate)
        activated = pre_gate * sigmoid_gate
        hidden_ref[:, columns] = (activated * pre_up).astype(BF16)
        pair_units_ref[:, columns] = (
            hidden_cot * pre_up * sigmoid_gate * (1.0 + pre_gate * (1.0 - sigmoid_gate))
        ).astype(BF16)
        pair_units_ref[:, units + start : units + start + block] = (
            hidden_cot * activated
        ).astype(BF16)
    block = min(512, model)
    for start in range(0, model, block):
        columns = slice(start, start + block)
        pair_cot = dot(pair_units_ref[...], both_ref[:, columns]).astype(BF16)
        for which in range(count):
            outs[which][:, columns] = pair_cot[which * cap : (which + 1) * cap]


def expert(arrived, weights, begun, flops, after):
    count = len(arrived)
    _, cap, model = arrived[0].shape
    units = weights[0].shape[1]
    rows = count * cap
    kept = [resident(rows, model)] * (1 if begun else 2)
    kept += [resident(rows, 2 * units), resident(rows, units)]
    result = pl.pallas_call(
        functools.partial(expert_kernel, count, bool(begun)),
        in_specs=[VMEM] * (count + 4 + len(begun[1:])) + [ANYWHERE] * len(after),
        out_specs=[VMEM] * (count + len(kept)),
        out_shape=[array((cap, model))] * count + kept,
        compiler_params=PARAMS,
        cost_estimate=estimate(flops),
        name="expert",
    )(*arrived, *in_vmem(*weights, *begun[1:]), *after)
    return result[:count], list(begun[:1]) + list(result[count:])


STEPS = 4


def lend_kernel(planes, ids_ref, *refs):
    saved = [refs[4 * which : 4 * which + 4] for which in range(planes)]
    sent_out, sent_ref, sems = refs[-3:]
    model, units = saved[0][0].shape[1], saved[0][3].shape[1]
    half = ids_ref[ids_ref.shape[0] - 1]
    height, width = model // 2 // STEPS, model // STEPS
    rest = units // 2 - height
    fold = height // rest
    part = width // fold
    own_units = pl.ds(pl.multiple_of(half * (units // 2), 128), units // 2)
    flipped_hidden = jnp.concatenate([kept[3][:, own_units].T for kept in saved], axis=1)
    pair_units = jnp.concatenate([kept[2][...] for kept in saved], axis=0)
    copies = []
    for step in range(STEPS):
        at = slice(step * height, (step + 1) * height)
        across = slice(step * width, (step + 1) * width)
        own_rows = pl.ds(pl.multiple_of(half * (model // 2) + step * height, 128), height)
        flipped = jnp.concatenate([kept[0][:, own_rows].T for kept in saved], axis=1)
        both = dot(flipped, pair_units)
        down = dot(flipped_hidden, jnp.concatenate([kept[1][:, across] for kept in saved], axis=0))
        slot = step % 2
        if step >= 2:
            copies[step - 2].wait()
        sent_ref[slot, :, : 2 * units] = both.astype(BF16)
        down = down.astype(BF16)
        sent_ref[slot, :, 2 * units : 2 * units + width] = down[:height]
        for which in range(fold):
            lower = slice(which * rest, (which + 1) * rest)
            sent_ref[slot, lower, 2 * units + width :] = down[
                height:, which * part : (which + 1) * part
            ]
        copy = pltpu.make_async_copy(sent_ref.at[slot], sent_out.at[at], sems.at[slot])
        copy.start()
        copies.append(copy)
    for copy in copies[-2:]:
        copy.wait()


def lend(ids, saved, flops, after):
    model, units = saved[0][0].shape[1], saved[0][3].shape[1]
    height = model // 2 // STEPS
    return pl.pallas_call(
        functools.partial(lend_kernel, len(saved)),
        in_specs=[SMEM] + [VMEM] * (4 * len(saved)) + [ANYWHERE],
        out_specs=HBM,
        out_shape=array((model // 2, 3 * units)),
        scratch_shapes=[pltpu.VMEM((2, height, 3 * units), BF16), pltpu.SemaphoreType.DMA((2,))],
        compiler_params=LARGE,
        cost_estimate=estimate(flops),
        name="lend",
    )(ids, *in_vmem(*(part for kept in saved for part in kept)), after)


def share_kernel(planes, ids_ref, *refs):
    saved = [refs[4 * which : 4 * which + 4] for which in range(planes)]
    both_ref, down_ref = refs[-2:]
    model, units = saved[0][0].shape[1], saved[0][3].shape[1]
    half = ids_ref[ids_ref.shape[0] - 2]
    height, width = model // 2 // STEPS, model // STEPS
    own_units = pl.ds(pl.multiple_of(half * (units // 2), 128), units // 2)
    flipped_hidden = jnp.concatenate([kept[3][:, own_units].T for kept in saved], axis=1)
    pair_units = jnp.concatenate([kept[2][...] for kept in saved], axis=0)
    for step in range(STEPS):
        across = slice(step * width, (step + 1) * width)
        own_rows = pl.ds(pl.multiple_of(half * (model // 2) + step * height, 128), height)
        flipped = jnp.concatenate([kept[0][:, own_rows].T for kept in saved], axis=1)
        both_ref[step * height : (step + 1) * height, :] = dot(flipped, pair_units)
        down_ref[:, across] = dot(
            flipped_hidden, jnp.concatenate([kept[1][:, across] for kept in saved], axis=0)
        )


def share(ids, saved, flops, after):
    model, units = saved[0][0].shape[1], saved[0][3].shape[1]
    return pl.pallas_call(
        functools.partial(share_kernel, len(saved)),
        in_specs=[SMEM] + [VMEM] * (4 * len(saved)) + [ANYWHERE],
        out_specs=[VMEM] * 2,
        out_shape=[
            resident(model // 2, 2 * units, dtype=F32),
            resident(units // 2, model, dtype=F32),
        ],
        compiler_params=LARGE,
        cost_estimate=estimate(flops),
        name="share",
    )(ids, *in_vmem(*(part for kept in saved for part in kept)), after)


def finish_kernel(
    both_ref, down_ref, other, _, gate_out, up_out, down_out, token, gate_ref, up_ref, own_ref, sems
):
    model, units = down_ref.shape[1], down_ref.shape[0] * 2
    height, width = model // 2 // STEPS, model // STEPS
    rest = units // 2 - height
    fold = height // rest
    part = width // fold
    token[...] = jnp.zeros(token.shape, F32)
    copies = []
    for step in range(STEPS):
        at = slice(step * height, (step + 1) * height)
        across = slice(step * width, (step + 1) * width)
        both = both_ref[at, :] + other[at, : 2 * units].astype(F32)
        gate_ref[at, :] = both[:, :units]
        up_ref[at, :] = both[:, units:]
        own_ref[:height, across] = down_ref[:height, across] + other[
            at, 2 * units : 2 * units + width
        ].astype(F32)
        for which in range(fold):
            lower = slice(step * height + which * rest, step * height + (which + 1) * rest)
            target = slice(step * width + which * part, step * width + (which + 1) * part)
            own_ref[height:, target] = down_ref[height:, target] + other[
                lower, 2 * units + width :
            ].astype(F32)
        moves = (
            (gate_ref.at[at], gate_out.at[at]),
            (up_ref.at[at], up_out.at[at]),
            (own_ref.at[:, across], down_out.at[:, across]),
        )
        for which, (source, target) in enumerate(moves):
            copy = pltpu.make_async_copy(source, target, sems.at[step, which])
            copy.start()
            copies.append(copy)
    for copy in copies:
        copy.wait()


def finish(sums, received, flops, after):
    model, units = sums[1].shape[1], sums[1].shape[0] * 2
    shapes = [(model // 2, units), (model // 2, units), (units // 2, model)]
    return pl.pallas_call(
        finish_kernel,
        in_specs=[VMEM] * 3 + [ANYWHERE],
        out_specs=[HBM] * 3 + [VMEM],
        out_shape=[array(shape, F32) for shape in shapes] + [array((8, 128), F32)],
        scratch_shapes=[pltpu.VMEM(shape, F32) for shape in shapes]
        + [pltpu.SemaphoreType.DMA((STEPS, 3))],
        compiler_params=LARGE,
        cost_estimate=estimate(flops),
        name="finish",
    )(*in_vmem(*sums), received, after)


def expand_kernel(count, top, ids_ref, meta_ref, *refs):
    back, out = refs[:count], refs[-1]
    cap, model = back[0].shape
    onehot, _ = slot_masks(ids_ref, meta_ref[...], count, cap, top)
    spread = onehot.T.astype(BF16)
    step = min(512, model)
    for start in range(0, model, step):
        columns = slice(start, start + step)
        value = dot(spread, jnp.concatenate([ref[:, columns] for ref in back], axis=0))
        out[:, columns] = value.astype(out.dtype)


def expand(ids, packed, back, top, dtype, flops, after):
    count = len(back)
    cap, model = back[0].shape
    tokens = packed.shape[0] - META
    whole = lambda *shape: pl.BlockSpec(shape, lambda s: (0, 0))
    return pl.pallas_call(
        functools.partial(expand_kernel, count, top),
        grid=(1,),
        out_shape=array((tokens, model), dtype),
        in_specs=[SMEM, pl.BlockSpec((META, tokens), lambda s: (tokens // META, 0))]
        + [whole(cap, model)] * count
        + [ANYWHERE],
        out_specs=whole(tokens, model),
        compiler_params=PARAMS,
        cost_estimate=estimate(flops),
        name="expand",
    )(ids, packed, *back, after)


def total_kernel(count, own_ref, *refs):
    value = own_ref[...]
    for ref in refs[:count]:
        value = value + ref[...].astype(F32)
    refs[-1][...] = value.astype(refs[-1].dtype)


def total(own, others, dtype, flops, after):
    return pl.pallas_call(
        functools.partial(total_kernel, len(others)),
        out_shape=array(own.shape, dtype),
        in_specs=[VMEM] * (1 + len(others)) + [ANYWHERE],
        out_specs=VMEM,
        compiler_params=PARAMS,
        cost_estimate=estimate(flops),
        name="total",
    )(own, *others, after)


FOUR_PLANES = (
    ("both", 0, 0),
    ("flip", 0, 0),
    ("rows", 2, 0),
    ("expert", 0, 0),
    ("begin", 2, 34),
    ("own", 0, 0),
    ("cots", 2, 0),
    ("both", 3, 0),
    ("expert", 2, 29),
    ("expert", 3, 0),
    ("both", 1, 0),
    ("expand", 2, 28),
    ("expand", 3, 0),
    ("total", 1, 0),
    ("expert", 1, 0),
    ("lend", 0, 37),
    ("expand", 1, 37),
    ("share", 0, 30),
    ("finish", 0, 0),
)
LATE = ()


def many_planes(outer):
    order = list(range(2, outer)) + [1]
    chain = [("both", 0, 0), ("flip", 0, 0), ("expert", 0, 0), ("own", 0, 0)]
    for plane in order:
        chain += [("both", plane, 0), ("expert", plane, 0)]
        chain += [("expand", plane, 0)]
    return chain + [("lend", 0, 0), ("share", 0, 0), ("finish", 0, 0)]


def local(tokens, cotangent, experts, mixing, gate_matrix, up_matrix, down_matrix):
    expert_count = lax.axis_size("expert")
    inner = min(4, expert_count)
    outer = expert_count // inner
    tok_rows, top = experts.shape
    cap = 2 * tok_rows * top // expert_count
    weight_gate, weight_up, weight_down = gate_matrix[0], up_matrix[0], down_matrix[0]

    def swap(value, mask):
        pairs = [(device, device ^ mask) for device in range(expert_count)]
        return lax.ppermute(value, "expert", pairs)

    def swap_inner(values):
        return [values[0]] + [swap(values[which], which) for which in range(1, inner)]

    core = lax.axis_index("dp").astype(jnp.int32)
    plane_ids = jnp.bitwise_xor(lax.axis_index("expert").astype(jnp.int32), jnp.arange(inner, dtype=jnp.int32))
    ids = jnp.concatenate([plane_ids, jnp.stack([core, 1 - core])])
    chain = FOUR_PLANES if outer == 4 else many_planes(outer)
    planes = [plane for kind, plane, _ in chain if kind == "expert"]
    packed = {0: pack(tokens, experts, mixing)}
    cots = {0: cotangent}
    arrived, returned, partial, saved, begun = {}, {}, [], {}, {}
    late = LATE if outer == 4 else ()
    late_planes = [plane for plane, _, _ in late]
    split = [plane for kind, plane, _ in chain if kind == "rows"]
    for plane in planes[1:]:
        if plane == plane & -plane and plane not in late_planes:
            packed[plane] = swap(packed[0], plane * inner)
            if plane not in split:
                cots[plane] = swap(cotangent, plane * inner)

    def send(kind, plane, flops, last):
        parts = ("rows", "cots") if kind == "both" else (kind,)
        onward = [other for other in planes if other ^ (other & -other) == plane and plane]
        copied = []
        if onward and "rows" in parts:
            copied.append(packed[plane])
        if onward and "cots" in parts:
            copied.append(cots[plane])
        if kind == "rows":
            copied.append(cotangent)
        waiting = [other for other, what, where in late if (what, where) == (kind, plane)]
        if waiting:
            copied += [packed[0], cotangent]
        value = cots.get(plane, cotangent)
        sent, copies = select(ids, packed[plane], value, cap, top, parts, copied, flops, last)
        copies = list(copies)
        arrived[plane, kind] = swap_inner(sent)
        for part, held in (("rows", packed), ("cots", cots)):
            if onward and part in parts:
                copy = copies.pop(0)
                for other in onward:
                    held[other] = swap(copy, (other & -other) * inner)
        if kind == "rows":
            cots[plane] = swap(copies.pop(0), plane * inner)
        for other in waiting:
            packed[other] = swap(copies[0], other * inner)
            cots[other] = swap(copies[1], other * inner)
        return sent[0]

    last, weights, own, received, sums, results = None, None, None, None, None, None
    for kind, plane, size in chain:
        after = [] if last is None else [last]
        flops = 1 << size
        if kind in ("both", "rows", "cots"):
            last = send(kind, plane, flops, after)
        elif kind == "flip":
            weights = flip(weight_gate, weight_up, weight_down, flops, last)
            last = weights[3]
        elif kind == "begin":
            begun[plane] = begin(arrived[plane, "rows"], weights, flops, after)
            last = begun[plane][1]
        elif kind == "expert":
            pieces = arrived[plane, "cots" if plane in begun else "both"]
            pair_cot, saved[plane] = expert(pieces, weights, begun.get(plane, []), flops, after)
            returned[plane] = swap_inner(pair_cot)
            last = pair_cot[0]
        elif kind == "own":
            own = last = expand(ids, packed[0], returned[0], top, F32, flops, last)
        elif kind == "expand":
            last = expand(ids, packed[plane], returned[plane], top, BF16, flops, last)
            partial.append(swap(last, plane * inner))
        elif kind == "total":
            own = last = total(own, partial[:plane], F32, flops, last)
            del partial[:plane]
        elif kind == "lend":
            last = lend(ids, [saved[other] for other in planes], flops, last)
            received = lax.ppermute(last, "dp", [(0, 1), (1, 0)])
        elif kind == "share":
            sums = share(ids, [saved[other] for other in planes], flops, last)
            last = sums[1]
        elif kind == "finish":
            *results, last = finish(sums, received, flops, last)
    input_grad = total(own, partial, BF16, 1, last)
    return (input_grad, *(value[None] for value in results))


def solution(mesh):
    return jax.shard_map(
        local,
        mesh=mesh,
        in_specs=(
            P(("dp", "expert"), None),
            P(("dp", "expert"), None),
            P(("dp", "expert"), None),
            P(("dp", "expert"), None),
            P("expert", None, None),
            P("expert", None, None),
            P("expert", None, None),
        ),
        out_specs=(
            P(("dp", "expert"), None),
            P("expert", "dp", None),
            P("expert", "dp", None),
            P("expert", "dp", None),
        ),
        check_vma=False,
    )
```

```python
import functools

import jax
import jax.numpy as jnp
from jax import lax
from jax.experimental import pallas as pl
from jax.experimental.pallas import tpu as pltpu
from jax.sharding import PartitionSpec as P

BF16 = jnp.bfloat16
F32 = jnp.float32
META = 16
PARAMS = pltpu.CompilerParams(vmem_limit_bytes=8 << 20)
LARGE = pltpu.CompilerParams(vmem_limit_bytes=18 << 20)
VMEM = pl.BlockSpec(memory_space=pltpu.VMEM)
SMEM = pl.BlockSpec(memory_space=pltpu.SMEM)
ANYWHERE = pl.BlockSpec(memory_space=pl.ANY)
HBM = pl.BlockSpec(memory_space=pltpu.HBM)


def estimate(flops):
    return pl.CostEstimate(flops=flops, transcendentals=0, bytes_accessed=1)


def dot(left, right, dims=((1,), (0,))):
    return lax.dot_general(left, right, (dims, ((), ())), preferred_element_type=F32)


def array(shape, dtype=BF16):
    return jax.ShapeDtypeStruct(shape, dtype)


def in_hbm(*values):
    return [pltpu.with_memory_space_constraint(value, pltpu.HBM) for value in values]


def in_vmem(*values):
    return [pltpu.with_memory_space_constraint(value, pltpu.VMEM) for value in values]


def resident(*shape, dtype=BF16):
    return pltpu.VMEM(shape, dtype)


def pack_kernel(in_ref, experts_ref, mixing_ref, out_ref, block_ref, sems):
    tokens, model = in_ref.shape
    rows = pltpu.make_async_copy(in_ref, out_ref.at[:tokens], sems.at[0])
    rows.start()
    mixing = mixing_ref[...]
    high = mixing.astype(BF16).astype(F32)
    middle = (mixing - high).astype(BF16).astype(F32)
    low = mixing - high - middle
    block = [experts_ref[...].astype(F32), high, middle, low]
    if META > 4 * mixing.shape[0]:
        block.append(jnp.zeros((META - 4 * mixing.shape[0], tokens), F32))
    block_ref[:, :tokens] = jnp.concatenate(block, axis=0).astype(BF16)
    block_ref[:, tokens:] = jnp.zeros((META, model - tokens), BF16)
    routing = pltpu.make_async_copy(block_ref, out_ref.at[tokens:], sems.at[1])
    routing.start()
    rows.wait()
    routing.wait()


def pack(tokens, experts, mixing, flops=1):
    rows, model = tokens.shape
    return pl.pallas_call(
        pack_kernel,
        out_shape=array((rows + META, model)),
        in_specs=[HBM, VMEM, VMEM],
        out_specs=HBM,
        scratch_shapes=[pltpu.VMEM((META, model), BF16), pltpu.SemaphoreType.DMA((2,))],
        compiler_params=PARAMS,
        cost_estimate=estimate(flops),
        name="pack",
    )(*in_hbm(tokens), experts.T, mixing.T)


def slot_masks(ids_ref, block, count, cap, top):
    block = block.astype(F32)
    chosen, high, middle, low = (block[top * part : top * (part + 1)] for part in range(4))
    mixing = (high + middle) + low
    tokens = chosen.shape[1]
    earlier = lax.broadcasted_iota(jnp.int32, (tokens, tokens), 0)
    later = lax.broadcasted_iota(jnp.int32, (tokens, tokens), 1)
    before = (earlier < later).astype(F32)
    slot = lax.broadcasted_iota(jnp.int32, (cap, tokens), 0).astype(F32)
    named, weights = [], []
    for which in range(count):
        hit = chosen == ids_ref[which].astype(F32)
        named.append(jnp.sum(jnp.where(hit, 1.0, 0.0), axis=0, keepdims=True))
        weights.append(jnp.sum(jnp.where(hit, mixing, 0.0), axis=0, keepdims=True))
    position = dot(jnp.concatenate(named, axis=0), before)
    onehot, slot_weight = [], []
    for which in range(count):
        here = (slot == position[which : which + 1]) & (named[which] > 0.5)
        onehot.append(jnp.where(here, 1.0, 0.0))
        slot_weight.append(jnp.sum(jnp.where(here, weights[which], 0.0), axis=1, keepdims=True))
    return jnp.concatenate(onehot, axis=0), jnp.concatenate(slot_weight, axis=0)


def select_kernel(count, cap, top, parts, copied, ids_ref, *refs):
    packed_ref, cots_ref = refs[:2]
    sources = refs[2 : 2 + copied]
    targets, sems = refs[-1 - copied : -1], refs[-1]
    outs = refs[-1 - copied - count : -1 - copied]
    copies = [
        pltpu.make_async_copy(source, target, sems.at[which])
        for which, (source, target) in enumerate(zip(sources, targets))
    ]
    for copy in copies:
        copy.start()
    model = packed_ref.shape[1]
    tokens = packed_ref.shape[0] - META
    masks, weight = slot_masks(ids_ref, packed_ref[tokens:, :tokens], count, cap, top)
    onehot = masks.astype(BF16)
    step = min(512, model)
    for start in range(0, model, step):
        columns = slice(start, start + step)
        for place, part in enumerate(parts):
            if part == "rows":
                value = dot(onehot, packed_ref[:tokens, columns])
            else:
                value = dot(onehot, cots_ref[:, columns]) * weight
            value = value.astype(BF16)
            for which in range(count):
                outs[which][place, :, columns] = value[which * cap : (which + 1) * cap]
    for copy in copies:
        copy.wait()


def select(ids, packed, cots, cap, top, parts, copied, flops, after):
    count = ids.shape[0] - 2
    model = packed.shape[1]
    result = pl.pallas_call(
        functools.partial(select_kernel, count, cap, top, parts, len(copied)),
        out_shape=[array((len(parts), cap, model))] * count
        + [array(value.shape) for value in copied],
        in_specs=[SMEM, VMEM, VMEM if "cots" in parts else ANYWHERE]
        + [ANYWHERE] * (len(copied) + len(after)),
        out_specs=[VMEM] * count + [HBM] * len(copied),
        scratch_shapes=[pltpu.SemaphoreType.DMA((max(1, len(copied)),))],
        compiler_params=PARAMS,
        cost_estimate=estimate(flops),
        name="select",
    )(ids, packed, cots, *copied, *after)
    return result[:count], result[count:]


def flip_kernel(gate_in, up_in, down_in, _, gate_ref, up_ref, both_ref, flipped_ref, down, sems):
    copies = [
        pltpu.make_async_copy(source, target, sems.at[which])
        for which, (source, target) in enumerate(
            ((gate_in, gate_ref), (up_in, up_ref), (down_in, down))
        )
    ]
    for copy in copies:
        copy.start()
    model, units = gate_ref.shape
    step = min(512, model)
    for which, source in enumerate((gate_ref, up_ref)):
        copies[which].wait()
        for start in range(0, model, step):
            both_ref[which * units : (which + 1) * units, start : start + step] = source[
                start : start + step, :
            ].T
    copies[2].wait()
    for start in range(0, model, step):
        flipped_ref[start : start + step, :] = down[:, start : start + step].T


def flip(weight_gate, weight_up, weight_down, flops, after):
    model, units = weight_gate.shape
    return pl.pallas_call(
        flip_kernel,
        in_specs=[HBM] * 3 + [ANYWHERE],
        out_specs=[VMEM] * 4,
        out_shape=[
            resident(model, units),
            resident(model, units),
            resident(2 * units, model),
            resident(model, units),
        ],
        scratch_shapes=[pltpu.VMEM((units, model), BF16), pltpu.SemaphoreType.DMA((3,))],
        compiler_params=PARAMS,
        cost_estimate=estimate(flops),
        name="flip",
    )(*in_hbm(weight_gate, weight_up, weight_down), after)


def begin_kernel(count, *refs):
    ins = refs[:count]
    gate_ref, up_ref = refs[count : count + 2]
    rows_ref, pre_gate_ref, pre_up_ref = refs[-3:]
    cap = ins[0].shape[1]
    for which in range(count):
        rows_ref[which * cap : (which + 1) * cap, :] = ins[which][0]
    pre_gate_ref[...] = dot(rows_ref[...], gate_ref[...])
    pre_up_ref[...] = dot(rows_ref[...], up_ref[...])


def begin(arrived, weights, flops, after):
    count = len(arrived)
    _, cap, model = arrived[0].shape
    units = weights[0].shape[1]
    rows = count * cap
    return pl.pallas_call(
        functools.partial(begin_kernel, count),
        in_specs=[VMEM] * (count + 2) + [ANYWHERE] * len(after),
        out_specs=[VMEM] * 3,
        out_shape=[resident(rows, model)] + [resident(rows, units, dtype=F32)] * 2,
        compiler_params=PARAMS,
        cost_estimate=estimate(flops),
        name="begin",
    )(*arrived, *in_vmem(*weights[:2]), *after)


def expert_kernel(count, begun, *refs):
    ins = refs[:count]
    gate_ref, up_ref, both_ref, flipped_ref = refs[count : count + 4]
    cap = ins[0].shape[1]
    model, units = gate_ref.shape
    if begun:
        pre_gate_ref, pre_up_ref = refs[count + 4 : count + 6]
        outs, (cots_ref, pair_units_ref, hidden_ref) = refs[-count - 3 : -3], refs[-3:]
    else:
        outs = refs[-count - 4 : -4]
        rows_ref, cots_ref, pair_units_ref, hidden_ref = refs[-4:]
    for which in range(count):
        part = slice(which * cap, (which + 1) * cap)
        if not begun:
            rows_ref[part, :] = ins[which][0]
        cots_ref[part, :] = ins[which][0 if begun else 1]
    block = min(256, units)
    for start in range(0, units, block):
        columns = slice(start, start + block)
        if begun:
            pre_gate, pre_up = pre_gate_ref[:, columns], pre_up_ref[:, columns]
        else:
            pre_gate = dot(rows_ref[...], gate_ref[:, columns])
            pre_up = dot(rows_ref[...], up_ref[:, columns])
        hidden_cot = dot(cots_ref[...], flipped_ref[:, columns])
        sigmoid_gate = jax.nn.sigmoid(pre_gate)
        activated = pre_gate * sigmoid_gate
        hidden_ref[:, columns] = (activated * pre_up).astype(BF16)
        pair_units_ref[:, columns] = (
            hidden_cot * pre_up * sigmoid_gate * (1.0 + pre_gate * (1.0 - sigmoid_gate))
        ).astype(BF16)
        pair_units_ref[:, units + start : units + start + block] = (
            hidden_cot * activated
        ).astype(BF16)
    block = min(512, model)
    for start in range(0, model, block):
        columns = slice(start, start + block)
        pair_cot = dot(pair_units_ref[...], both_ref[:, columns]).astype(BF16)
        for which in range(count):
            outs[which][:, columns] = pair_cot[which * cap : (which + 1) * cap]


def expert(arrived, weights, begun, flops, after):
    count = len(arrived)
    _, cap, model = arrived[0].shape
    units = weights[0].shape[1]
    rows = count * cap
    kept = [resident(rows, model)] * (1 if begun else 2)
    kept += [resident(rows, 2 * units), resident(rows, units)]
    result = pl.pallas_call(
        functools.partial(expert_kernel, count, bool(begun)),
        in_specs=[VMEM] * (count + 4 + len(begun[1:])) + [ANYWHERE] * len(after),
        out_specs=[VMEM] * (count + len(kept)),
        out_shape=[array((cap, model))] * count + kept,
        compiler_params=PARAMS,
        cost_estimate=estimate(flops),
        name="expert",
    )(*arrived, *in_vmem(*weights, *begun[1:]), *after)
    return result[:count], list(begun[:1]) + list(result[count:])


STEPS = 4


def lend_kernel(planes, ids_ref, *refs):
    saved = [refs[4 * which : 4 * which + 4] for which in range(planes)]
    sent_out, sent_ref, sems = refs[-3:]
    model, units = saved[0][0].shape[1], saved[0][3].shape[1]
    half = ids_ref[ids_ref.shape[0] - 1]
    height, width = model // 2 // STEPS, model // STEPS
    rest = units // 2 - height
    fold = height // rest
    part = width // fold
    own_units = pl.ds(pl.multiple_of(half * (units // 2), 128), units // 2)
    flipped_hidden = jnp.concatenate([kept[3][:, own_units].T for kept in saved], axis=1)
    pair_units = jnp.concatenate([kept[2][...] for kept in saved], axis=0)
    copies = []
    for step in range(STEPS):
        at = slice(step * height, (step + 1) * height)
        across = slice(step * width, (step + 1) * width)
        own_rows = pl.ds(pl.multiple_of(half * (model // 2) + step * height, 128), height)
        flipped = jnp.concatenate([kept[0][:, own_rows].T for kept in saved], axis=1)
        both = dot(flipped, pair_units)
        down = dot(flipped_hidden, jnp.concatenate([kept[1][:, across] for kept in saved], axis=0))
        slot = step % 2
        if step >= 2:
            copies[step - 2].wait()
        sent_ref[slot, :, : 2 * units] = both.astype(BF16)
        down = down.astype(BF16)
        sent_ref[slot, :, 2 * units : 2 * units + width] = down[:height]
        for which in range(fold):
            lower = slice(which * rest, (which + 1) * rest)
            sent_ref[slot, lower, 2 * units + width :] = down[
                height:, which * part : (which + 1) * part
            ]
        copy = pltpu.make_async_copy(sent_ref.at[slot], sent_out.at[at], sems.at[slot])
        copy.start()
        copies.append(copy)
    for copy in copies[-2:]:
        copy.wait()


def lend(ids, saved, flops, after):
    model, units = saved[0][0].shape[1], saved[0][3].shape[1]
    height = model // 2 // STEPS
    return pl.pallas_call(
        functools.partial(lend_kernel, len(saved)),
        in_specs=[SMEM] + [VMEM] * (4 * len(saved)) + [ANYWHERE],
        out_specs=HBM,
        out_shape=array((model // 2, 3 * units)),
        scratch_shapes=[pltpu.VMEM((2, height, 3 * units), BF16), pltpu.SemaphoreType.DMA((2,))],
        compiler_params=LARGE,
        cost_estimate=estimate(flops),
        name="lend",
    )(ids, *in_vmem(*(part for kept in saved for part in kept)), after)


def share_kernel(planes, ids_ref, *refs):
    saved = [refs[4 * which : 4 * which + 4] for which in range(planes)]
    both_ref, down_ref = refs[-2:]
    model, units = saved[0][0].shape[1], saved[0][3].shape[1]
    half = ids_ref[ids_ref.shape[0] - 2]
    height, width = model // 2 // STEPS, model // STEPS
    own_units = pl.ds(pl.multiple_of(half * (units // 2), 128), units // 2)
    flipped_hidden = jnp.concatenate([kept[3][:, own_units].T for kept in saved], axis=1)
    pair_units = jnp.concatenate([kept[2][...] for kept in saved], axis=0)
    for step in range(STEPS):
        across = slice(step * width, (step + 1) * width)
        own_rows = pl.ds(pl.multiple_of(half * (model // 2) + step * height, 128), height)
        flipped = jnp.concatenate([kept[0][:, own_rows].T for kept in saved], axis=1)
        both_ref[step * height : (step + 1) * height, :] = dot(flipped, pair_units)
        down_ref[:, across] = dot(
            flipped_hidden, jnp.concatenate([kept[1][:, across] for kept in saved], axis=0)
        )


def share(ids, saved, flops, after):
    model, units = saved[0][0].shape[1], saved[0][3].shape[1]
    return pl.pallas_call(
        functools.partial(share_kernel, len(saved)),
        in_specs=[SMEM] + [VMEM] * (4 * len(saved)) + [ANYWHERE],
        out_specs=[VMEM] * 2,
        out_shape=[
            resident(model // 2, 2 * units, dtype=F32),
            resident(units // 2, model, dtype=F32),
        ],
        compiler_params=LARGE,
        cost_estimate=estimate(flops),
        name="share",
    )(ids, *in_vmem(*(part for kept in saved for part in kept)), after)


def finish_kernel(
    both_ref, down_ref, other, _, gate_out, up_out, down_out, token, gate_ref, up_ref, own_ref, sems
):
    model, units = down_ref.shape[1], down_ref.shape[0] * 2
    height, width = model // 2 // STEPS, model // STEPS
    rest = units // 2 - height
    fold = height // rest
    part = width // fold
    token[...] = jnp.zeros(token.shape, F32)
    copies = []
    for step in range(STEPS):
        at = slice(step * height, (step + 1) * height)
        across = slice(step * width, (step + 1) * width)
        both = both_ref[at, :] + other[at, : 2 * units].astype(F32)
        gate_ref[at, :] = both[:, :units]
        up_ref[at, :] = both[:, units:]
        own_ref[:height, across] = down_ref[:height, across] + other[
            at, 2 * units : 2 * units + width
        ].astype(F32)
        for which in range(fold):
            lower = slice(step * height + which * rest, step * height + (which + 1) * rest)
            target = slice(step * width + which * part, step * width + (which + 1) * part)
            own_ref[height:, target] = down_ref[height:, target] + other[
                lower, 2 * units + width :
            ].astype(F32)
        moves = (
            (gate_ref.at[at], gate_out.at[at]),
            (up_ref.at[at], up_out.at[at]),
            (own_ref.at[:, across], down_out.at[:, across]),
        )
        for which, (source, target) in enumerate(moves):
            copy = pltpu.make_async_copy(source, target, sems.at[step, which])
            copy.start()
            copies.append(copy)
    for copy in copies:
        copy.wait()


def finish(sums, received, flops, after):
    model, units = sums[1].shape[1], sums[1].shape[0] * 2
    shapes = [(model // 2, units), (model // 2, units), (units // 2, model)]
    return pl.pallas_call(
        finish_kernel,
        in_specs=[VMEM] * 3 + [ANYWHERE],
        out_specs=[HBM] * 3 + [VMEM],
        out_shape=[array(shape, F32) for shape in shapes] + [array((8, 128), F32)],
        scratch_shapes=[pltpu.VMEM(shape, F32) for shape in shapes]
        + [pltpu.SemaphoreType.DMA((STEPS, 3))],
        compiler_params=LARGE,
        cost_estimate=estimate(flops),
        name="finish",
    )(*in_vmem(*sums), received, after)


def expand_kernel(count, top, ids_ref, meta_ref, *refs):
    back, out = refs[:count], refs[-1]
    cap, model = back[0].shape
    onehot, _ = slot_masks(ids_ref, meta_ref[...], count, cap, top)
    spread = onehot.T.astype(BF16)
    step = min(512, model)
    for start in range(0, model, step):
        columns = slice(start, start + step)
        value = dot(spread, jnp.concatenate([ref[:, columns] for ref in back], axis=0))
        out[:, columns] = value.astype(out.dtype)


def expand(ids, packed, back, top, dtype, flops, after):
    count = len(back)
    cap, model = back[0].shape
    tokens = packed.shape[0] - META
    whole = lambda *shape: pl.BlockSpec(shape, lambda s: (0, 0))
    return pl.pallas_call(
        functools.partial(expand_kernel, count, top),
        grid=(1,),
        out_shape=array((tokens, model), dtype),
        in_specs=[SMEM, pl.BlockSpec((META, tokens), lambda s: (tokens // META, 0))]
        + [whole(cap, model)] * count
        + [ANYWHERE],
        out_specs=whole(tokens, model),
        compiler_params=PARAMS,
        cost_estimate=estimate(flops),
        name="expand",
    )(ids, packed, *back, after)


def total_kernel(count, own_ref, *refs):
    value = own_ref[...]
    for ref in refs[:count]:
        value = value + ref[...].astype(F32)
    refs[-1][...] = value.astype(refs[-1].dtype)


def total(own, others, dtype, flops, after):
    return pl.pallas_call(
        functools.partial(total_kernel, len(others)),
        out_shape=array(own.shape, dtype),
        in_specs=[VMEM] * (1 + len(others)) + [ANYWHERE],
        out_specs=VMEM,
        compiler_params=PARAMS,
        cost_estimate=estimate(flops),
        name="total",
    )(own, *others, after)


FOUR_PLANES = (
    ("both", 0, 31),
    ("flip", 0, 0),
    ("rows", 2, 0),
    ("expert", 0, 0),
    ("begin", 2, 34),
    ("cots", 2, 0),
    ("own", 0, 32),
    ("both", 3, 0),
    ("expert", 2, 29),
    ("expert", 3, 0),
    ("both", 1, 28),
    ("expand", 2, 28),
    ("expand", 3, 0),
    ("expert", 1, 0),
    ("total", 1, 0),
    ("lend", 0, 37),
    ("expand", 1, 37),
    ("share", 0, 30),
    ("finish", 0, 0),
    ("total", 1, 0),
)
LATE = ()


def many_planes(outer):
    order = list(range(2, outer)) + [1]
    chain = [("both", 0, 0), ("flip", 0, 0), ("expert", 0, 0), ("own", 0, 0)]
    for plane in order:
        chain += [("both", plane, 0), ("expert", plane, 0)]
        chain += [("expand", plane, 0)]
    return chain + [("lend", 0, 0), ("share", 0, 0), ("finish", 0, 0)]


def local(tokens, cotangent, experts, mixing, gate_matrix, up_matrix, down_matrix):
    expert_count = lax.axis_size("expert")
    inner = min(4, expert_count)
    outer = expert_count // inner
    tok_rows, top = experts.shape
    cap = 2 * tok_rows * top // expert_count
    weight_gate, weight_up, weight_down = gate_matrix[0], up_matrix[0], down_matrix[0]

    def swap(value, mask):
        pairs = [(device, device ^ mask) for device in range(expert_count)]
        return lax.ppermute(value, "expert", pairs)

    def swap_inner(values):
        return [values[0]] + [swap(values[which], which) for which in range(1, inner)]

    core = lax.axis_index("dp").astype(jnp.int32)
    plane_ids = jnp.bitwise_xor(lax.axis_index("expert").astype(jnp.int32), jnp.arange(inner, dtype=jnp.int32))
    ids = jnp.concatenate([plane_ids, jnp.stack([core, 1 - core])])
    chain = FOUR_PLANES if outer == 4 else many_planes(outer)
    planes = [plane for kind, plane, _ in chain if kind == "expert"]
    packed = {0: pack(tokens, experts, mixing)}
    cots = {0: cotangent}
    arrived, returned, partial, saved, begun = {}, {}, [], {}, {}
    late = LATE if outer == 4 else ()
    late_planes = [plane for plane, _, _ in late]
    split = [plane for kind, plane, _ in chain if kind == "rows"]
    for plane in planes[1:]:
        if plane == plane & -plane and plane not in late_planes:
            packed[plane] = swap(packed[0], plane * inner)
            if plane not in split:
                cots[plane] = swap(cotangent, plane * inner)

    def send(kind, plane, flops, last):
        parts = ("rows", "cots") if kind == "both" else (kind,)
        onward = [other for other in planes if other ^ (other & -other) == plane and plane]
        copied = []
        if onward and "rows" in parts:
            copied.append(packed[plane])
        if onward and "cots" in parts:
            copied.append(cots[plane])
        direct = kind == "rows" and plane == plane & -plane
        if direct:
            copied.append(cotangent)
        waiting = [other for other, what, where in late if (what, where) == (kind, plane)]
        if waiting:
            copied += [packed[0], cotangent]
        value = cots.get(plane, cotangent)
        sent, copies = select(ids, packed[plane], value, cap, top, parts, copied, flops, last)
        copies = list(copies)
        arrived[plane, kind] = swap_inner(sent)
        for part, held in (("rows", packed), ("cots", cots)):
            if onward and part in parts:
                copy = copies.pop(0)
                for other in onward:
                    held[other] = swap(copy, (other & -other) * inner)
        if direct:
            cots[plane] = swap(copies.pop(0), plane * inner)
        for other in waiting:
            packed[other] = swap(copies[0], other * inner)
            cots[other] = swap(copies[1], other * inner)
        return sent[0]

    last, weights, own, received, sums, results = None, None, None, None, None, None
    for kind, plane, size in chain:
        after = [] if last is None else [last]
        flops = 1 << size
        if kind in ("both", "rows", "cots"):
            last = send(kind, plane, flops, after)
        elif kind == "flip":
            weights = flip(weight_gate, weight_up, weight_down, flops, last)
            last = weights[3]
        elif kind == "begin":
            begun[plane] = begin(arrived[plane, "rows"], weights, flops, after)
            last = begun[plane][1]
        elif kind == "expert":
            pieces = arrived[plane, "cots" if plane in begun else "both"]
            pair_cot, saved[plane] = expert(pieces, weights, begun.get(plane, []), flops, after)
            returned[plane] = swap_inner(pair_cot)
            last = pair_cot[0]
        elif kind == "own":
            own = last = expand(ids, packed[0], returned[0], top, F32, flops, last)
        elif kind == "expand":
            last = expand(ids, packed[plane], returned[plane], top, BF16, flops, last)
            partial.append(swap(last, plane * inner))
        elif kind == "total":
            own = last = total(own, partial[:plane], F32, flops, last)
            del partial[:plane]
        elif kind == "lend":
            last = lend(ids, [saved[other] for other in planes], flops, last)
            received = lax.ppermute(last, "dp", [(0, 1), (1, 0)])
        elif kind == "share":
            sums = share(ids, [saved[other] for other in planes], flops, last)
            last = sums[1]
        elif kind == "finish":
            *results, last = finish(sums, received, flops, last)
    input_grad = total(own, partial, BF16, 1, last)
    return (input_grad, *(value[None] for value in results))


def solution(mesh):
    return jax.shard_map(
        local,
        mesh=mesh,
        in_specs=(
            P(("dp", "expert"), None),
            P(("dp", "expert"), None),
            P(("dp", "expert"), None),
            P(("dp", "expert"), None),
            P("expert", None, None),
            P("expert", None, None),
            P("expert", None, None),
        ),
        out_specs=(
            P(("dp", "expert"), None),
            P("expert", "dp", None),
            P("expert", "dp", None),
            P("expert", "dp", None),
        ),
        check_vma=False,
    )
```

```python
import functools

import jax
import jax.numpy as jnp
from jax import lax
from jax.experimental import pallas as pl
from jax.experimental.pallas import tpu as pltpu
from jax.sharding import PartitionSpec as P

BF16 = jnp.bfloat16
F32 = jnp.float32
META = 16
PARAMS = pltpu.CompilerParams(vmem_limit_bytes=8 << 20)
LARGE = pltpu.CompilerParams(vmem_limit_bytes=18 << 20)
VMEM = pl.BlockSpec(memory_space=pltpu.VMEM)
SMEM = pl.BlockSpec(memory_space=pltpu.SMEM)
ANYWHERE = pl.BlockSpec(memory_space=pl.ANY)
HBM = pl.BlockSpec(memory_space=pltpu.HBM)


def estimate(flops):
    return pl.CostEstimate(flops=flops, transcendentals=0, bytes_accessed=1)


def dot(left, right, dims=((1,), (0,))):
    return lax.dot_general(left, right, (dims, ((), ())), preferred_element_type=F32)


def array(shape, dtype=BF16):
    return jax.ShapeDtypeStruct(shape, dtype)


def in_hbm(*values):
    return [pltpu.with_memory_space_constraint(value, pltpu.HBM) for value in values]


def in_vmem(*values):
    return [pltpu.with_memory_space_constraint(value, pltpu.VMEM) for value in values]


def resident(*shape, dtype=BF16):
    return pltpu.VMEM(shape, dtype)


def pack_kernel(in_ref, experts_ref, mixing_ref, out_ref, meta_ref, block_ref, sems):
    tokens, model = in_ref.shape
    rows = pltpu.make_async_copy(in_ref, out_ref.at[:tokens], sems.at[0])
    rows.start()
    mixing = mixing_ref[...]
    high = mixing.astype(BF16).astype(F32)
    middle = (mixing - high).astype(BF16).astype(F32)
    low = mixing - high - middle
    block = [experts_ref[...].astype(F32), high, middle, low]
    if META > 4 * mixing.shape[0]:
        block.append(jnp.zeros((META - 4 * mixing.shape[0], tokens), F32))
    block_ref[:, :tokens] = jnp.concatenate(block, axis=0).astype(BF16)
    meta_ref[...] = block_ref[:, :tokens]
    block_ref[:, tokens:] = jnp.zeros((META, model - tokens), BF16)
    routing = pltpu.make_async_copy(block_ref, out_ref.at[tokens:], sems.at[1])
    routing.start()
    rows.wait()
    routing.wait()


def pack(tokens, experts, mixing, flops=1):
    rows, model = tokens.shape
    return pl.pallas_call(
        pack_kernel,
        out_shape=[array((rows + META, model)), array((META, rows))],
        in_specs=[HBM, VMEM, VMEM],
        out_specs=[HBM, VMEM],
        scratch_shapes=[pltpu.VMEM((META, model), BF16), pltpu.SemaphoreType.DMA((2,))],
        compiler_params=PARAMS,
        cost_estimate=estimate(flops),
        name="pack",
    )(*in_hbm(tokens), experts.T, mixing.T)


def slot_masks(ids_ref, block, count, cap, top):
    block = block.astype(F32)
    chosen, high, middle, low = (block[top * part : top * (part + 1)] for part in range(4))
    mixing = (high + middle) + low
    tokens = chosen.shape[1]
    earlier = lax.broadcasted_iota(jnp.int32, (tokens, tokens), 0)
    later = lax.broadcasted_iota(jnp.int32, (tokens, tokens), 1)
    before = (earlier < later).astype(F32)
    slot = lax.broadcasted_iota(jnp.int32, (cap, tokens), 0).astype(F32)
    named, weights = [], []
    for which in range(count):
        hit = chosen == ids_ref[which].astype(F32)
        named.append(jnp.sum(jnp.where(hit, 1.0, 0.0), axis=0, keepdims=True))
        weights.append(jnp.sum(jnp.where(hit, mixing, 0.0), axis=0, keepdims=True))
    position = dot(jnp.concatenate(named, axis=0), before)
    onehot, slot_weight = [], []
    for which in range(count):
        here = (slot == position[which : which + 1]) & (named[which] > 0.5)
        onehot.append(jnp.where(here, 1.0, 0.0))
        slot_weight.append(jnp.sum(jnp.where(here, weights[which], 0.0), axis=1, keepdims=True))
    return jnp.concatenate(onehot, axis=0), jnp.concatenate(slot_weight, axis=0)


def select_kernel(count, cap, top, parts, copied, join, ids_ref, *refs):
    packed_ref, cots_ref, meta_ref = refs[:3]
    sources = list(refs[3 : 3 + copied])
    targets, sems = list(refs[-1 - copied : -1]), refs[-1]
    if join:
        rows, width = sources[0].shape
        whole = targets[0]
        targets[0] = whole.at[:rows]
        sources.append(meta_ref)
        targets.append(whole.at[rows:, : meta_ref.shape[1]])
    outs = refs[-1 - copied - count : -1 - copied]
    copies = [
        pltpu.make_async_copy(source, target, sems.at[which])
        for which, (source, target) in enumerate(zip(sources, targets))
    ]
    for copy in copies:
        copy.start()
    model = packed_ref.shape[1]
    tokens = meta_ref.shape[1] if meta_ref.shape[0] == META else packed_ref.shape[0] - META
    block = meta_ref[...] if meta_ref.shape[0] == META else packed_ref[tokens:, :tokens]
    masks, weight = slot_masks(ids_ref, block, count, cap, top)
    onehot = masks.astype(BF16)
    step = min(512, model)
    for start in range(0, model, step):
        columns = slice(start, start + step)
        for place, part in enumerate(parts):
            if part == "rows":
                value = dot(onehot, packed_ref[:tokens, columns])
            else:
                value = dot(onehot, cots_ref[:, columns]) * weight
            value = value.astype(BF16)
            for which in range(count):
                outs[which][place, :, columns] = value[which * cap : (which + 1) * cap]
    for copy in copies:
        copy.wait()


def select(ids, packed, cots, meta, cap, top, parts, copied, join, flops, after):
    count = ids.shape[0] - 2
    model = packed.shape[1]
    result = pl.pallas_call(
        functools.partial(select_kernel, count, cap, top, parts, len(copied), join),
        out_shape=[array((len(parts), cap, model))] * count
        + [
            array((value.shape[0] + META * (join and which == 0), value.shape[1]))
            for which, value in enumerate(copied)
        ],
        in_specs=[SMEM, VMEM if "rows" in parts or meta is None else ANYWHERE]
        + [VMEM if "cots" in parts else ANYWHERE, ANYWHERE if meta is None else VMEM]
        + [ANYWHERE] * (len(copied) + len(after)),
        out_specs=[VMEM] * count + [HBM] * len(copied),
        scratch_shapes=[pltpu.SemaphoreType.DMA((1 + len(copied),))],
        compiler_params=PARAMS,
        cost_estimate=estimate(flops),
        name="select",
    )(ids, packed, cots, packed if meta is None else meta, *copied, *after)
    return result[:count], result[count:]


def flip_kernel(gate_in, up_in, down_in, _, gate_ref, up_ref, both_ref, flipped_ref, down, sems):
    copies = [
        pltpu.make_async_copy(source, target, sems.at[which])
        for which, (source, target) in enumerate(
            ((gate_in, gate_ref), (up_in, up_ref), (down_in, down))
        )
    ]
    for copy in copies:
        copy.start()
    model, units = gate_ref.shape
    step = min(512, model)
    for which, source in enumerate((gate_ref, up_ref)):
        copies[which].wait()
        for start in range(0, model, step):
            both_ref[which * units : (which + 1) * units, start : start + step] = source[
                start : start + step, :
            ].T
    copies[2].wait()
    for start in range(0, model, step):
        flipped_ref[start : start + step, :] = down[:, start : start + step].T


def flip(weight_gate, weight_up, weight_down, flops, after):
    model, units = weight_gate.shape
    return pl.pallas_call(
        flip_kernel,
        in_specs=[HBM] * 3 + [ANYWHERE],
        out_specs=[VMEM] * 4,
        out_shape=[
            resident(model, units),
            resident(model, units),
            resident(2 * units, model),
            resident(model, units),
        ],
        scratch_shapes=[pltpu.VMEM((units, model), BF16), pltpu.SemaphoreType.DMA((3,))],
        compiler_params=PARAMS,
        cost_estimate=estimate(flops),
        name="flip",
    )(*in_hbm(weight_gate, weight_up, weight_down), after)


def begin_kernel(count, *refs):
    ins = refs[:count]
    gate_ref, up_ref = refs[count : count + 2]
    rows_ref, pre_gate_ref, pre_up_ref = refs[-3:]
    cap = ins[0].shape[1]
    for which in range(count):
        rows_ref[which * cap : (which + 1) * cap, :] = ins[which][0]
    pre_gate_ref[...] = dot(rows_ref[...], gate_ref[...])
    pre_up_ref[...] = dot(rows_ref[...], up_ref[...])


def begin(arrived, weights, flops, after):
    count = len(arrived)
    _, cap, model = arrived[0].shape
    units = weights[0].shape[1]
    rows = count * cap
    return pl.pallas_call(
        functools.partial(begin_kernel, count),
        in_specs=[VMEM] * (count + 2) + [ANYWHERE] * len(after),
        out_specs=[VMEM] * 3,
        out_shape=[resident(rows, model)] + [resident(rows, units, dtype=F32)] * 2,
        compiler_params=PARAMS,
        cost_estimate=estimate(flops),
        name="begin",
    )(*arrived, *in_vmem(*weights[:2]), *after)


def expert_kernel(count, begun, *refs):
    ins = refs[:count]
    gate_ref, up_ref, both_ref, flipped_ref = refs[count : count + 4]
    cap = ins[0].shape[1]
    model, units = gate_ref.shape
    if begun:
        pre_gate_ref, pre_up_ref = refs[count + 4 : count + 6]
        outs, (cots_ref, pair_units_ref, hidden_ref) = refs[-count - 3 : -3], refs[-3:]
    else:
        outs = refs[-count - 4 : -4]
        rows_ref, cots_ref, pair_units_ref, hidden_ref = refs[-4:]
    for which in range(count):
        part = slice(which * cap, (which + 1) * cap)
        if not begun:
            rows_ref[part, :] = ins[which][0]
        cots_ref[part, :] = ins[which][0 if begun else 1]
    block = min(256, units)
    for start in range(0, units, block):
        columns = slice(start, start + block)
        if begun:
            pre_gate, pre_up = pre_gate_ref[:, columns], pre_up_ref[:, columns]
        else:
            pre_gate = dot(rows_ref[...], gate_ref[:, columns])
            pre_up = dot(rows_ref[...], up_ref[:, columns])
        hidden_cot = dot(cots_ref[...], flipped_ref[:, columns])
        sigmoid_gate = jax.nn.sigmoid(pre_gate)
        activated = pre_gate * sigmoid_gate
        hidden_ref[:, columns] = (activated * pre_up).astype(BF16)
        pair_units_ref[:, columns] = (
            hidden_cot * pre_up * sigmoid_gate * (1.0 + pre_gate * (1.0 - sigmoid_gate))
        ).astype(BF16)
        pair_units_ref[:, units + start : units + start + block] = (
            hidden_cot * activated
        ).astype(BF16)
    block = min(512, model)
    for start in range(0, model, block):
        columns = slice(start, start + block)
        pair_cot = dot(pair_units_ref[...], both_ref[:, columns]).astype(BF16)
        for which in range(count):
            outs[which][:, columns] = pair_cot[which * cap : (which + 1) * cap]


def expert(arrived, weights, begun, flops, after):
    count = len(arrived)
    _, cap, model = arrived[0].shape
    units = weights[0].shape[1]
    rows = count * cap
    kept = [resident(rows, model)] * (1 if begun else 2)
    kept += [resident(rows, 2 * units), resident(rows, units)]
    result = pl.pallas_call(
        functools.partial(expert_kernel, count, bool(begun)),
        in_specs=[VMEM] * (count + 4 + len(begun[1:])) + [ANYWHERE] * len(after),
        out_specs=[VMEM] * (count + len(kept)),
        out_shape=[array((cap, model))] * count + kept,
        compiler_params=PARAMS,
        cost_estimate=estimate(flops),
        name="expert",
    )(*arrived, *in_vmem(*weights, *begun[1:]), *after)
    return result[:count], list(begun[:1]) + list(result[count:])


STEPS = 4


def lend_kernel(planes, ids_ref, *refs):
    saved = [refs[4 * which : 4 * which + 4] for which in range(planes)]
    sent_out, sent_ref, sems = refs[-3:]
    model, units = saved[0][0].shape[1], saved[0][3].shape[1]
    half = ids_ref[ids_ref.shape[0] - 1]
    height, width = model // 2 // STEPS, model // STEPS
    rest = units // 2 - height
    fold = height // rest
    part = width // fold
    own_units = pl.ds(pl.multiple_of(half * (units // 2), 128), units // 2)
    flipped_hidden = jnp.concatenate([kept[3][:, own_units].T for kept in saved], axis=1)
    pair_units = jnp.concatenate([kept[2][...] for kept in saved], axis=0)
    copies = []
    for step in range(STEPS):
        at = slice(step * height, (step + 1) * height)
        across = slice(step * width, (step + 1) * width)
        own_rows = pl.ds(pl.multiple_of(half * (model // 2) + step * height, 128), height)
        flipped = jnp.concatenate([kept[0][:, own_rows].T for kept in saved], axis=1)
        both = dot(flipped, pair_units)
        down = dot(flipped_hidden, jnp.concatenate([kept[1][:, across] for kept in saved], axis=0))
        slot = step % 2
        if step >= 2:
            copies[step - 2].wait()
        sent_ref[slot, :, : 2 * units] = both.astype(BF16)
        down = down.astype(BF16)
        sent_ref[slot, :, 2 * units : 2 * units + width] = down[:height]
        for which in range(fold):
            lower = slice(which * rest, (which + 1) * rest)
            sent_ref[slot, lower, 2 * units + width :] = down[
                height:, which * part : (which + 1) * part
            ]
        copy = pltpu.make_async_copy(sent_ref.at[slot], sent_out.at[at], sems.at[slot])
        copy.start()
        copies.append(copy)
    for copy in copies[-2:]:
        copy.wait()


def lend(ids, saved, flops, after):
    model, units = saved[0][0].shape[1], saved[0][3].shape[1]
    height = model // 2 // STEPS
    return pl.pallas_call(
        functools.partial(lend_kernel, len(saved)),
        in_specs=[SMEM] + [VMEM] * (4 * len(saved)) + [ANYWHERE],
        out_specs=HBM,
        out_shape=array((model // 2, 3 * units)),
        scratch_shapes=[pltpu.VMEM((2, height, 3 * units), BF16), pltpu.SemaphoreType.DMA((2,))],
        compiler_params=LARGE,
        cost_estimate=estimate(flops),
        name="lend",
    )(ids, *in_vmem(*(part for kept in saved for part in kept)), after)


def share_kernel(planes, ids_ref, *refs):
    saved = [refs[4 * which : 4 * which + 4] for which in range(planes)]
    both_ref, down_ref = refs[-2:]
    model, units = saved[0][0].shape[1], saved[0][3].shape[1]
    half = ids_ref[ids_ref.shape[0] - 2]
    height, width = model // 2 // STEPS, model // STEPS
    own_units = pl.ds(pl.multiple_of(half * (units // 2), 128), units // 2)
    flipped_hidden = jnp.concatenate([kept[3][:, own_units].T for kept in saved], axis=1)
    pair_units = jnp.concatenate([kept[2][...] for kept in saved], axis=0)
    for step in range(STEPS):
        across = slice(step * width, (step + 1) * width)
        own_rows = pl.ds(pl.multiple_of(half * (model // 2) + step * height, 128), height)
        flipped = jnp.concatenate([kept[0][:, own_rows].T for kept in saved], axis=1)
        both_ref[step * height : (step + 1) * height, :] = dot(flipped, pair_units)
        down_ref[:, across] = dot(
            flipped_hidden, jnp.concatenate([kept[1][:, across] for kept in saved], axis=0)
        )


def share(ids, saved, flops, after):
    model, units = saved[0][0].shape[1], saved[0][3].shape[1]
    return pl.pallas_call(
        functools.partial(share_kernel, len(saved)),
        in_specs=[SMEM] + [VMEM] * (4 * len(saved)) + [ANYWHERE],
        out_specs=[VMEM] * 2,
        out_shape=[
            resident(model // 2, 2 * units, dtype=F32),
            resident(units // 2, model, dtype=F32),
        ],
        compiler_params=LARGE,
        cost_estimate=estimate(flops),
        name="share",
    )(ids, *in_vmem(*(part for kept in saved for part in kept)), after)


def finish_kernel(
    both_ref, down_ref, other, _, gate_out, up_out, down_out, token, gate_ref, up_ref, own_ref, sems
):
    model, units = down_ref.shape[1], down_ref.shape[0] * 2
    height, width = model // 2 // STEPS, model // STEPS
    rest = units // 2 - height
    fold = height // rest
    part = width // fold
    token[...] = jnp.zeros(token.shape, F32)
    copies = []
    for step in range(STEPS):
        at = slice(step * height, (step + 1) * height)
        across = slice(step * width, (step + 1) * width)
        both = both_ref[at, :] + other[at, : 2 * units].astype(F32)
        gate_ref[at, :] = both[:, :units]
        up_ref[at, :] = both[:, units:]
        own_ref[:height, across] = down_ref[:height, across] + other[
            at, 2 * units : 2 * units + width
        ].astype(F32)
        for which in range(fold):
            lower = slice(step * height + which * rest, step * height + (which + 1) * rest)
            target = slice(step * width + which * part, step * width + (which + 1) * part)
            own_ref[height:, target] = down_ref[height:, target] + other[
                lower, 2 * units + width :
            ].astype(F32)
        moves = (
            (gate_ref.at[at], gate_out.at[at]),
            (up_ref.at[at], up_out.at[at]),
            (own_ref.at[:, across], down_out.at[:, across]),
        )
        for which, (source, target) in enumerate(moves):
            copy = pltpu.make_async_copy(source, target, sems.at[step, which])
            copy.start()
            copies.append(copy)
    for copy in copies:
        copy.wait()


def finish(sums, received, flops, after):
    model, units = sums[1].shape[1], sums[1].shape[0] * 2
    shapes = [(model // 2, units), (model // 2, units), (units // 2, model)]
    return pl.pallas_call(
        finish_kernel,
        in_specs=[VMEM] * 3 + [ANYWHERE],
        out_specs=[HBM] * 3 + [VMEM],
        out_shape=[array(shape, F32) for shape in shapes] + [array((8, 128), F32)],
        scratch_shapes=[pltpu.VMEM(shape, F32) for shape in shapes]
        + [pltpu.SemaphoreType.DMA((STEPS, 3))],
        compiler_params=LARGE,
        cost_estimate=estimate(flops),
        name="finish",
    )(*in_vmem(*sums), received, after)


def expand_kernel(count, top, ids_ref, meta_ref, *refs):
    back, out = refs[:count], refs[-1]
    cap, model = back[0].shape
    onehot, _ = slot_masks(ids_ref, meta_ref[...], count, cap, top)
    spread = onehot.T.astype(BF16)
    step = min(512, model)
    for start in range(0, model, step):
        columns = slice(start, start + step)
        value = dot(spread, jnp.concatenate([ref[:, columns] for ref in back], axis=0))
        out[:, columns] = value.astype(out.dtype)


def expand(ids, packed, meta, back, top, dtype, flops, after):
    count = len(back)
    cap, model = back[0].shape
    tokens = packed.shape[0] - META if meta is None else meta.shape[1]
    at = tokens // META if meta is None else 0
    whole = lambda *shape: pl.BlockSpec(shape, lambda s: (0, 0))
    return pl.pallas_call(
        functools.partial(expand_kernel, count, top),
        grid=(1,),
        out_shape=array((tokens, model), dtype),
        in_specs=[SMEM, pl.BlockSpec((META, tokens), lambda s: (at, 0))]
        + [whole(cap, model)] * count
        + [ANYWHERE],
        out_specs=whole(tokens, model),
        compiler_params=PARAMS,
        cost_estimate=estimate(flops),
        name="expand",
    )(ids, packed if meta is None else meta, *back, after)


def total_kernel(count, own_ref, *refs):
    value = own_ref[...]
    for ref in refs[:count]:
        value = value + ref[...].astype(F32)
    refs[-1][...] = value.astype(refs[-1].dtype)


def total(own, others, dtype, flops, after):
    return pl.pallas_call(
        functools.partial(total_kernel, len(others)),
        out_shape=array(own.shape, dtype),
        in_specs=[VMEM] * (1 + len(others)) + [ANYWHERE],
        out_specs=VMEM,
        compiler_params=PARAMS,
        cost_estimate=estimate(flops),
        name="total",
    )(own, *others, after)


FOUR_PLANES = (
    ("both", 0, 0),
    ("flip", 0, 0),
    ("rows", 2, 0),
    ("expert", 0, 0),
    ("begin", 2, 34),
    ("own", 0, 0),
    ("cots", 2, 0),
    ("both", 3, 0),
    ("expert", 2, 29),
    ("expert", 3, 0),
    ("both", 1, 0),
    ("expand", 2, 28),
    ("expand", 3, 0),
    ("total", 1, 0),
    ("expert", 1, 0),
    ("lend", 0, 37),
    ("expand", 1, 37),
    ("share", 0, 30),
    ("finish", 0, 0),
)
LATE = ()


def many_planes(outer):
    order = list(range(2, outer)) + [1]
    chain = [("both", 0, 0), ("flip", 0, 0), ("expert", 0, 0), ("own", 0, 0)]
    for plane in order:
        chain += [("both", plane, 0), ("expert", plane, 0)]
        chain += [("expand", plane, 0)]
    return chain + [("lend", 0, 0), ("share", 0, 0), ("finish", 0, 0)]


def local(tokens, cotangent, experts, mixing, gate_matrix, up_matrix, down_matrix):
    expert_count = lax.axis_size("expert")
    inner = min(4, expert_count)
    outer = expert_count // inner
    tok_rows, top = experts.shape
    cap = 2 * tok_rows * top // expert_count
    weight_gate, weight_up, weight_down = gate_matrix[0], up_matrix[0], down_matrix[0]

    def swap(value, mask):
        pairs = [(device, device ^ mask) for device in range(expert_count)]
        return lax.ppermute(value, "expert", pairs)

    def swap_inner(values):
        return [values[0]] + [swap(values[which], which) for which in range(1, inner)]

    core = lax.axis_index("dp").astype(jnp.int32)
    plane_ids = jnp.bitwise_xor(lax.axis_index("expert").astype(jnp.int32), jnp.arange(inner, dtype=jnp.int32))
    ids = jnp.concatenate([plane_ids, jnp.stack([core, 1 - core])])
    chain = FOUR_PLANES if outer == 4 else many_planes(outer)
    planes = [plane for kind, plane, _ in chain if kind == "expert"]
    first, routing = pack(tokens, experts, mixing)
    packed, metas = {0: first}, {}
    cots = {0: cotangent}
    arrived, returned, partial, saved, begun = {}, {}, [], {}, {}
    late = LATE if outer == 4 else ()
    late_planes = [plane for plane, _, _ in late]
    split = [plane for kind, plane, _ in chain if kind == "rows"]
    for plane in planes[1:]:
        if plane == plane & -plane and plane not in late_planes:
            if plane in split:
                packed[plane] = swap(tokens, plane * inner)
                metas[plane] = swap(routing, plane * inner)
            else:
                packed[plane] = swap(packed[0], plane * inner)
            if plane not in split:
                cots[plane] = swap(cotangent, plane * inner)

    def send(kind, plane, flops, last):
        parts = ("rows", "cots") if kind == "both" else (kind,)
        onward = [other for other in planes if other ^ (other & -other) == plane and plane]
        copied = []
        if onward and "rows" in parts:
            copied.append(packed[plane])
        if onward and "cots" in parts:
            copied.append(cots[plane])
        if kind == "rows":
            copied.append(cotangent)
        waiting = [other for other, what, where in late if (what, where) == (kind, plane)]
        if waiting:
            copied += [packed[0], cotangent]
        value = cots.get(plane, cotangent)
        meta = metas.get(plane)
        join = meta is not None and bool(onward) and "rows" in parts
        sent, copies = select(
            ids, packed[plane], value, meta, cap, top, parts, copied, join, flops, last
        )
        copies = list(copies)
        arrived[plane, kind] = swap_inner(sent)
        for part, held in (("rows", packed), ("cots", cots)):
            if onward and part in parts:
                copy = copies.pop(0)
                for other in onward:
                    held[other] = swap(copy, (other & -other) * inner)
        if kind == "rows":
            cots[plane] = swap(copies.pop(0), plane * inner)
        for other in waiting:
            packed[other] = swap(copies[0], other * inner)
            cots[other] = swap(copies[1], other * inner)
        return sent[0]

    last, weights, own, received, sums, results = None, None, None, None, None, None
    for kind, plane, size in chain:
        after = [] if last is None else [last]
        flops = 1 << size
        if kind in ("both", "rows", "cots"):
            last = send(kind, plane, flops, after)
        elif kind == "flip":
            weights = flip(weight_gate, weight_up, weight_down, flops, last)
            last = weights[3]
        elif kind == "begin":
            begun[plane] = begin(arrived[plane, "rows"], weights, flops, after)
            last = begun[plane][1]
        elif kind == "expert":
            pieces = arrived[plane, "cots" if plane in begun else "both"]
            pair_cot, saved[plane] = expert(pieces, weights, begun.get(plane, []), flops, after)
            returned[plane] = swap_inner(pair_cot)
            last = pair_cot[0]
        elif kind == "own":
            own = last = expand(ids, packed[0], None, returned[0], top, F32, flops, last)
        elif kind == "expand":
            last = expand(ids, packed[plane], metas.get(plane), returned[plane], top, BF16, flops, last)
            partial.append(swap(last, plane * inner))
        elif kind == "total":
            own = last = total(own, partial[:plane], F32, flops, last)
            del partial[:plane]
        elif kind == "lend":
            last = lend(ids, [saved[other] for other in planes], flops, last)
            received = lax.ppermute(last, "dp", [(0, 1), (1, 0)])
        elif kind == "share":
            sums = share(ids, [saved[other] for other in planes], flops, last)
            last = sums[1]
        elif kind == "finish":
            *results, last = finish(sums, received, flops, last)
    input_grad = total(own, partial, BF16, 1, last)
    return (input_grad, *(value[None] for value in results))


def solution(mesh):
    return jax.shard_map(
        local,
        mesh=mesh,
        in_specs=(
            P(("dp", "expert"), None),
            P(("dp", "expert"), None),
            P(("dp", "expert"), None),
            P(("dp", "expert"), None),
            P("expert", None, None),
            P("expert", None, None),
            P("expert", None, None),
        ),
        out_specs=(
            P(("dp", "expert"), None),
            P("expert", "dp", None),
            P("expert", "dp", None),
            P("expert", "dp", None),
        ),
        check_vma=False,
    )
```
